32 devices in a mesh: seq: 2 (over x), shard: 16 (over z, y, core).
Axes of the slice: x: 2, y: 2, z: 4, core: 2. Of those that a mesh axis runs over, the one named last changes fastest.
Arguments:
- tokens: bfloat16 [16, 1024, 1024], P('shard', 'seq'), may hold values from -6 to 6
- doc_starts: int32 [16, 4], P('shard'), may hold values from 0 to 1023, as said below
- norm_gain: bfloat16 [1024], P('shard'), may hold values from 0.5 to 1.5
- query_weight: bfloat16 [1024, 1024], P('shard'), may hold values from -0.1875 to 0.1875
- key_weight: bfloat16 [1024, 1024], P('shard'), may hold values from -0.1875 to 0.1875
- value_weight: bfloat16 [1024, 2048], P('shard'), may hold values from -0.1875 to 0.1875
- gate_weight: bfloat16 [1024, 2048], P('shard'), may hold values from -0.1875 to 0.1875
- beta_decay_weight: bfloat16 [1024, 16], P('shard'), may hold values from -0.1875 to 0.1875
- conv_filters: float32 [4, 8, 512], P(None, 'seq'), may hold values from -2.5 to 2.5
- decay_params: float32 [8, 2], P('seq'), may hold values from -10 to 2.5
- out_norm_gain: bfloat16 [256], P('shard'), may hold values from 0.5 to 1.5
- out_weight: bfloat16 [2048, 1024], P('shard'), may hold values from -0.125 to 0.125
- ffn_norm_gain: bfloat16 [1024], P('shard'), may hold values from 0.5 to 1.5
- ffn_gate_weight: bfloat16 [1024, 2816], P('shard'), may hold values from -0.1875 to 0.1875
- ffn_up_weight: bfloat16 [1024, 2816], P('shard'), may hold values from -0.1875 to 0.1875
- down_weight: bfloat16 [2816, 1024], P('shard'), may hold values from -0.109375 to 0.109375
- out_cotangent: bfloat16 [16, 1024, 1024], P('shard', 'seq'), may hold values from -6 to 6
Outputs:
- block_out: bfloat16 [16, 1024, 1024], P('shard', 'seq')
- tokens_grad: float32 [16, 1024, 1024], P('shard', 'seq')
- norm_gain_grad: float32 [1024], P('shard')
- query_weight_grad: float32 [1024, 1024], P('shard')
- key_weight_grad: float32 [1024, 1024], P('shard')
- value_weight_grad: float32 [1024, 2048], P('shard')
- gate_weight_grad: float32 [1024, 2048], P('shard')
- beta_decay_weight_grad: float32 [1024, 16], P('shard')
- conv_filters_grad: float32 [4, 8, 512], P(None, 'seq')
- decay_params_grad: float32 [8, 2], P('seq')
- out_norm_gain_grad: float32 [256], P('shard')
- out_weight_grad: float32 [2048, 1024], P('shard')
- ffn_norm_gain_grad: float32 [1024], P('shard')
- ffn_gate_weight_grad: float32 [1024, 2816], P('shard')
- ffn_up_weight_grad: float32 [1024, 2816], P('shard')
- down_weight_grad: float32 [2816, 1024], P('shard')
The draws below stay inside these ranges and needn't reach their ends.
Inputs may be any that keep to these rules, and one draw needn't show every extreme that they name: `doc_starts`: each row holds 4 document start positions in strictly increasing order, the first of which is 0.
All inputs are finite; a program needn't handle non-finite values.
Results may differ from the reference program's by a relative error of at most 0.022.
Values may be sent and summed in bfloat16 or wider, within the bound.
No kernel may reach another device: no remote copies, remote signals or barrier semaphores. Data moves between devices by JAX's collectives and lax.ppermute only.
A program may use at most 320 MiB of HBM per device.

```python
import jax
import jax.numpy as jnp
from jax import lax

D = 1024
HEADS = 8
KEY = 128
VALUE = 256
FF = 2816
CONV = 4
GROUP = 64
DOCS = 4
LEN = 1024
STREAMS = 16
KD = 1024
VD = 2048


def draw_decay_params(key, part):
    first_key, second_key = jax.random.split(jax.random.fold_in(key, 11))
    scales = jax.random.uniform(first_key, (HEADS,), jnp.float32, -1.0, 2.5)
    biases = jax.random.uniform(second_key, (HEADS,), jnp.float32, -9.0, -3.0)
    return jnp.stack([scales, biases], axis=1)


def draw_doc_starts(key, part):
    stream_keys = jax.random.split(jax.random.fold_in(key, 23), STREAMS)

    def one_stream(stream_key):
        picked = jax.random.permutation(stream_key, LEN - 1)[:DOCS - 1] + 1
        return jnp.concatenate([jnp.zeros((1,), jnp.int32), jnp.sort(picked.astype(jnp.int32))])
    starts = jax.vmap(one_stream)(stream_keys)
    return starts.at[0, DOCS - 1].set(LEN - 1)


def shard_levels(own_key, extent, cuts, low, top_value):
    level = 1.0
    for axis_at, blocks in cuts:
        heights = jax.random.uniform(jax.random.fold_in(jax.random.fold_in(own_key, 6), axis_at), (blocks,), jnp.float32, low / len(cuts), top_value / len(cuts))
        level = level * jnp.repeat(jnp.exp(heights), extent[axis_at] // blocks).reshape((-1,) + (1,) * (len(extent) - 1 - axis_at))
    return level


def gaussian(key, shape, scale, bound, cuts=(), kind=jnp.bfloat16):
    values = scale * jax.random.normal(key, shape, jnp.float32)
    if cuts:
        values = values * shard_levels(key, shape, cuts, -0.22, 0.18)
    return jnp.clip(values, -bound, bound).astype(kind)


def setup_inputs(seed: int = 0) -> dict:
    seeds = jax.random.split(jax.random.key(seed), 18)
    return {
        "tokens": gaussian(seeds[0], (STREAMS, LEN, D), 1.0, 6.0, ((0, 16), (1, 2))),
        "doc_starts": draw_doc_starts(jax.random.fold_in(seeds[17], 71), 0),
        "norm_gain": jnp.clip(1.0 + 0.1 * jax.random.normal(seeds[2], (D,), jnp.float32), 0.5, 1.5).astype(jnp.bfloat16),
        "query_weight": gaussian(seeds[3], (D, KD), D ** -0.5, 0.1875, ((0, 16),)),
        "key_weight": gaussian(seeds[4], (D, KD), D ** -0.5, 0.1875, ((0, 16),)),
        "value_weight": gaussian(seeds[5], (D, VD), D ** -0.5, 0.1875, ((0, 16),)),
        "gate_weight": gaussian(seeds[6], (D, VD), D ** -0.5, 0.1875, ((0, 16),)),
        "beta_decay_weight": gaussian(seeds[7], (D, 2 * HEADS), D ** -0.5, 0.1875, ((0, 16),)),
        "conv_filters": gaussian(seeds[8], (CONV, HEADS, 2 * KEY + VALUE), 0.5, 2.5, ((1, 2),), jnp.float32),
        "decay_params": draw_decay_params(jax.random.fold_in(seeds[17], 71), 0),
        "out_norm_gain": jnp.clip(1.0 + 0.1 * jax.random.normal(seeds[10], (VALUE,), jnp.float32), 0.5, 1.5).astype(jnp.bfloat16),
        "out_weight": gaussian(seeds[11], (VD, D), VD ** -0.5, 0.125, ((0, 16),)),
        "ffn_norm_gain": jnp.clip(1.0 + 0.1 * jax.random.normal(seeds[12], (D,), jnp.float32), 0.5, 1.5).astype(jnp.bfloat16),
        "ffn_gate_weight": gaussian(seeds[13], (D, FF), D ** -0.5, 0.1875, ((0, 16),)),
        "ffn_up_weight": gaussian(seeds[14], (D, FF), D ** -0.5, 0.1875, ((0, 16),)),
        "down_weight": gaussian(seeds[15], (FF, D), FF ** -0.5, 0.109375, ((0, 16),)),
        "out_cotangent": gaussian(seeds[16], (STREAMS, LEN, D), 1.0, 6.0, ((0, 16), (1, 2))),
    }


epsilon = 1e-06
highest = lax.Precision.HIGHEST

@jax.custom_vjp
def low(v):
    return lax.optimization_barrier(v.astype(jnp.bfloat16)).astype(jnp.float32)

@jax.custom_vjp
def low_back(v):
    return v

def low_keep(v):
    return (low(v), None)

def low_pass(kept, grad):
    return (grad,)

def back_keep(v):
    return (v, None)

def back_low(kept, grad):
    return (low(grad),)
low.defvjp(low_keep, low_pass)
low_back.defvjp(back_keep, back_low)

def product(left_side, right_side):
    return jnp.dot(left_side.astype(jnp.float32), right_side.astype(jnp.float32), precision=highest, preferred_element_type=jnp.float32)

def rms_norm(values, gain):
    return values * lax.rsqrt(lax.optimization_barrier(jnp.mean(values * values, axis=-1, keepdims=True)) + epsilon) * gain

def gated_norm(values, gates, gain):
    return rms_norm(values, gain) * jax.nn.silu(gates)

def swiglu(gate_rows, up_rows):
    return jax.nn.silu(gate_rows) * up_rows

def document_ids(starts, length):
    places = lax.broadcasted_iota(jnp.int32, (length, starts.shape[0]), 0)
    return lax.optimization_barrier(jnp.sum((places >= starts[None, :]).astype(jnp.int32), axis=1)) - 1

def causal_conv(inputs, filters, doc_ids):
    length, channels = inputs.shape
    summed = inputs * filters[CONV - 1]
    for offset in range(1, CONV):
        shifted = jnp.concatenate([jnp.zeros((offset, channels), jnp.float32), inputs[:length - offset]], axis=0)
        shifted_docs = jnp.concatenate([jnp.full((offset,), -1, jnp.int32), doc_ids[:length - offset]])
        same_doc = (shifted_docs == doc_ids).astype(jnp.float32)
        summed = summed + shifted * same_doc[:, None] * filters[CONV - 1 - offset]
    return jax.nn.silu(summed)

def delta_rule(query_rows, key_rows, value_rows, strength, log_decay, doc_ids):
    length, key_width = key_rows.shape
    value_width = value_rows.shape[1]
    blocks = length // GROUP
    query_blocks = query_rows.reshape(blocks, GROUP, key_width)
    key_blocks = key_rows.reshape(blocks, GROUP, key_width)
    value_blocks = value_rows.reshape(blocks, GROUP, value_width)
    beta_blocks = strength.reshape(blocks, GROUP)
    decay_sums = jnp.cumsum(log_decay.reshape(blocks, GROUP), axis=1)
    doc_blocks = doc_ids.reshape(blocks, GROUP)
    previous = jnp.concatenate([jnp.full((1,), -1, jnp.int32), doc_ids[GROUP - 1:length - 1:GROUP]])
    carried = (doc_blocks == previous[:, None]).astype(jnp.float32)
    same_doc = doc_blocks[:, :, None] == doc_blocks[:, None, :]
    row_index = lax.broadcasted_iota(jnp.int32, (GROUP, GROUP), 0)
    column_index = lax.broadcasted_iota(jnp.int32, (GROUP, GROUP), 1)
    strictly = same_doc & (row_index > column_index)[None]
    inclusive = same_doc & (row_index >= column_index)[None]
    decay_gap = decay_sums[:, :, None] - decay_sums[:, None, :]
    fade_lower = jnp.where(strictly, jnp.exp(jnp.where(strictly, decay_gap, 0.0)), 0.0)
    fade_upper = jnp.where(inclusive, jnp.exp(jnp.where(inclusive, decay_gap, 0.0)), 0.0)
    key_gram = jnp.einsum('cik,cjk->cij', key_blocks, key_blocks, precision=highest)
    system = jnp.eye(GROUP, dtype=jnp.float32)[None] + beta_blocks[:, :, None] * key_gram * fade_lower
    entering = jnp.exp(decay_sums) * carried
    right_side = jnp.concatenate([beta_blocks[:, :, None] * value_blocks, (beta_blocks * entering)[:, :, None] * key_blocks], axis=2)
    solved = jax.scipy.linalg.solve_triangular(system, right_side, lower=True, unit_diagonal=True)
    new_values = solved[:, :, :value_width]
    corrections = solved[:, :, value_width:]
    scores = jnp.einsum('cik,cjk->cij', query_blocks, key_blocks, precision=highest) * fade_upper
    query_in = entering[:, :, None] * query_blocks
    same_last = doc_blocks == doc_blocks[:, -1:]
    fade_last = jnp.where(same_last, jnp.exp(jnp.where(same_last, decay_sums[:, -1:] - decay_sums, 0.0)), 0.0)
    key_out = fade_last[:, :, None] * key_blocks
    retain = entering[:, -1]

    def advance(memory, pieces):
        block_values, block_corr, block_scores, block_query, block_keys, block_retain = pieces
        deltas = block_values - product(block_corr, memory)
        outputs = product(block_query, memory) + product(block_scores, deltas)
        memory = block_retain * memory + product(block_keys.T, deltas)
        return (memory, outputs)
    start = jnp.zeros((key_width, value_width), jnp.float32)
    final_memory, outputs = lax.scan(jax.checkpoint(advance), start, (new_values, corrections, scores, query_in, key_out, retain))
    return outputs.reshape(length, value_width)

def head_mixer(query_raw, key_raw, value_raw, logits, filters, decay_pair, doc_ids):
    key_width = query_raw.shape[1]
    convolved = causal_conv(jnp.concatenate([query_raw, key_raw, value_raw], axis=1), filters, doc_ids)
    query_rows = convolved[:, :key_width]
    key_rows = convolved[:, key_width:2 * key_width]
    value_rows = convolved[:, 2 * key_width:]
    query_rows = query_rows * lax.rsqrt(lax.optimization_barrier(jnp.sum(query_rows * query_rows, axis=1, keepdims=True)) + epsilon) * key_width ** (-0.5)
    key_rows = key_rows * lax.rsqrt(lax.optimization_barrier(jnp.sum(key_rows * key_rows, axis=1, keepdims=True)) + epsilon)
    strength = jax.nn.sigmoid(logits[:, 0])
    log_decay = -jnp.exp(decay_pair[0]) * jax.nn.softplus(logits[:, 1] + decay_pair[1])
    return delta_rule(query_rows, key_rows, value_rows, strength, log_decay, doc_ids)

def residual_block(inputs, doc_ids, params):
    norm_gain, query_weight, key_weight, value_weight, gate_weight, beta_decay_weight, conv_filters, decay_params, out_norm_gain, out_weight, ffn_norm_gain, ffn_gate_weight, ffn_up_weight, down_weight = params
    length = inputs.shape[0]
    normed = low(rms_norm(inputs, norm_gain))
    query_raw = low_back(low(product(normed, query_weight)))
    key_raw = low_back(low(product(normed, key_weight)))
    value_raw = low_back(low(product(normed, value_weight)))
    logits = low_back(low(product(normed, beta_decay_weight)))
    gate_rows = low_back(product(normed, gate_weight))
    mixer = jax.vmap(head_mixer, in_axes=(1, 1, 1, 1, 1, 0, None), out_axes=1)
    mixed = mixer(query_raw.reshape(length, HEADS, KEY), key_raw.reshape(length, HEADS, KEY), value_raw.reshape(length, HEADS, VALUE), logits.reshape(length, HEADS, 2), conv_filters, decay_params, doc_ids)
    mixed = low_back(low(mixed))
    gated = low(gated_norm(mixed, gate_rows.reshape(length, HEADS, VALUE), out_norm_gain))
    branch = low_back(product(gated.reshape(length, HEADS * VALUE), out_weight))
    middle = inputs + branch
    hidden = low(rms_norm(middle, ffn_norm_gain))
    gate_ffn = low_back(product(hidden, ffn_gate_weight))
    up_ffn = low_back(product(hidden, ffn_up_weight))
    activated = low(swiglu(gate_ffn, up_ffn))
    return middle + product(activated, down_weight)

def reference(tokens, doc_starts, norm_gain, query_weight, key_weight, value_weight, gate_weight, beta_decay_weight, conv_filters, decay_params, out_norm_gain, out_weight, ffn_norm_gain, ffn_gate_weight, ffn_up_weight, down_weight, out_cotangent):
    weights = (norm_gain.astype(jnp.float32), query_weight.astype(jnp.float32), key_weight.astype(jnp.float32), value_weight.astype(jnp.float32), gate_weight.astype(jnp.float32), beta_decay_weight.astype(jnp.float32), conv_filters.astype(jnp.float32), decay_params.astype(jnp.float32), out_norm_gain.astype(jnp.float32), out_weight.astype(jnp.float32), ffn_norm_gain.astype(jnp.float32), ffn_gate_weight.astype(jnp.float32), ffn_up_weight.astype(jnp.float32), down_weight.astype(jnp.float32))

    def one_stream(totals, item):
        stream, starts, cotangent = item
        doc_ids = document_ids(starts, stream.shape[0])

        def run_block(inputs, params):
            return residual_block(inputs, doc_ids, params)
        result, pull = jax.vjp(run_block, stream.astype(jnp.float32), weights)
        input_grad, weight_grads = pull(cotangent.astype(jnp.float32))
        totals = jax.tree.map(jnp.add, totals, weight_grads)
        return (totals, (result.astype(jnp.bfloat16), input_grad))
    zeros = jax.tree.map(jnp.zeros_like, weights)
    totals, outputs = lax.scan(one_stream, zeros, (tokens, doc_starts, out_cotangent))
    return (outputs[0], outputs[1], totals[0], totals[1], totals[2], totals[3], totals[4], totals[5], totals[6], totals[7], totals[8], totals[9], totals[10], totals[11], totals[12], totals[13])
```

```python
import functools

import jax
import jax.numpy as jnp
from jax import lax
from jax.experimental import pallas as pl
from jax.experimental.pallas import tpu as pltpu
from jax.sharding import PartitionSpec as P

HEADS = 8
KEY = 128
VALUE = 256
CONV = 4
GROUP = 64
HALO = 16
SUB = 4
epsilon = 1e-06
f32 = jnp.float32
bf16 = jnp.bfloat16


def dot(a, b, ca=1, cb=0):
    return lax.dot_general(a, b, (((ca,), (cb,)), ((), ())), preferred_element_type=f32)


def iota(shape, dim):
    return lax.broadcasted_iota(jnp.int32, shape, dim)


def doc_count(starts_ref, times):
    count = jnp.zeros(times.shape, jnp.int32)
    for s in range(starts_ref.shape[1]):
        count = count + jnp.where(times >= starts_ref[0, s], 1, 0)
    return count


def scalar_doc(starts_ref, time):
    count = 0
    for s in range(starts_ref.shape[1]):
        count = count + (time >= starts_ref[0, s]).astype(jnp.int32)
    return count


def per_head(cols, heads, width):
    rows = cols.shape[0]
    lane = iota((rows, heads * width), 1)
    out = jnp.broadcast_to(cols[:, heads - 1 : heads], (rows, heads * width))
    for h in range(heads - 2, -1, -1):
        out = jnp.where(lane < (h + 1) * width, cols[:, h : h + 1], out)
    return out


def head_sums(panel, heads, width):
    lane = iota(panel.shape, 1)
    sums = []
    for h in range(heads):
        inside = (lane >= h * width) & (lane < (h + 1) * width)
        sums.append(jnp.sum(jnp.where(inside, panel, 0.0), axis=1, keepdims=True))
    return columns(sums)


def columns(parts):
    rows = parts[0].shape[0]
    lane = iota((rows, len(parts)), 1)
    out = jnp.broadcast_to(parts[-1], (rows, len(parts)))
    for h in range(len(parts) - 2, -1, -1):
        out = jnp.where(lane == h, parts[h], out)
    return out


def block_diagonal(panel, heads):
    if heads == 1:
        return panel
    lane = iota(panel.shape, 1)
    zero = jnp.zeros_like(panel)
    parts = []
    for h in range(heads):
        inside = (lane >= h * GROUP) & (lane < (h + 1) * GROUP)
        parts.append(jnp.where(inside, panel, zero))
    return jnp.concatenate(parts, axis=0)


def diagonal_panel(full, heads):
    if heads == 1:
        return full
    lane = iota((GROUP, heads * GROUP), 1)
    out = full[(heads - 1) * GROUP :]
    for h in range(heads - 2, -1, -1):
        out = jnp.where(lane < (h + 1) * GROUP, full[h * GROUP : (h + 1) * GROUP], out)
    return out


def key_diagonal(keys):
    heads = len(keys)
    if heads == 1:
        return keys[0]
    zero = jnp.zeros_like(keys[0])
    rows = []
    for h in range(heads):
        rows.append(jnp.concatenate([keys[h] if o == h else zero for o in range(heads)], axis=1))
    return jnp.concatenate(rows, axis=0)


def scan_rows(values, reverse=False):
    rows = values.shape[0]
    index = iota(values.shape, 0)
    step = 1
    while step < rows:
        if reverse:
            moved = pltpu.roll(values, rows - step, 0)
            values = values + jnp.where(index < rows - step, moved, 0.0)
        else:
            moved = pltpu.roll(values, step, 0)
            values = values + jnp.where(index >= step, moved, 0.0)
        step *= 2
    return values


def sigmoid(v):
    return 1.0 / (1.0 + jnp.exp(-v))


def softplus(v):
    return jnp.maximum(v, 0.0) + jnp.log(1.0 + jnp.exp(-jnp.abs(v)))


class Block:
    def __init__(self, heads, base, raw_ref, filters_ref, decay_ref, starts_ref, backward=False):
        self.heads = heads
        width = heads * (2 * KEY + VALUE)
        times = base + iota((GROUP, 1), 0)
        docs = doc_count(starts_ref, times)
        self.masks = [
            (docs == doc_count(starts_ref, times - o)).astype(f32) for o in range(1, CONV)
        ]
        self.base = base
        self.raw_ref = raw_ref
        self.filters_ref = filters_ref
        self.query, self.keys, self.query_pre, self.key_pre = [], [], [], []
        self.query_conv, self.key_conv, self.query_scale, self.key_scale = [], [], [], []
        for h in range(heads):
            pre = self.convolve(h * KEY, KEY)
            conv = pre * sigmoid(pre)
            scale = lax.rsqrt(jnp.sum(conv * conv, axis=1, keepdims=True) + epsilon)
            self.query_pre.append(pre)
            self.query_conv.append(conv)
            self.query_scale.append(scale)
            self.query.append(conv * scale * KEY ** (-0.5))
        for h in range(heads):
            pre = self.convolve((heads + h) * KEY, KEY)
            conv = pre * sigmoid(pre)
            scale = lax.rsqrt(jnp.sum(conv * conv, axis=1, keepdims=True) + epsilon)
            self.key_pre.append(pre)
            self.key_conv.append(conv)
            self.key_scale.append(scale)
            self.keys.append(conv * scale)
        logits = raw_ref[pl.ds(base, GROUP), width : width + 2 * KEY // 2].astype(f32)
        self.strength = sigmoid(logits[:, :heads])
        self.decay_logit = logits[:, heads : 2 * heads] + decay_ref[1:2, :heads]
        self.decay_rate = -jnp.exp(decay_ref[0:1, :heads])
        self.log_decay = self.decay_rate * softplus(self.decay_logit)
        sums = scan_rows(self.log_decay)
        self.sums = sums
        last = sums[GROUP - 1 : GROUP]
        before = scalar_doc(starts_ref, base - 1)
        final = scalar_doc(starts_ref, base + GROUP - 1)
        self.entering = jnp.where(docs == before, jnp.exp(sums), 0.0)
        same_last = docs == final
        self.leaving = jnp.where(same_last, jnp.exp(jnp.where(same_last, last - sums, 0.0)), 0.0)
        self.retain = self.entering[GROUP - 1 : GROUP]
        shape = (GROUP, heads * GROUP)
        row = iota(shape, 0)
        place = jnp.bitwise_and(iota(shape, 1), GROUP - 1)
        self.row, self.place = row, place
        across = jnp.bitwise_and(iota((1, heads * GROUP), 1), GROUP - 1)
        docs_across = doc_count(starts_ref, base + across)
        same = docs == docs_across
        self.inclusive = same & (row >= place)
        self.strict = same & (row > place)
        sums_down = per_head(sums, heads, GROUP)
        sums_across = jnp.sum(jnp.where(row == place, sums_down, 0.0), axis=0, keepdims=True)
        gap = jnp.where(self.inclusive, sums_down - sums_across, 0.0)
        self.fade = jnp.where(self.inclusive, jnp.exp(gap), 0.0)
        self.strength_down = per_head(self.strength, heads, GROUP)
        low_keys = [k.astype(bf16) for k in self.keys]
        low_query = [q.astype(bf16) for q in self.query]
        self.low_keys, self.low_query = low_keys, low_query
        self.key_diag = key_diagonal(low_keys)
        left = jnp.concatenate(
            [jnp.concatenate(low_keys, axis=1), jnp.concatenate(low_query, axis=1)], axis=0
        )
        self.query_key_rows = left
        grams = dot(left, self.key_diag, 1, 1)
        self.key_gram = grams[:GROUP]
        self.score_gram = grams[GROUP:]
        self.system = jnp.where(self.strict, self.strength_down * self.key_gram * self.fade, 0.0)
        self.scores = self.score_gram * self.fade

    def taps(self, start, width):
        current = self.raw_ref[pl.ds(self.base, GROUP), start : start + width].astype(f32)
        earlier = pl.multiple_of(jnp.maximum(self.base - HALO, 0), HALO)
        halo = self.raw_ref[pl.ds(earlier, HALO), start : start + width].astype(f32)
        extended = jnp.concatenate([halo, current], axis=0)
        return [current] + [
            pltpu.roll(extended, o, 0)[HALO:] * self.masks[o - 1] for o in range(1, CONV)
        ]

    def convolve(self, start, width):
        taps = self.taps(start, width)
        filters = self.filters_ref[:, start : start + width]
        total = taps[0] * filters[CONV - 1 : CONV]
        for o in range(1, CONV):
            total = total + taps[o] * filters[CONV - 1 - o : CONV - o]
        return total


def inverse(system, heads, row, place):
    eye = (row == place).astype(f32)

    def part(size):
        apart = jnp.bitwise_xor(row, place)
        return jnp.where((apart >= size) & (apart < 2 * size), system, 0.0)

    result = eye - part(1)
    size = 2
    while size < GROUP:
        low = result.astype(bf16)
        inner = dot(part(size).astype(bf16), block_diagonal(low, heads))
        result = result - dot(low, block_diagonal(inner.astype(bf16), heads))
        size *= 2
    return result


def forward_kernel(
    heads, starts_ref, raw_ref, filters_ref, decay_ref,
    mixed_ref, inverse_ref, delta_ref, rest_ref, memory_ref, state,
):
    step = pl.program_id(0)

    @pl.when(step == 0)
    def _():
        state[...] = jnp.zeros_like(state)

    blocks = []
    for s in range(SUB):
        base = pl.multiple_of((step * SUB + s) * GROUP, GROUP)
        block = Block(heads, base, raw_ref, filters_ref, decay_ref, starts_ref)
        block.values = []
        for h in range(heads):
            pre = block.convolve(2 * heads * KEY + h * VALUE, VALUE)
            block.values.append(pre * sigmoid(pre))
        block.solve = inverse(block.system, heads, block.row, block.place).astype(bf16)
        inverse_ref[s * GROUP : (s + 1) * GROUP] = block.solve
        blocks.append(block)
    for s, block in enumerate(blocks):
        from_state, rest, right = [], [], []
        for h in range(heads):
            entering = block.entering[:, h : h + 1]
            memory = state[h * KEY : (h + 1) * KEY].astype(bf16)
            memory_ref[(s * heads + h) * KEY : (s * heads + h + 1) * KEY] = memory
            both = jnp.concatenate([entering * block.keys[h], entering * block.query[h]], axis=0)
            read = dot(both.astype(bf16), memory)
            from_state.append(read[GROUP:])
            missing = block.values[h] - read[:GROUP]
            rest.append(missing.astype(bf16))
            right.append((block.strength[:, h : h + 1] * missing).astype(bf16))
        rest_ref[s * heads * GROUP : (s + 1) * heads * GROUP] = jnp.concatenate(rest, axis=0)
        delta = dot(block_diagonal(block.solve, heads), jnp.concatenate(right, axis=0)).astype(bf16)
        delta_ref[s * heads * GROUP : (s + 1) * heads * GROUP] = delta
        outputs = dot(block_diagonal(block.scores.astype(bf16), heads), delta)
        for h in range(heads):
            rows = slice(h * GROUP, (h + 1) * GROUP)
            out = from_state[h] + outputs[rows]
            mixed_ref[s * GROUP : (s + 1) * GROUP, h * VALUE : (h + 1) * VALUE] = out.astype(bf16)
            leaving = (block.leaving[:, h : h + 1] * block.keys[h]).astype(bf16)
            keep = block.retain[:, h : h + 1]
            own = slice(h * KEY, (h + 1) * KEY)
            state[own] = keep * state[own] + dot(leaving, delta[rows], 0, 0)


def silu_slope(pre):
    gate = sigmoid(pre)
    return gate * (1.0 + pre * (1.0 - gate))


def backward_kernel(
    heads, starts_ref, raw_ref, filters_ref, decay_ref,
    mixed_grad_ref, inverse_ref, delta_ref, rest_ref, memory_ref,
    raw_grad_ref, filters_grad_ref, decay_grad_ref, state, halo,
):
    step = pl.program_id(0)
    steps = pl.num_programs(0)
    width = heads * (2 * KEY + VALUE)

    @pl.when(step == 0)
    def _():
        state[...] = jnp.zeros_like(state)
        halo[...] = jnp.zeros_like(halo)
        filters_grad_ref[...] = jnp.zeros_like(filters_grad_ref)
        decay_grad_ref[...] = jnp.zeros_like(decay_grad_ref)

    for s in range(SUB - 1, -1, -1):
        base = pl.multiple_of(((steps - 1 - step) * SUB + s) * GROUP, GROUP)
        block = Block(heads, base, raw_ref, filters_ref, decay_ref, starts_ref)
        here = slice(s * GROUP, (s + 1) * GROUP)
        stacked = slice(s * heads * GROUP, (s + 1) * heads * GROUP)
        solve = inverse_ref[here]
        delta = delta_ref[stacked]
        rest = rest_ref[stacked]
        out_grad = jnp.concatenate(
            [mixed_grad_ref[here, h * VALUE : (h + 1) * VALUE] for h in range(heads)], axis=0
        )
        later = [state[h * KEY : (h + 1) * KEY] for h in range(heads)]
        later_low = [m.astype(bf16) for m in later]
        leaving = [
            (block.leaving[:, h : h + 1] * block.keys[h]).astype(bf16) for h in range(heads)
        ]
        pulled = jnp.concatenate([dot(leaving[h], later_low[h]) for h in range(heads)], axis=0)
        delta_grad = pulled + dot(block_diagonal(block.scores.astype(bf16), heads), out_grad, 0, 0)
        right_grad = dot(block_diagonal(solve, heads), delta_grad.astype(bf16), 0, 0)
        rest_grad, strength_grad = [], []
        for h in range(heads):
            rows = slice(h * GROUP, (h + 1) * GROUP)
            rest_grad.append(block.strength[:, h : h + 1] * right_grad[rows])
            strength_grad.append(
                jnp.sum(right_grad[rows] * rest[rows].astype(f32), axis=1, keepdims=True)
            )
        rest_low = [r.astype(bf16) for r in rest_grad]
        entering_query_grad, entering_key_grad, leaving_key_grad, retain_grad = [], [], [], []
        for h in range(heads):
            rows = slice(h * GROUP, (h + 1) * GROUP)
            entering = block.entering[:, h : h + 1]
            memory = memory_ref[(s * heads + h) * KEY : (s * heads + h + 1) * KEY]
            pair = jnp.concatenate([out_grad[rows], rest_low[h]], axis=0)
            back = dot(pair, memory, 1, 1)
            entering_query_grad.append(back[:GROUP])
            entering_key_grad.append(-back[GROUP:])
            leaving_key_grad.append(dot(delta[rows], later_low[h], 1, 1))
            product = later[h] * memory.astype(f32)
            retain_grad.append(
                jnp.sum(jnp.sum(product, axis=0, keepdims=True), axis=1, keepdims=True)
            )
            left = jnp.concatenate(
                [entering * block.query[h], -entering * block.keys[h]], axis=0
            ).astype(bf16)
            state[h * KEY : (h + 1) * KEY] = (
                block.retain[:, h : h + 1] * later[h] + dot(left, pair, 0, 0)
            )
        right_low = right_grad.astype(bf16)
        score_part = diagonal_panel(dot(out_grad, delta, 1, 1), heads)
        system_part = diagonal_panel(dot(right_low, delta, 1, 1), heads)
        scores_grad = jnp.where(block.inclusive, score_part, 0.0)
        system_grad = jnp.where(block.strict, -system_part, 0.0)
        score_gram_grad = scores_grad * block.fade
        faded = system_grad * block.fade
        key_gram_grad = block.strength_down * faded
        gap_grad = score_gram_grad * block.score_gram + key_gram_grad * block.key_gram
        strength_panel = head_sums(faded * block.key_gram, heads, GROUP)
        down = jnp.sum(gap_grad, axis=0, keepdims=True)
        gap_rows = head_sums(
            gap_grad - jnp.where(block.row == block.place, down, 0.0), heads, GROUP
        )
        both_low = jnp.concatenate([key_gram_grad, score_gram_grad], axis=0).astype(bf16)
        straight = dot(both_low, block.key_diag)
        turned = dot(both_low, block.query_key_rows, 0, 0)
        entering_grad, leaving_grad = [], []
        for h in range(heads):
            lanes = slice(h * KEY, (h + 1) * KEY)
            entering = block.entering[:, h : h + 1]
            fading = block.leaving[:, h : h + 1]
            query_grad = entering * entering_query_grad[h] + straight[GROUP:, lanes]
            key_grad = (
                turned[h * GROUP : (h + 1) * GROUP, lanes]
                + straight[:GROUP, lanes]
                + fading * leaving_key_grad[h]
                + entering * entering_key_grad[h]
            )
            entering_grad.append(
                jnp.sum(
                    entering_query_grad[h] * block.query[h] + entering_key_grad[h] * block.keys[h],
                    axis=1,
                    keepdims=True,
                )
            )
            leaving_grad.append(
                jnp.sum(leaving_key_grad[h] * block.keys[h], axis=1, keepdims=True)
            )
            for start, grad, conv, scale, pre, factor in (
                (h * KEY, query_grad, block.query_conv[h], block.query_scale[h],
                 block.query_pre[h], KEY ** (-0.5)),
                ((heads + h) * KEY, key_grad, block.key_conv[h], block.key_scale[h],
                 block.key_pre[h], 1.0),
            ):
                along = jnp.sum(grad * conv, axis=1, keepdims=True)
                conv_grad = (factor * scale) * (grad - conv * (scale * scale * along))
                convolve_back(
                    block, s, start, KEY, conv_grad * silu_slope(pre), starts_ref,
                    raw_grad_ref, filters_grad_ref, halo,
                )
            start = 2 * heads * KEY + h * VALUE
            pre = block.convolve(start, VALUE)
            convolve_back(
                block, s, start, VALUE, rest_grad[h] * silu_slope(pre), starts_ref,
                raw_grad_ref, filters_grad_ref, halo,
            )
        entering_grad = columns(entering_grad) * block.entering
        leaving_grad = columns(leaving_grad) * block.leaving
        strength_grad = columns(strength_grad) + strength_panel
        retain_grad = columns(retain_grad) * block.retain
        at_last = jnp.sum(leaving_grad, axis=0, keepdims=True) + retain_grad
        index = iota((GROUP, heads), 0)
        sums_grad = (
            entering_grad - leaving_grad + gap_rows + jnp.where(index == GROUP - 1, at_last, 0.0)
        )
        log_decay_grad = scan_rows(sums_grad, reverse=True)
        logit_grad = log_decay_grad * block.decay_rate * sigmoid(block.decay_logit)
        beta_grad = strength_grad * block.strength * (1.0 - block.strength)
        lane = iota((GROUP, KEY), 1)
        packed = jnp.zeros((GROUP, KEY), f32)
        for h in range(heads):
            packed = jnp.where(lane == h, beta_grad[:, h : h + 1], packed)
            packed = jnp.where(lane == heads + h, logit_grad[:, h : h + 1], packed)
        raw_grad_ref[here, width : width + KEY] = packed.astype(bf16)
        scale_sum = jnp.sum(log_decay_grad * block.log_decay, axis=0, keepdims=True)
        bias_sum = jnp.sum(logit_grad, axis=0, keepdims=True)
        decay_grad_ref[0:1] = decay_grad_ref[0:1] + scale_sum
        decay_grad_ref[1:2] = decay_grad_ref[1:2] + bias_sum


def convolve_back(
    block, s, start, width, pre_grad, starts_ref, raw_grad_ref, filters_grad_ref, halo
):
    lanes = slice(start, start + width)
    taps = block.taps(start, width)
    for o in range(CONV):
        j = CONV - 1 - o
        product = (pre_grad * taps[o]).reshape(GROUP // 8, 8, width)
        filters_grad_ref[j * 8 : (j + 1) * 8, lanes] = filters_grad_ref[
            j * 8 : (j + 1) * 8, lanes
        ] + jnp.sum(product, axis=0)
    filters = block.filters_ref[:, lanes]
    extended = jnp.concatenate([pre_grad, halo[:, lanes]], axis=0)
    rows = GROUP + 8
    times = block.base + iota((rows, 1), 0)
    docs = doc_count(starts_ref, times)
    total = pre_grad * filters[CONV - 1 : CONV]
    for o in range(1, CONV):
        mask = (docs == doc_count(starts_ref, times - o)).astype(f32)
        moved = pltpu.roll(extended * mask, rows - o, 0)[:GROUP]
        total = total + moved * filters[CONV - 1 - o : CONV - o]
    raw_grad_ref[s * GROUP : (s + 1) * GROUP, lanes] = total.astype(bf16)
    halo[:, lanes] = pre_grad[:8]


SPACE = 56 * 2**20


def mixer_forward(raw, filters, decays, starts, heads):
    length, wide = raw.shape
    steps = length // (SUB * GROUP)
    rows = SUB * GROUP
    blocks = length // GROUP
    whole = lambda a: pl.BlockSpec(a.shape, lambda i: (0, 0))
    part = lambda r, c: pl.BlockSpec((r, c), lambda i: (i, 0))
    return pl.pallas_call(
        functools.partial(forward_kernel, heads),
        grid=(steps,),
        in_specs=[
            pl.BlockSpec(memory_space=pltpu.SMEM), whole(raw), whole(filters), whole(decays),
        ],
        out_specs=[
            part(rows, heads * VALUE), part(rows, heads * GROUP), part(rows * heads, VALUE),
            part(rows * heads, VALUE), part(SUB * heads * KEY, VALUE),
        ],
        out_shape=[
            jax.ShapeDtypeStruct((length, heads * VALUE), bf16),
            jax.ShapeDtypeStruct((length, heads * GROUP), bf16),
            jax.ShapeDtypeStruct((length * heads, VALUE), bf16),
            jax.ShapeDtypeStruct((length * heads, VALUE), bf16),
            jax.ShapeDtypeStruct((blocks * heads * KEY, VALUE), bf16),
        ],
        scratch_shapes=[pltpu.VMEM((heads * KEY, VALUE), f32)],
        compiler_params=pltpu.CompilerParams(vmem_limit_bytes=SPACE),
        name="mixer_forward",
    )(starts, raw, filters, decays)


def mixer_backward(raw, filters, decays, starts, mixed_grad, kept, heads):
    length, wide = raw.shape
    steps = length // (SUB * GROUP)
    rows = SUB * GROUP
    whole = lambda a: pl.BlockSpec(a.shape, lambda i: (0, 0))
    part = lambda r, c: pl.BlockSpec((r, c), lambda i: (steps - 1 - i, 0))
    return pl.pallas_call(
        functools.partial(backward_kernel, heads),
        grid=(steps,),
        in_specs=[
            pl.BlockSpec(memory_space=pltpu.SMEM), whole(raw), whole(filters), whole(decays),
            part(rows, heads * VALUE), part(rows, heads * GROUP), part(rows * heads, VALUE),
            part(rows * heads, VALUE), part(SUB * heads * KEY, VALUE),
        ],
        out_specs=[
            part(rows, wide),
            pl.BlockSpec((8 * CONV, filters.shape[1]), lambda i: (0, 0)),
            pl.BlockSpec((2, heads), lambda i: (0, 0)),
        ],
        out_shape=[
            jax.ShapeDtypeStruct((length, wide), bf16),
            jax.ShapeDtypeStruct((8 * CONV, filters.shape[1]), f32),
            jax.ShapeDtypeStruct((2, heads), f32),
        ],
        scratch_shapes=[
            pltpu.VMEM((heads * KEY, VALUE), f32),
            pltpu.VMEM((8, filters.shape[1]), f32),
        ],
        compiler_params=pltpu.CompilerParams(vmem_limit_bytes=SPACE),
        name="mixer_backward",
    )(starts, raw, filters, decays, mixed_grad, *kept)


def forward_dot(left_side, right_side):
    return jnp.dot(left_side, right_side, preferred_element_type=f32)


def times_transposed(left_side, right_side):
    return dot(left_side, right_side, 1, 1)


def transposed_times(left_side, right_side):
    return dot(left_side, right_side, 0, 0)


def rms_norm(values, gain):
    return values * lax.rsqrt(jnp.mean(values * values, axis=-1, keepdims=True) + epsilon) * gain


def gated_norm(values, gates, gain):
    return rms_norm(values, gain) * jax.nn.silu(gates)


def swiglu(gate_rows, up_rows):
    return jax.nn.silu(gate_rows) * up_rows


def swap_seq(values):
    return lax.ppermute(values, "seq", [(0, 1), (1, 0)])


def in_order(own, other, axis):
    first = lax.axis_index("seq") == 0
    return jnp.where(
        first,
        jnp.concatenate([own, other], axis=axis),
        jnp.concatenate([other, own], axis=axis),
    )


def gather_seq(values, axis):
    if lax.axis_size("seq") == 2:
        return in_order(values, swap_seq(values), axis)
    return lax.all_gather(values, "seq", axis=axis, tiled=True)


def own_part(values, axis, index=None):
    size = values.shape[axis] // lax.axis_size("seq")
    index = lax.axis_index("seq") if index is None else index
    return lax.dynamic_slice_in_dim(values, index * size, size, axis=axis)


def sum_scatter_seq(values, axis):
    if lax.axis_size("seq") == 2:
        other = own_part(values, axis, 1 - lax.axis_index("seq")).astype(bf16)
        return own_part(values, axis) + swap_seq(other).astype(f32)
    return lax.psum_scatter(
        values.astype(bf16), "seq", scatter_dimension=axis, tiled=True
    ).astype(f32)


def sum_seq(values):
    if lax.axis_size("seq") == 2:
        low = values.astype(bf16)
        return low.astype(f32) + swap_seq(low).astype(f32)
    return lax.psum(values.astype(bf16), "seq").astype(f32)


def exchange_seq(values, split, join):
    if lax.axis_size("seq") == 2:
        other = own_part(values, split, 1 - lax.axis_index("seq"))
        return in_order(own_part(values, split), swap_seq(other), join)
    return lax.all_to_all(values, "seq", split_axis=split, concat_axis=join, tiled=True)


def gather_shard(values):
    return lax.all_gather(values, "shard", axis=0, tiled=True)


def scatter_shard(values):
    return lax.psum_scatter(values, "shard", scatter_dimension=0, tiled=True)


def on_device(
    tokens,
    doc_starts,
    norm_gain,
    query_weight,
    key_weight,
    value_weight,
    gate_weight,
    beta_decay_weight,
    conv_filters,
    decay_params,
    out_norm_gain,
    out_weight,
    ffn_norm_gain,
    ffn_gate_weight,
    ffn_up_weight,
    down_weight,
    out_cotangent,
):
    heads = HEADS // lax.axis_size("seq")
    shards = lax.axis_size("shard")
    rows = query_weight.shape[0]
    width = heads * (2 * KEY + VALUE)
    wide = width + KEY
    ff = ffn_gate_weight.shape[1]

    logit_weight = own_part(beta_decay_weight.reshape(rows, HEADS, 2), 1)
    gain_rows = out_norm_gain.shape[0]
    extra = jnp.concatenate(
        [
            logit_weight[:, :, 0],
            logit_weight[:, :, 1],
            norm_gain[:, None],
            ffn_norm_gain[:, None],
            jnp.pad(out_norm_gain, (0, rows - gain_rows))[:, None],
            jnp.zeros((rows, KEY - 2 * heads - 3), bf16),
        ],
        axis=1,
    )
    mixer_piece = jnp.concatenate(
        [
            own_part(query_weight, 1),
            own_part(key_weight, 1),
            own_part(value_weight, 1),
            extra,
            own_part(gate_weight, 1),
        ],
        axis=1,
    )
    mixer_full = gather_shard(mixer_piece)
    out_full = gather_shard(out_weight)
    ffn_full = gather_shard(jnp.concatenate([ffn_gate_weight, ffn_up_weight], axis=1))
    down_full = gather_shard(down_weight)
    raw_full = mixer_full[:, :wide]
    gate_full = mixer_full[:, wide:]
    first_gain = mixer_full[:, width + 2 * heads].astype(f32)
    second_gain = mixer_full[:, width + 2 * heads + 1].astype(f32)
    third_gain = (
        mixer_full[:, width + 2 * heads + 2]
        .reshape(shards, rows)[:, :gain_rows]
        .reshape(shards * gain_rows)
        .astype(f32)
    )

    own_tokens = tokens[0]
    token_count = own_tokens.shape[0]
    inputs = own_tokens.astype(f32)
    all_inputs = gather_seq(own_tokens, 0).astype(f32)
    length = all_inputs.shape[0]
    all_scaled = all_inputs * lax.rsqrt(
        jnp.mean(all_inputs * all_inputs, axis=-1, keepdims=True) + epsilon
    )
    normed = (all_scaled * first_gain).astype(bf16)
    raw = forward_dot(normed, raw_full).astype(bf16)
    gate_rows = forward_dot(normed, gate_full)
    filters = jnp.concatenate(
        [
            conv_filters[:, :, :KEY].reshape(CONV, heads * KEY),
            conv_filters[:, :, KEY : 2 * KEY].reshape(CONV, heads * KEY),
            conv_filters[:, :, 2 * KEY :].reshape(CONV, heads * VALUE),
        ],
        axis=1,
    )
    decays = decay_params.T
    mixed, *kept = mixer_forward(raw, filters, decays, doc_starts, heads)
    gated, gated_pull = jax.vjp(
        gated_norm,
        mixed.astype(f32).reshape(length, heads, VALUE),
        gate_rows.reshape(length, heads, VALUE),
        third_gain,
    )
    gated_low = exchange_seq(gated.astype(bf16).reshape(length, heads * VALUE), 0, 1)
    middle = inputs + forward_dot(gated_low, out_full)
    second_norm, second_pull = jax.vjp(rms_norm, middle, second_gain)
    hidden = second_norm.astype(bf16)
    both_ffn = forward_dot(hidden, ffn_full)
    activated, swiglu_pull = jax.vjp(swiglu, both_ffn[:, :ff], both_ffn[:, ff:])
    activated_low = activated.astype(bf16)
    block_out = (middle + forward_dot(activated_low, down_full)).astype(bf16)

    cotangent = out_cotangent[0]
    act_grad = times_transposed(cotangent, down_full)
    down_grad = transposed_times(activated_low, cotangent).astype(bf16)
    both_grad = jnp.concatenate([g.astype(bf16) for g in swiglu_pull(act_grad)], axis=1)
    ffn_grad = transposed_times(hidden, both_grad).astype(bf16)
    hidden_grad = times_transposed(both_grad, ffn_full)
    middle_part, ffn_gain_grad = second_pull(hidden_grad)
    middle_grad = cotangent.astype(f32) + middle_part
    branch_low = middle_grad.astype(bf16)
    out_grad = transposed_times(gated_low, branch_low).astype(bf16)
    gated_grad = exchange_seq(times_transposed(branch_low, out_full).astype(bf16), 1, 0)
    mixed_grad, gate_rows_grad, out_gain_grad = gated_pull(
        gated_grad.astype(f32).reshape(length, heads, VALUE)
    )
    raw_grad, filters_grad, decays_grad = mixer_backward(
        raw,
        filters,
        decays,
        doc_starts,
        mixed_grad.astype(bf16).reshape(length, heads * VALUE),
        kept,
        heads,
    )
    gate_low = gate_rows_grad.astype(bf16).reshape(length, heads * VALUE)
    normed_grad = times_transposed(raw_grad, raw_full) + times_transposed(gate_low, gate_full)
    raw_weight_grad = transposed_times(normed, raw_grad).astype(bf16)
    gate_weight_grad = transposed_times(normed, gate_low).astype(bf16)
    norm_gain_grad = jnp.sum(normed_grad * all_scaled, axis=0)
    own_normed_grad = sum_scatter_seq(normed_grad, 0)
    _, first_pull = jax.vjp(lambda v: rms_norm(v, first_gain), inputs)
    tokens_grad = middle_grad + first_pull(own_normed_grad)[0]

    down_share = sum_seq(scatter_shard(down_grad))
    ffn_share = sum_seq(scatter_shard(ffn_grad))
    out_share = sum_seq(scatter_shard(out_grad))
    gate_share = gather_seq(scatter_shard(gate_weight_grad), 1).astype(f32)
    raw_share = scatter_shard(raw_weight_grad)
    query_share = gather_seq(raw_share[:, : heads * KEY], 1).astype(f32)
    key_share = gather_seq(raw_share[:, heads * KEY : 2 * heads * KEY], 1).astype(f32)
    value_share = gather_seq(raw_share[:, 2 * heads * KEY : width], 1).astype(f32)
    logit_share = jnp.stack(
        [
            raw_share[:, width : width + heads],
            raw_share[:, width + heads : width + 2 * heads],
        ],
        axis=2,
    ).reshape(rows, 2 * heads)
    logit_share = gather_seq(logit_share, 1).astype(f32)

    filters_grad = jnp.sum(filters_grad.reshape(CONV, 8, width), axis=1)
    filters_grad, decays_grad = lax.psum((filters_grad, decays_grad), "shard")
    split = (heads * KEY, 2 * heads * KEY)
    filters_out = jnp.concatenate(
        [
            filters_grad[:, : split[0]].reshape(CONV, heads, KEY),
            filters_grad[:, split[0] : split[1]].reshape(CONV, heads, KEY),
            filters_grad[:, split[1] :].reshape(CONV, heads, VALUE),
        ],
        axis=2,
    )
    gains = lax.psum((norm_gain_grad, out_gain_grad, ffn_gain_grad), ("seq", "shard"))
    place = lax.axis_index("shard")
    gains = [
        lax.dynamic_slice_in_dim(g, place * (g.shape[0] // shards), g.shape[0] // shards)
        for g in gains
    ]
    return (
        block_out[None],
        tokens_grad[None],
        gains[0],
        query_share,
        key_share,
        value_share,
        gate_share,
        logit_share,
        filters_out,
        decays_grad.T,
        gains[1],
        out_share,
        gains[2],
        ffn_share[:, :ff],
        ffn_share[:, ff:],
        down_share,
    )


def solution(mesh):
    in_specs = (
        P("shard", "seq", None),
        P("shard", None),
        P("shard"),
        P("shard", None),
        P("shard", None),
        P("shard", None),
        P("shard", None),
        P("shard", None),
        P(None, "seq", None),
        P("seq", None),
        P("shard"),
        P("shard", None),
        P("shard"),
        P("shard", None),
        P("shard", None),
        P("shard", None),
        P("shard", "seq", None),
    )
    out_specs = (
        P("shard", "seq", None),
        P("shard", "seq", None),
        P("shard"),
        P("shard", None),
        P("shard", None),
        P("shard", None),
        P("shard", None),
        P("shard", None),
        P(None, "seq", None),
        P("seq", None),
        P("shard"),
        P("shard", None),
        P("shard"),
        P("shard", None),
        P("shard", None),
        P("shard", None),
    )
    return jax.shard_map(
        on_device, mesh=mesh, in_specs=in_specs, out_specs=out_specs, check_vma=False
    )
```

```python
import functools

import jax
import jax.numpy as jnp
from jax import lax
from jax.experimental import pallas as pl
from jax.experimental.pallas import tpu as pltpu
from jax.sharding import PartitionSpec as P

HEADS = 8
KEY = 128
VALUE = 256
CONV = 4
GROUP = 64
HALO = 16
SUB = 4
epsilon = 1e-06
f32 = jnp.float32
bf16 = jnp.bfloat16


def dot(a, b, ca=1, cb=0):
    return lax.dot_general(a, b, (((ca,), (cb,)), ((), ())), preferred_element_type=f32)


def iota(shape, dim):
    return lax.broadcasted_iota(jnp.int32, shape, dim)


def doc_count(starts_ref, times):
    count = jnp.zeros(times.shape, jnp.int32)
    for s in range(starts_ref.shape[1]):
        count = count + jnp.where(times >= starts_ref[0, s], 1, 0)
    return count


def scalar_doc(starts_ref, time):
    count = 0
    for s in range(starts_ref.shape[1]):
        count = count + (time >= starts_ref[0, s]).astype(jnp.int32)
    return count


def per_head(cols, heads, width):
    rows = cols.shape[0]
    lane = iota((rows, heads * width), 1)
    out = jnp.broadcast_to(cols[:, heads - 1 : heads], (rows, heads * width))
    for h in range(heads - 2, -1, -1):
        out = jnp.where(lane < (h + 1) * width, cols[:, h : h + 1], out)
    return out


def head_sums(panel, heads, width):
    lane = iota(panel.shape, 1)
    sums = []
    for h in range(heads):
        inside = (lane >= h * width) & (lane < (h + 1) * width)
        sums.append(jnp.sum(jnp.where(inside, panel, 0.0), axis=1, keepdims=True))
    return columns(sums)


def columns(parts):
    rows = parts[0].shape[0]
    lane = iota((rows, len(parts)), 1)
    out = jnp.broadcast_to(parts[-1], (rows, len(parts)))
    for h in range(len(parts) - 2, -1, -1):
        out = jnp.where(lane == h, parts[h], out)
    return out


def block_diagonal(panel, heads):
    if heads == 1:
        return panel
    lane = iota(panel.shape, 1)
    zero = jnp.zeros_like(panel)
    parts = []
    for h in range(heads):
        inside = (lane >= h * GROUP) & (lane < (h + 1) * GROUP)
        parts.append(jnp.where(inside, panel, zero))
    return jnp.concatenate(parts, axis=0)


def diagonal_panel(full, heads):
    if heads == 1:
        return full
    lane = iota((GROUP, heads * GROUP), 1)
    out = full[(heads - 1) * GROUP :]
    for h in range(heads - 2, -1, -1):
        out = jnp.where(lane < (h + 1) * GROUP, full[h * GROUP : (h + 1) * GROUP], out)
    return out


def key_diagonal(keys):
    heads = len(keys)
    if heads == 1:
        return keys[0]
    zero = jnp.zeros_like(keys[0])
    rows = []
    for h in range(heads):
        rows.append(jnp.concatenate([keys[h] if o == h else zero for o in range(heads)], axis=1))
    return jnp.concatenate(rows, axis=0)


def scan_rows(values, reverse=False):
    rows = values.shape[0]
    index = iota(values.shape, 0)
    step = 1
    while step < rows:
        if reverse:
            moved = pltpu.roll(values, rows - step, 0)
            values = values + jnp.where(index < rows - step, moved, 0.0)
        else:
            moved = pltpu.roll(values, step, 0)
            values = values + jnp.where(index >= step, moved, 0.0)
        step *= 2
    return values


def sigmoid(v):
    return 1.0 / (1.0 + jnp.exp(-v))


def softplus(v):
    return jnp.maximum(v, 0.0) + jnp.log(1.0 + jnp.exp(-jnp.abs(v)))


class Block:
    def __init__(self, heads, base, raw_ref, value_ref, filters_ref, decay_ref, starts_ref):
        self.heads = heads
        width = 2 * heads * KEY
        times = base + iota((GROUP, 1), 0)
        docs = doc_count(starts_ref, times)
        self.masks = [
            (docs == doc_count(starts_ref, times - o)).astype(f32) for o in range(1, CONV)
        ]
        self.base = base
        self.raw_ref = raw_ref
        self.value_ref = value_ref
        self.filters_ref = filters_ref
        self.query, self.keys, self.query_pre, self.key_pre = [], [], [], []
        self.query_conv, self.key_conv, self.query_scale, self.key_scale = [], [], [], []
        for h in range(heads):
            pre = self.convolve(h * KEY, KEY)
            conv = pre * sigmoid(pre)
            scale = lax.rsqrt(jnp.sum(conv * conv, axis=1, keepdims=True) + epsilon)
            self.query_pre.append(pre)
            self.query_conv.append(conv)
            self.query_scale.append(scale)
            self.query.append(conv * scale * KEY ** (-0.5))
        for h in range(heads):
            pre = self.convolve((heads + h) * KEY, KEY)
            conv = pre * sigmoid(pre)
            scale = lax.rsqrt(jnp.sum(conv * conv, axis=1, keepdims=True) + epsilon)
            self.key_pre.append(pre)
            self.key_conv.append(conv)
            self.key_scale.append(scale)
            self.keys.append(conv * scale)
        logits = raw_ref[pl.ds(base, GROUP), width : width + KEY].astype(f32)
        self.strength = sigmoid(logits[:, :heads])
        self.decay_logit = logits[:, heads : 2 * heads] + decay_ref[1:2, :heads]
        self.decay_rate = -jnp.exp(decay_ref[0:1, :heads])
        self.log_decay = self.decay_rate * softplus(self.decay_logit)
        sums = scan_rows(self.log_decay)
        self.sums = sums
        last = sums[GROUP - 1 : GROUP]
        before = scalar_doc(starts_ref, base - 1)
        final = scalar_doc(starts_ref, base + GROUP - 1)
        self.entering = jnp.where(docs == before, jnp.exp(sums), 0.0)
        same_last = docs == final
        self.leaving = jnp.where(same_last, jnp.exp(jnp.where(same_last, last - sums, 0.0)), 0.0)
        self.retain = self.entering[GROUP - 1 : GROUP]
        shape = (GROUP, heads * GROUP)
        row = iota(shape, 0)
        place = jnp.bitwise_and(iota(shape, 1), GROUP - 1)
        self.row, self.place = row, place
        across = jnp.bitwise_and(iota((1, heads * GROUP), 1), GROUP - 1)
        docs_across = doc_count(starts_ref, base + across)
        same = docs == docs_across
        self.inclusive = same & (row >= place)
        self.strict = same & (row > place)
        sums_down = per_head(sums, heads, GROUP)
        sums_across = jnp.sum(jnp.where(row == place, sums_down, 0.0), axis=0, keepdims=True)
        gap = jnp.where(self.inclusive, sums_down - sums_across, 0.0)
        self.fade = jnp.where(self.inclusive, jnp.exp(gap), 0.0)
        self.strength_down = per_head(self.strength, heads, GROUP)
        low_keys = [k.astype(bf16) for k in self.keys]
        low_query = [q.astype(bf16) for q in self.query]
        self.low_keys, self.low_query = low_keys, low_query
        self.key_diag = key_diagonal(low_keys)
        left = jnp.concatenate(
            [jnp.concatenate(low_keys, axis=1), jnp.concatenate(low_query, axis=1)], axis=0
        )
        self.query_key_rows = left
        grams = dot(left, self.key_diag, 1, 1)
        self.key_gram = grams[:GROUP]
        self.score_gram = grams[GROUP:]
        self.system = jnp.where(self.strict, self.strength_down * self.key_gram * self.fade, 0.0)
        self.scores = self.score_gram * self.fade

    def taps(self, start, width):
        source = self.raw_ref
        if start >= 2 * self.heads * KEY:
            source = self.value_ref
            start = start - 2 * self.heads * KEY
        current = source[pl.ds(self.base, GROUP), start : start + width].astype(f32)
        earlier = pl.multiple_of(jnp.maximum(self.base - HALO, 0), HALO)
        halo = source[pl.ds(earlier, HALO), start : start + width].astype(f32)
        extended = jnp.concatenate([halo, current], axis=0)
        return [current] + [
            pltpu.roll(extended, o, 0)[HALO:] * self.masks[o - 1] for o in range(1, CONV)
        ]

    def convolve(self, start, width):
        taps = self.taps(start, width)
        filters = self.filters_ref[:, start : start + width]
        total = taps[0] * filters[CONV - 1 : CONV]
        for o in range(1, CONV):
            total = total + taps[o] * filters[CONV - 1 - o : CONV - o]
        return total


def inverse(system, heads, row, place):
    eye = (row == place).astype(f32)

    def part(size):
        apart = jnp.bitwise_xor(row, place)
        return jnp.where((apart >= size) & (apart < 2 * size), system, 0.0)

    result = eye - part(1)
    size = 2
    while size < GROUP:
        low = result.astype(bf16)
        inner = dot(part(size).astype(bf16), block_diagonal(low, heads))
        result = result - dot(low, block_diagonal(inner.astype(bf16), heads))
        size *= 2
    return result


def forward_kernel(
    heads, starts_ref, raw_ref, value_ref, filters_ref, decay_ref, gate_ref, gain_ref,
    gated_ref, mixed_ref, inverse_ref, delta_ref, rest_ref, memory_ref, state,
):
    step = pl.program_id(0)

    @pl.when(step == 0)
    def _():
        state[...] = jnp.zeros_like(state)

    blocks = []
    for s in range(SUB):
        base = pl.multiple_of((step * SUB + s) * GROUP, GROUP)
        block = Block(heads, base, raw_ref, value_ref, filters_ref, decay_ref, starts_ref)
        block.values = []
        for h in range(heads):
            pre = block.convolve(2 * heads * KEY + h * VALUE, VALUE)
            block.values.append(pre * sigmoid(pre))
        block.solve = inverse(block.system, heads, block.row, block.place).astype(bf16)
        inverse_ref[s * GROUP : (s + 1) * GROUP] = block.solve
        blocks.append(block)
    for s, block in enumerate(blocks):
        from_state, rest, right = [], [], []
        for h in range(heads):
            entering = block.entering[:, h : h + 1]
            memory = state[h * KEY : (h + 1) * KEY].astype(bf16)
            memory_ref[(s * heads + h) * KEY : (s * heads + h + 1) * KEY] = memory
            both = jnp.concatenate([entering * block.keys[h], entering * block.query[h]], axis=0)
            read = dot(both.astype(bf16), memory)
            from_state.append(read[GROUP:])
            missing = block.values[h] - read[:GROUP]
            rest.append(missing.astype(bf16))
            right.append((block.strength[:, h : h + 1] * missing).astype(bf16))
        rest_ref[s * heads * GROUP : (s + 1) * heads * GROUP] = jnp.concatenate(rest, axis=0)
        delta = dot(block_diagonal(block.solve, heads), jnp.concatenate(right, axis=0)).astype(bf16)
        delta_ref[s * heads * GROUP : (s + 1) * heads * GROUP] = delta
        outputs = dot(block_diagonal(block.scores.astype(bf16), heads), delta)
        for h in range(heads):
            rows = slice(h * GROUP, (h + 1) * GROUP)
            out = from_state[h] + outputs[rows]
            here = slice(s * GROUP, (s + 1) * GROUP)
            lanes = slice(h * VALUE, (h + 1) * VALUE)
            low = out.astype(bf16)
            mixed_ref[here, lanes] = low
            low = low.astype(f32)
            gate = gate_ref[here, lanes]
            scale = lax.rsqrt(jnp.mean(low * low, axis=1, keepdims=True) + epsilon)
            gated = low * scale * gain_ref[0:1] * (gate * sigmoid(gate))
            gated_ref[here, lanes] = gated.astype(bf16)
            leaving = (block.leaving[:, h : h + 1] * block.keys[h]).astype(bf16)
            keep = block.retain[:, h : h + 1]
            own = slice(h * KEY, (h + 1) * KEY)
            state[own] = keep * state[own] + dot(leaving, delta[rows], 0, 0)


def silu_slope(pre):
    gate = sigmoid(pre)
    return gate * (1.0 + pre * (1.0 - gate))


def backward_kernel(
    heads, starts_ref, raw_ref, value_ref, filters_ref, decay_ref, gate_ref, gain_ref,
    gated_grad_ref, mixed_ref, inverse_ref, delta_ref, rest_ref, memory_ref,
    raw_grad_ref, value_grad_ref, gate_grad_ref, filters_grad_ref, decay_grad_ref, gain_grad_ref,
    state, halo,
):
    step = pl.program_id(0)
    steps = pl.num_programs(0)
    width = 2 * heads * KEY

    @pl.when(step == 0)
    def _():
        state[...] = jnp.zeros_like(state)
        gain_grad_ref[...] = jnp.zeros_like(gain_grad_ref)
        halo[...] = jnp.zeros_like(halo)
        filters_grad_ref[...] = jnp.zeros_like(filters_grad_ref)
        decay_grad_ref[...] = jnp.zeros_like(decay_grad_ref)

    for s in range(SUB - 1, -1, -1):
        base = pl.multiple_of(((steps - 1 - step) * SUB + s) * GROUP, GROUP)
        block = Block(heads, base, raw_ref, value_ref, filters_ref, decay_ref, starts_ref)
        here = slice(s * GROUP, (s + 1) * GROUP)
        stacked = slice(s * heads * GROUP, (s + 1) * heads * GROUP)
        solve = inverse_ref[here]
        delta = delta_ref[stacked]
        rest = rest_ref[stacked]
        mixed_grads = []
        for h in range(heads):
            lanes = slice(h * VALUE, (h + 1) * VALUE)
            grad = gated_grad_ref[here, lanes].astype(f32)
            mixed = mixed_ref[here, lanes].astype(f32)
            gate = gate_ref[here, lanes]
            scale = lax.rsqrt(jnp.mean(mixed * mixed, axis=1, keepdims=True) + epsilon)
            unit = mixed * scale
            open_gate = sigmoid(gate)
            swish = gate * open_gate
            along = grad * unit
            product = (along * swish).reshape(GROUP // 8, 8, VALUE)
            gain_grad_ref[...] = gain_grad_ref[...] + jnp.sum(product, axis=0)
            gate_grad = along * gain_ref[0:1] * (open_gate * (1.0 + gate * (1.0 - open_gate)))
            gate_grad_ref[here, lanes] = gate_grad.astype(bf16)
            unit_grad = grad * swish * gain_ref[0:1]
            inner = jnp.mean(unit_grad * unit, axis=1, keepdims=True)
            mixed_grads.append((scale * (unit_grad - unit * inner)).astype(bf16))
        out_grad = jnp.concatenate(mixed_grads, axis=0)
        later = [state[h * KEY : (h + 1) * KEY] for h in range(heads)]
        later_low = [m.astype(bf16) for m in later]
        leaving = [
            (block.leaving[:, h : h + 1] * block.keys[h]).astype(bf16) for h in range(heads)
        ]
        pulled = jnp.concatenate([dot(leaving[h], later_low[h]) for h in range(heads)], axis=0)
        delta_grad = pulled + dot(block_diagonal(block.scores.astype(bf16), heads), out_grad, 0, 0)
        right_grad = dot(block_diagonal(solve, heads), delta_grad.astype(bf16), 0, 0)
        rest_grad, strength_grad = [], []
        for h in range(heads):
            rows = slice(h * GROUP, (h + 1) * GROUP)
            rest_grad.append(block.strength[:, h : h + 1] * right_grad[rows])
            strength_grad.append(
                jnp.sum(right_grad[rows] * rest[rows].astype(f32), axis=1, keepdims=True)
            )
        rest_low = [r.astype(bf16) for r in rest_grad]
        entering_query_grad, entering_key_grad, leaving_key_grad, retain_grad = [], [], [], []
        for h in range(heads):
            rows = slice(h * GROUP, (h + 1) * GROUP)
            entering = block.entering[:, h : h + 1]
            memory = memory_ref[(s * heads + h) * KEY : (s * heads + h + 1) * KEY]
            pair = jnp.concatenate([out_grad[rows], rest_low[h]], axis=0)
            back = dot(pair, memory, 1, 1)
            entering_query_grad.append(back[:GROUP])
            entering_key_grad.append(-back[GROUP:])
            leaving_key_grad.append(dot(delta[rows], later_low[h], 1, 1))
            product = later[h] * memory.astype(f32)
            retain_grad.append(
                jnp.sum(jnp.sum(product, axis=0, keepdims=True), axis=1, keepdims=True)
            )
            left = jnp.concatenate(
                [entering * block.query[h], -entering * block.keys[h]], axis=0
            ).astype(bf16)
            state[h * KEY : (h + 1) * KEY] = (
                block.retain[:, h : h + 1] * later[h] + dot(left, pair, 0, 0)
            )
        right_low = right_grad.astype(bf16)
        score_part = diagonal_panel(dot(out_grad, delta, 1, 1), heads)
        system_part = diagonal_panel(dot(right_low, delta, 1, 1), heads)
        scores_grad = jnp.where(block.inclusive, score_part, 0.0)
        system_grad = jnp.where(block.strict, -system_part, 0.0)
        score_gram_grad = scores_grad * block.fade
        faded = system_grad * block.fade
        key_gram_grad = block.strength_down * faded
        gap_grad = score_gram_grad * block.score_gram + key_gram_grad * block.key_gram
        strength_panel = head_sums(faded * block.key_gram, heads, GROUP)
        down = jnp.sum(gap_grad, axis=0, keepdims=True)
        gap_rows = head_sums(
            gap_grad - jnp.where(block.row == block.place, down, 0.0), heads, GROUP
        )
        both_low = jnp.concatenate([key_gram_grad, score_gram_grad], axis=0).astype(bf16)
        straight = dot(both_low, block.key_diag)
        turned = dot(both_low, block.query_key_rows, 0, 0)
        entering_grad, leaving_grad = [], []
        for h in range(heads):
            lanes = slice(h * KEY, (h + 1) * KEY)
            entering = block.entering[:, h : h + 1]
            fading = block.leaving[:, h : h + 1]
            query_grad = entering * entering_query_grad[h] + straight[GROUP:, lanes]
            key_grad = (
                turned[h * GROUP : (h + 1) * GROUP, lanes]
                + straight[:GROUP, lanes]
                + fading * leaving_key_grad[h]
                + entering * entering_key_grad[h]
            )
            entering_grad.append(
                jnp.sum(
                    entering_query_grad[h] * block.query[h] + entering_key_grad[h] * block.keys[h],
                    axis=1,
                    keepdims=True,
                )
            )
            leaving_grad.append(
                jnp.sum(leaving_key_grad[h] * block.keys[h], axis=1, keepdims=True)
            )
            for start, grad, conv, scale, pre, factor in (
                (h * KEY, query_grad, block.query_conv[h], block.query_scale[h],
                 block.query_pre[h], KEY ** (-0.5)),
                ((heads + h) * KEY, key_grad, block.key_conv[h], block.key_scale[h],
                 block.key_pre[h], 1.0),
            ):
                along = jnp.sum(grad * conv, axis=1, keepdims=True)
                conv_grad = (factor * scale) * (grad - conv * (scale * scale * along))
                convolve_back(
                    block, s, start, start, KEY, conv_grad * silu_slope(pre), starts_ref,
                    raw_grad_ref, filters_grad_ref, halo,
                )
            start = 2 * heads * KEY + h * VALUE
            pre = block.convolve(start, VALUE)
            convolve_back(
                block, s, start, h * VALUE, VALUE, rest_grad[h] * silu_slope(pre), starts_ref,
                value_grad_ref, filters_grad_ref, halo,
            )
        entering_grad = columns(entering_grad) * block.entering
        leaving_grad = columns(leaving_grad) * block.leaving
        strength_grad = columns(strength_grad) + strength_panel
        retain_grad = columns(retain_grad) * block.retain
        at_last = jnp.sum(leaving_grad, axis=0, keepdims=True) + retain_grad
        index = iota((GROUP, heads), 0)
        sums_grad = (
            entering_grad - leaving_grad + gap_rows + jnp.where(index == GROUP - 1, at_last, 0.0)
        )
        log_decay_grad = scan_rows(sums_grad, reverse=True)
        logit_grad = log_decay_grad * block.decay_rate * sigmoid(block.decay_logit)
        beta_grad = strength_grad * block.strength * (1.0 - block.strength)
        lane = iota((GROUP, KEY), 1)
        packed = jnp.zeros((GROUP, KEY), f32)
        for h in range(heads):
            packed = jnp.where(lane == h, beta_grad[:, h : h + 1], packed)
            packed = jnp.where(lane == heads + h, logit_grad[:, h : h + 1], packed)
        raw_grad_ref[here, width : width + KEY] = packed.astype(bf16)
        scale_sum = jnp.sum(log_decay_grad * block.log_decay, axis=0, keepdims=True)
        bias_sum = jnp.sum(logit_grad, axis=0, keepdims=True)
        decay_grad_ref[0:1] = decay_grad_ref[0:1] + scale_sum
        decay_grad_ref[1:2] = decay_grad_ref[1:2] + bias_sum


def convolve_back(
    block, s, start, place, width, pre_grad, starts_ref, grad_ref, filters_grad_ref, halo
):
    lanes = slice(start, start + width)
    taps = block.taps(start, width)
    for o in range(CONV):
        j = CONV - 1 - o
        product = (pre_grad * taps[o]).reshape(GROUP // 8, 8, width)
        filters_grad_ref[j * 8 : (j + 1) * 8, lanes] = filters_grad_ref[
            j * 8 : (j + 1) * 8, lanes
        ] + jnp.sum(product, axis=0)
    filters = block.filters_ref[:, lanes]
    extended = jnp.concatenate([pre_grad, halo[:, lanes]], axis=0)
    rows = GROUP + 8
    times = block.base + iota((rows, 1), 0)
    docs = doc_count(starts_ref, times)
    total = pre_grad * filters[CONV - 1 : CONV]
    for o in range(1, CONV):
        mask = (docs == doc_count(starts_ref, times - o)).astype(f32)
        moved = pltpu.roll(extended * mask, rows - o, 0)[:GROUP]
        total = total + moved * filters[CONV - 1 - o : CONV - o]
    grad_ref[s * GROUP : (s + 1) * GROUP, place : place + width] = total.astype(bf16)
    halo[:, lanes] = pre_grad[:8]


SPACE = 56 * 2**20


def mixer_forward(raw, values, filters, decays, starts, gates, gain, heads):
    length, wide = raw.shape
    steps = length // (SUB * GROUP)
    rows = SUB * GROUP
    blocks = length // GROUP
    whole = lambda a: pl.BlockSpec(a.shape, lambda i: (0, 0))
    part = lambda r, c: pl.BlockSpec((r, c), lambda i: (i, 0))
    return pl.pallas_call(
        functools.partial(forward_kernel, heads),
        grid=(steps,),
        in_specs=[
            pl.BlockSpec(memory_space=pltpu.SMEM),
            whole(raw),
            whole(values),
            whole(filters),
            whole(decays),
            part(rows, heads * VALUE),
            whole(gain),
        ],
        out_specs=[
            part(rows, heads * VALUE),
            part(rows, heads * VALUE),
            part(rows, heads * GROUP),
            part(rows * heads, VALUE),
            part(rows * heads, VALUE),
            part(SUB * heads * KEY, VALUE),
        ],
        out_shape=[
            jax.ShapeDtypeStruct((length, heads * VALUE), bf16),
            jax.ShapeDtypeStruct((length, heads * VALUE), bf16),
            jax.ShapeDtypeStruct((length, heads * GROUP), bf16),
            jax.ShapeDtypeStruct((length * heads, VALUE), bf16),
            jax.ShapeDtypeStruct((length * heads, VALUE), bf16),
            jax.ShapeDtypeStruct((blocks * heads * KEY, VALUE), bf16),
        ],
        scratch_shapes=[pltpu.VMEM((heads * KEY, VALUE), f32)],
        compiler_params=pltpu.CompilerParams(vmem_limit_bytes=SPACE),
        cost_estimate=pl.CostEstimate(
            flops=length * heads * 11_000_000, bytes_accessed=2**24, transcendentals=0
        ),
        name="mixer_forward",
    )(starts, raw, values, filters, decays, gates, gain)


def mixer_backward(raw, values, filters, decays, starts, gates, gain, gated_grad, kept, heads):
    length, wide = raw.shape
    steps = length // (SUB * GROUP)
    rows = SUB * GROUP
    whole = lambda a: pl.BlockSpec(a.shape, lambda i: (0, 0))
    same = lambda r, c: pl.BlockSpec((r, c), lambda i: (0, 0))
    part = lambda r, c: pl.BlockSpec((r, c), lambda i: (steps - 1 - i, 0))
    return pl.pallas_call(
        functools.partial(backward_kernel, heads),
        grid=(steps,),
        in_specs=[
            pl.BlockSpec(memory_space=pltpu.SMEM),
            whole(raw),
            whole(values),
            whole(filters),
            whole(decays),
            part(rows, heads * VALUE),
            whole(gain),
            part(rows, heads * VALUE),
            part(rows, heads * VALUE),
            part(rows, heads * GROUP),
            part(rows * heads, VALUE),
            part(rows * heads, VALUE),
            part(SUB * heads * KEY, VALUE),
        ],
        out_specs=[
            part(rows, wide),
            part(rows, heads * VALUE),
            part(rows, heads * VALUE),
            same(8 * CONV, filters.shape[1]),
            same(2, heads),
            same(8, VALUE),
        ],
        out_shape=[
            jax.ShapeDtypeStruct((length, wide), bf16),
            jax.ShapeDtypeStruct((length, heads * VALUE), bf16),
            jax.ShapeDtypeStruct((length, heads * VALUE), bf16),
            jax.ShapeDtypeStruct((8 * CONV, filters.shape[1]), f32),
            jax.ShapeDtypeStruct((2, heads), f32),
            jax.ShapeDtypeStruct((8, VALUE), f32),
        ],
        scratch_shapes=[
            pltpu.VMEM((heads * KEY, VALUE), f32),
            pltpu.VMEM((8, filters.shape[1]), f32),
        ],
        compiler_params=pltpu.CompilerParams(vmem_limit_bytes=SPACE),
        cost_estimate=pl.CostEstimate(
            flops=length * heads * 14_000_000, bytes_accessed=2**24, transcendentals=0
        ),
        name="mixer_backward",
    )(starts, raw, values, filters, decays, gates, gain, gated_grad, *kept)


def forward_dot(left_side, right_side):
    return jnp.dot(left_side, right_side, preferred_element_type=f32)


def times_transposed(left_side, right_side):
    return dot(left_side, right_side, 1, 1)


def transposed_times(left_side, right_side):
    return dot(left_side, right_side, 0, 0)


def rms_norm(values, gain):
    return values * lax.rsqrt(jnp.mean(values * values, axis=-1, keepdims=True) + epsilon) * gain


def swiglu(gate_rows, up_rows):
    return jax.nn.silu(gate_rows) * up_rows


def swap_seq(values):
    return lax.ppermute(values, "seq", [(0, 1), (1, 0)])


def in_order(own, other, axis):
    first = lax.axis_index("seq") == 0
    return jnp.where(
        first,
        jnp.concatenate([own, other], axis=axis),
        jnp.concatenate([other, own], axis=axis),
    )


def gather_seq(values, axis):
    if lax.axis_size("seq") == 2:
        return in_order(values, swap_seq(values), axis)
    return lax.all_gather(values, "seq", axis=axis, tiled=True)


def own_part(values, axis, index=None):
    size = values.shape[axis] // lax.axis_size("seq")
    index = lax.axis_index("seq") if index is None else index
    return lax.dynamic_slice_in_dim(values, index * size, size, axis=axis)


def sum_scatter_seq(values, axis):
    if lax.axis_size("seq") == 2:
        other = own_part(values, axis, 1 - lax.axis_index("seq")).astype(bf16)
        return own_part(values, axis) + swap_seq(other).astype(f32)
    return lax.psum_scatter(
        values.astype(bf16), "seq", scatter_dimension=axis, tiled=True
    ).astype(f32)


def sum_seq(values):
    if lax.axis_size("seq") == 2:
        low = values.astype(bf16)
        return low.astype(f32) + swap_seq(low).astype(f32)
    return lax.psum(values.astype(bf16), "seq").astype(f32)


def own_first(values):
    if lax.axis_size("seq") == 2:
        return jnp.concatenate([values, swap_seq(values)], axis=0)
    return lax.all_gather(values, "seq", axis=0, tiled=True)


def sum_own_first(values):
    if lax.axis_size("seq") == 2:
        half = values.shape[0] // 2
        return values[:half] + swap_seq(values[half:].astype(bf16)).astype(f32)
    return sum_scatter_seq(values, 0)


def exchange_seq(values, split, join):
    if lax.axis_size("seq") == 2:
        other = own_part(values, split, 1 - lax.axis_index("seq"))
        return in_order(own_part(values, split), swap_seq(other), join)
    return lax.all_to_all(values, "seq", split_axis=split, concat_axis=join, tiled=True)


PLACES = 4


def in_grid():
    return lax.axis_size("shard") == 4 * PLACES and lax.axis_size("seq") == 2


def position():
    place = lax.axis_index("shard")
    return place // 4, (place // 2) % 2, place % 2


def flip(values, mask):
    size = lax.axis_size("shard")
    return lax.ppermute(values, "shard", [(i, i ^ mask) for i in range(size)])


def from_place(values, step):
    size = lax.axis_size("shard")
    return lax.ppermute(values, "shard", [(i, (i - 4 * step) % size) for i in range(size)])


def assemble_kernel(place_ref, *refs):
    *parts, out_ref = refs
    own = place_ref[1] * 2 + place_ref[2]
    for k, part in enumerate(parts):
        out_ref[0, jnp.bitwise_xor(own, k)] = part[0]


def gather_shard(values, direct=False):
    if not direct or not in_grid():
        return lax.all_gather(values, "shard", axis=0, tiled=True)
    rows, columns = values.shape
    along = jnp.concatenate([values] + [from_place(values, r) for r in range(1, PLACES)], axis=0)
    beside = flip(along, 2)
    parts = [along, flip(along, 1), beside, flip(beside, 1)]
    place = jnp.stack(position()).astype(jnp.int32)
    block = pl.BlockSpec((1, rows, columns), lambda r, place: (r, 0, 0))
    full = pl.pallas_call(
        assemble_kernel,
        grid_spec=pltpu.PrefetchScalarGridSpec(
            num_scalar_prefetch=1,
            grid=(PLACES,),
            in_specs=[block] * 4,
            out_specs=pl.BlockSpec(
                (1, 4, rows, columns), lambda r, place: (lax.rem(place[0] + r, PLACES), 0, 0, 0)
            ),
        ),
        out_shape=jax.ShapeDtypeStruct((PLACES, 4, rows, columns), values.dtype),
        compiler_params=pltpu.CompilerParams(vmem_limit_bytes=SPACE),
        cost_estimate=pl.CostEstimate(
            flops=0, bytes_accessed=64 * PLACES * rows * columns, transcendentals=0
        ),
        name="assemble",
    )(place, *[p.reshape(PLACES, rows, columns) for p in parts])
    return full.reshape(4 * PLACES * rows, columns)


def scatter_shard(values, direct=False):
    if not direct or not in_grid():
        low = values.astype(bf16)
        return lax.psum_scatter(low, "shard", scatter_dimension=0, tiled=True).astype(f32)
    z, y, core = position()
    rows, columns = values.shape
    rows = rows // (4 * PLACES)

    def pick(array, index, axis):
        return lax.dynamic_index_in_dim(array, index, axis, keepdims=False)

    values = values.reshape(PLACES, 2, 2, rows, columns)
    held = pick(values, core, 2).astype(f32)
    held = (held + flip(pick(values, 1 - core, 2).astype(bf16), 1).astype(f32)).astype(bf16)
    kept = pick(held, y, 1).astype(f32)
    held = (kept + flip(pick(held, 1 - y, 1), 2).astype(f32)).astype(bf16)
    total = pick(held, z, 0).astype(f32)
    for r in range(1, PLACES):
        sent = pick(held, (z - r) % PLACES, 0)
        total = total + from_place(sent, r).astype(f32)
    return total


def sum_small(values, axes):
    if not in_grid():
        return lax.psum(values, axes)
    for mask in (1, 2, 4, 8):
        values = values + flip(values, mask)
    if "seq" in axes:
        values = values + swap_seq(values)
    return values


def on_device(
    tokens,
    doc_starts,
    norm_gain,
    query_weight,
    key_weight,
    value_weight,
    gate_weight,
    beta_decay_weight,
    conv_filters,
    decay_params,
    out_norm_gain,
    out_weight,
    ffn_norm_gain,
    ffn_gate_weight,
    ffn_up_weight,
    down_weight,
    out_cotangent,
):
    heads = HEADS // lax.axis_size("seq")
    shards = lax.axis_size("shard")
    rows = query_weight.shape[0]
    width = 2 * heads * KEY
    ff = ffn_gate_weight.shape[1]

    logit_weight = own_part(beta_decay_weight.reshape(rows, HEADS, 2), 1)
    gain_rows = out_norm_gain.shape[0]
    raw_piece = jnp.concatenate(
        [
            own_part(query_weight, 1),
            own_part(key_weight, 1),
            logit_weight[:, :, 0],
            logit_weight[:, :, 1],
            norm_gain[:, None],
            ffn_norm_gain[:, None],
            jnp.pad(out_norm_gain, (0, rows - gain_rows))[:, None],
            jnp.zeros((rows, KEY - 2 * heads - 3), bf16),
        ],
        axis=1,
    )
    units = ff // shards // lax.axis_size("seq")

    def own_units(weight):
        return own_part(weight.reshape(rows, shards, ff // shards), 2).reshape(rows, shards * units)

    gate_piece = own_part(gate_weight, 1)
    raw_wide = raw_piece.shape[1]
    first_full = gather_shard(jnp.concatenate([raw_piece, own_part(value_weight, 1)], axis=1))
    raw_full = first_full[:, :raw_wide]
    value_full = first_full[:, raw_wide:]
    gate_full = gather_shard(gate_piece, direct=True)
    half = shards * units
    model = out_weight.shape[1]
    out_wide = out_weight.size // rows
    rest_full = gather_shard(
        jnp.concatenate(
            [
                own_units(ffn_gate_weight),
                own_units(ffn_up_weight),
                out_weight.reshape(rows, out_wide),
                own_part(down_weight, 0).reshape(rows, units * model // rows),
            ],
            axis=1,
        )
    )
    ffn_full = rest_full[:, : 2 * half]
    out_full = rest_full[:, 2 * half : 2 * half + out_wide].reshape(shards * out_weight.shape[0], model)
    down_full = rest_full[:, 2 * half + out_wide :].reshape(half, model)
    first_gain = raw_full[:, width + 2 * heads].astype(f32)
    second_gain = raw_full[:, width + 2 * heads + 1].astype(f32)
    third_gain = (
        raw_full[:, width + 2 * heads + 2]
        .reshape(shards, rows)[:, :gain_rows]
        .reshape(1, shards * gain_rows)
        .astype(f32)
    )

    own_tokens = tokens[0]
    token_count = own_tokens.shape[0]
    inputs = own_tokens.astype(f32)
    all_inputs = gather_seq(own_tokens, 0).astype(f32)
    length = all_inputs.shape[0]
    all_scaled = all_inputs * lax.rsqrt(
        jnp.mean(all_inputs * all_inputs, axis=-1, keepdims=True) + epsilon
    )
    normed = (all_scaled * first_gain).astype(bf16)
    raw = forward_dot(normed, raw_full).astype(bf16)
    values = forward_dot(normed, value_full).astype(bf16)
    gate_rows = forward_dot(normed, gate_full)
    filters = jnp.concatenate(
        [
            conv_filters[:, :, :KEY].reshape(CONV, heads * KEY),
            conv_filters[:, :, KEY : 2 * KEY].reshape(CONV, heads * KEY),
            conv_filters[:, :, 2 * KEY :].reshape(CONV, heads * VALUE),
        ],
        axis=1,
    )
    decays = decay_params.T
    gated, *kept = mixer_forward(
        raw, values, filters, decays, doc_starts, gate_rows, third_gain, heads
    )
    gated_low = exchange_seq(gated, 0, 1)
    middle = inputs + forward_dot(gated_low, out_full)
    second_norm, second_pull = jax.vjp(rms_norm, middle, second_gain)
    hidden = own_first(second_norm.astype(bf16))
    cotangent = out_cotangent[0]
    all_cotangent = own_first(cotangent)
    both_ffn = forward_dot(hidden, ffn_full)
    activated, swiglu_pull = jax.vjp(swiglu, both_ffn[:, :half], both_ffn[:, half:])
    activated_low = activated.astype(bf16)
    act_grad = times_transposed(all_cotangent, down_full)
    both_grad = jnp.concatenate([g.astype(bf16) for g in swiglu_pull(act_grad)], axis=1)
    hidden_grad = sum_own_first(times_transposed(both_grad, ffn_full))
    block_out = (middle + sum_own_first(forward_dot(activated_low, down_full))).astype(bf16)
    down_grad = transposed_times(activated_low, all_cotangent).astype(bf16)
    ffn_grad = transposed_times(hidden, both_grad).astype(bf16)
    middle_part, ffn_gain_grad = second_pull(hidden_grad)
    middle_grad = cotangent.astype(f32) + middle_part
    branch_low = middle_grad.astype(bf16)
    out_grad = transposed_times(gated_low, branch_low).astype(bf16)
    gated_grad = exchange_seq(times_transposed(branch_low, out_full).astype(bf16), 1, 0)
    raw_grad, value_grad, gate_grad, filters_grad, decays_grad, out_gain_grad = mixer_backward(
        raw,
        values,
        filters,
        decays,
        doc_starts,
        gate_rows,
        third_gain,
        gated_grad,
        kept,
        heads,
    )
    normed_grad = (
        times_transposed(raw_grad, raw_full)
        + times_transposed(value_grad, value_full)
        + times_transposed(gate_grad, gate_full)
    )
    raw_weight_grad = transposed_times(normed, raw_grad).astype(bf16)
    value_weight_grad = transposed_times(normed, value_grad).astype(bf16)
    gate_weight_grad = transposed_times(normed, gate_grad).astype(bf16)
    norm_gain_grad = jnp.sum(normed_grad * all_scaled, axis=0)
    own_normed_grad = sum_scatter_seq(normed_grad, 0)
    _, first_pull = jax.vjp(lambda v: rms_norm(v, first_gain), inputs)
    tokens_grad = middle_grad + first_pull(own_normed_grad)[0]

    down_share = gather_seq(scatter_shard(down_grad).astype(bf16), 0).astype(f32)
    ffn_share = scatter_shard(ffn_grad).astype(bf16)

    def all_units(share):
        share = gather_seq(share.reshape(rows, shards, units), 2)
        return share.reshape(rows, ff).astype(f32)

    ffn_gate_share = all_units(ffn_share[:, :half])
    ffn_up_share = all_units(ffn_share[:, half:])
    out_share = sum_seq(scatter_shard(out_grad, direct=True))
    value_share = scatter_shard(value_weight_grad, direct=True).astype(bf16)
    value_share = gather_seq(value_share, 1).astype(f32)
    gate_share = scatter_shard(gate_weight_grad, direct=True).astype(bf16)
    gate_share = gather_seq(gate_share, 1).astype(f32)
    raw_share = scatter_shard(raw_weight_grad, direct=True).astype(bf16)
    query_share = gather_seq(raw_share[:, : heads * KEY], 1).astype(f32)
    key_share = gather_seq(raw_share[:, heads * KEY : width], 1).astype(f32)
    logit_share = jnp.stack(
        [
            raw_share[:, width : width + heads],
            raw_share[:, width + heads : width + 2 * heads],
        ],
        axis=2,
    ).reshape(rows, 2 * heads)
    logit_share = gather_seq(logit_share, 1).astype(f32)

    all_width = filters.shape[1]
    filters_grad = jnp.sum(filters_grad.reshape(CONV, 8, all_width), axis=1)
    own_sum = jnp.concatenate([filters_grad.reshape(CONV * all_width), decays_grad.reshape(-1)])
    own_sum = sum_small(own_sum, ("shard",))
    filters_grad = own_sum[: CONV * all_width].reshape(CONV, all_width)
    decays_grad = own_sum[CONV * all_width :].reshape(2, heads)
    split = (heads * KEY, 2 * heads * KEY)
    filters_out = jnp.concatenate(
        [
            filters_grad[:, : split[0]].reshape(CONV, heads, KEY),
            filters_grad[:, split[0] : split[1]].reshape(CONV, heads, KEY),
            filters_grad[:, split[1] :].reshape(CONV, heads, VALUE),
        ],
        axis=2,
    )
    lengths = [shards * n for n in (norm_gain.shape[0], gain_rows, ffn_norm_gain.shape[0])]
    gains = sum_small(
        jnp.concatenate([norm_gain_grad, jnp.sum(out_gain_grad, axis=0), ffn_gain_grad]),
        ("seq", "shard"),
    )
    gains = [
        gains[: lengths[0]],
        gains[lengths[0] : lengths[0] + lengths[1]],
        gains[lengths[0] + lengths[1] :],
    ]
    place = lax.axis_index("shard")
    gains = [
        lax.dynamic_slice_in_dim(g, place * (g.shape[0] // shards), g.shape[0] // shards)
        for g in gains
    ]
    return (
        block_out[None],
        tokens_grad[None],
        gains[0],
        query_share,
        key_share,
        value_share,
        gate_share,
        logit_share,
        filters_out,
        decays_grad.T,
        gains[1],
        out_share,
        gains[2],
        ffn_gate_share,
        ffn_up_share,
        down_share,
    )


def solution(mesh):
    in_specs = (
        P("shard", "seq", None),
        P("shard", None),
        P("shard"),
        P("shard", None),
        P("shard", None),
        P("shard", None),
        P("shard", None),
        P("shard", None),
        P(None, "seq", None),
        P("seq", None),
        P("shard"),
        P("shard", None),
        P("shard"),
        P("shard", None),
        P("shard", None),
        P("shard", None),
        P("shard", "seq", None),
    )
    out_specs = (
        P("shard", "seq", None),
        P("shard", "seq", None),
        P("shard"),
        P("shard", None),
        P("shard", None),
        P("shard", None),
        P("shard", None),
        P("shard", None),
        P(None, "seq", None),
        P("seq", None),
        P("shard"),
        P("shard", None),
        P("shard"),
        P("shard", None),
        P("shard", None),
        P("shard", None),
    )
    return jax.shard_map(
        on_device, mesh=mesh, in_specs=in_specs, out_specs=out_specs, check_vma=False
    )
```

```python
import functools

import jax
import jax.numpy as jnp
from jax import lax
from jax.experimental import pallas as pl
from jax.experimental.pallas import tpu as pltpu
from jax.sharding import PartitionSpec as P

HEADS = 8
KEY = 128
VALUE = 256
CONV = 4
GROUP = 64
HALO = 16
SUB = 4
epsilon = 1e-06
f32 = jnp.float32
bf16 = jnp.bfloat16


def dot(a, b, ca=1, cb=0):
    return lax.dot_general(a, b, (((ca,), (cb,)), ((), ())), preferred_element_type=f32)


def halves(values):
    high = values.astype(bf16)
    return high, (values - high.astype(f32)).astype(bf16)


def fine_dot(a, b, ca=1, cb=0):
    if not isinstance(a, tuple):
        return dot(a, b[0], ca, cb) + dot(a, b[1], ca, cb)
    if not isinstance(b, tuple):
        return dot(a[0], b, ca, cb) + dot(a[1], b, ca, cb)
    return dot(a[0], b[0], ca, cb) + (dot(a[0], b[1], ca, cb) + dot(a[1], b[0], ca, cb))


def iota(shape, dim):
    return lax.broadcasted_iota(jnp.int32, shape, dim)


def doc_count(starts_ref, times):
    count = jnp.zeros(times.shape, jnp.int32)
    for s in range(starts_ref.shape[1]):
        count = count + jnp.where(times >= starts_ref[0, s], 1, 0)
    return count


def scalar_doc(starts_ref, time):
    count = 0
    for s in range(starts_ref.shape[1]):
        count = count + (time >= starts_ref[0, s]).astype(jnp.int32)
    return count


def per_head(cols, heads, width):
    rows = cols.shape[0]
    lane = iota((rows, heads * width), 1)
    out = jnp.broadcast_to(cols[:, heads - 1 : heads], (rows, heads * width))
    for h in range(heads - 2, -1, -1):
        out = jnp.where(lane < (h + 1) * width, cols[:, h : h + 1], out)
    return out


def head_sums(panel, heads, width):
    lane = iota(panel.shape, 1)
    sums = []
    for h in range(heads):
        inside = (lane >= h * width) & (lane < (h + 1) * width)
        sums.append(jnp.sum(jnp.where(inside, panel, 0.0), axis=1, keepdims=True))
    return columns(sums)


def columns(parts):
    rows = parts[0].shape[0]
    lane = iota((rows, len(parts)), 1)
    out = jnp.broadcast_to(parts[-1], (rows, len(parts)))
    for h in range(len(parts) - 2, -1, -1):
        out = jnp.where(lane == h, parts[h], out)
    return out


def block_diagonal(panel, heads):
    if heads == 1:
        return panel
    lane = iota(panel.shape, 1)
    zero = jnp.zeros_like(panel)
    parts = []
    for h in range(heads):
        inside = (lane >= h * GROUP) & (lane < (h + 1) * GROUP)
        parts.append(jnp.where(inside, panel, zero))
    return jnp.concatenate(parts, axis=0)


def diagonal_panel(full, heads):
    if heads == 1:
        return full
    lane = iota((GROUP, heads * GROUP), 1)
    out = full[(heads - 1) * GROUP :]
    for h in range(heads - 2, -1, -1):
        out = jnp.where(lane < (h + 1) * GROUP, full[h * GROUP : (h + 1) * GROUP], out)
    return out


def key_diagonal(keys):
    heads = len(keys)
    if heads == 1:
        return keys[0]
    zero = jnp.zeros_like(keys[0])
    rows = []
    for h in range(heads):
        rows.append(jnp.concatenate([keys[h] if o == h else zero for o in range(heads)], axis=1))
    return jnp.concatenate(rows, axis=0)


def scan_rows(values, reverse=False):
    rows = values.shape[0]
    index = iota(values.shape, 0)
    step = 1
    while step < rows:
        if reverse:
            moved = pltpu.roll(values, rows - step, 0)
            values = values + jnp.where(index < rows - step, moved, 0.0)
        else:
            moved = pltpu.roll(values, step, 0)
            values = values + jnp.where(index >= step, moved, 0.0)
        step *= 2
    return values


def sigmoid(v):
    return 1.0 / (1.0 + jnp.exp(-v))


def softplus(v):
    return jnp.maximum(v, 0.0) + jnp.log(1.0 + jnp.exp(-jnp.abs(v)))


class Block:
    def __init__(self, heads, base, raw_ref, value_ref, filters_ref, decay_ref, starts_ref):
        self.heads = heads
        width = 2 * heads * KEY
        times = base + iota((GROUP, 1), 0)
        docs = doc_count(starts_ref, times)
        self.masks = [
            (docs == doc_count(starts_ref, times - o)).astype(f32) for o in range(1, CONV)
        ]
        self.base = base
        self.raw_ref = raw_ref
        self.value_ref = value_ref
        self.filters_ref = filters_ref
        self.query, self.keys, self.query_pre, self.key_pre = [], [], [], []
        self.query_conv, self.key_conv, self.query_scale, self.key_scale = [], [], [], []
        for h in range(heads):
            pre = self.convolve(h * KEY, KEY)
            conv = pre * sigmoid(pre)
            scale = lax.rsqrt(jnp.sum(conv * conv, axis=1, keepdims=True) + epsilon)
            self.query_pre.append(pre)
            self.query_conv.append(conv)
            self.query_scale.append(scale)
            self.query.append(conv * scale * KEY ** (-0.5))
        for h in range(heads):
            pre = self.convolve((heads + h) * KEY, KEY)
            conv = pre * sigmoid(pre)
            scale = lax.rsqrt(jnp.sum(conv * conv, axis=1, keepdims=True) + epsilon)
            self.key_pre.append(pre)
            self.key_conv.append(conv)
            self.key_scale.append(scale)
            self.keys.append(conv * scale)
        logits = raw_ref[pl.ds(base, GROUP), width : width + KEY].astype(f32)
        self.strength = sigmoid(logits[:, :heads])
        self.decay_logit = logits[:, heads : 2 * heads] + decay_ref[1:2, :heads]
        self.decay_rate = -jnp.exp(decay_ref[0:1, :heads])
        self.log_decay = self.decay_rate * softplus(self.decay_logit)
        sums = scan_rows(self.log_decay)
        self.sums = sums
        last = sums[GROUP - 1 : GROUP]
        before = scalar_doc(starts_ref, base - 1)
        final = scalar_doc(starts_ref, base + GROUP - 1)
        self.entering = jnp.where(docs == before, jnp.exp(sums), 0.0)
        same_last = docs == final
        self.leaving = jnp.where(same_last, jnp.exp(jnp.where(same_last, last - sums, 0.0)), 0.0)
        self.retain = self.entering[GROUP - 1 : GROUP]
        shape = (GROUP, heads * GROUP)
        row = iota(shape, 0)
        place = jnp.bitwise_and(iota(shape, 1), GROUP - 1)
        self.row, self.place = row, place
        across = jnp.bitwise_and(iota((1, heads * GROUP), 1), GROUP - 1)
        docs_across = doc_count(starts_ref, base + across)
        same = docs == docs_across
        self.inclusive = same & (row >= place)
        self.strict = same & (row > place)
        sums_down = per_head(sums, heads, GROUP)
        sums_across = jnp.sum(jnp.where(row == place, sums_down, 0.0), axis=0, keepdims=True)
        gap = jnp.where(self.inclusive, sums_down - sums_across, 0.0)
        self.fade = jnp.where(self.inclusive, jnp.exp(gap), 0.0)
        self.strength_down = per_head(self.strength, heads, GROUP)
        low_keys = [k.astype(bf16) for k in self.keys]
        low_query = [q.astype(bf16) for q in self.query]
        self.keys = [k.astype(f32) for k in low_keys]
        self.query = [q.astype(f32) for q in low_query]
        self.low_keys, self.low_query = low_keys, low_query
        self.key_diag = key_diagonal(low_keys)
        left = jnp.concatenate(
            [jnp.concatenate(low_keys, axis=1), jnp.concatenate(low_query, axis=1)], axis=0
        )
        self.query_key_rows = left
        grams = dot(left, self.key_diag, 1, 1)
        self.key_gram = grams[:GROUP]
        self.score_gram = grams[GROUP:]
        self.system = jnp.where(self.strict, self.strength_down * self.key_gram * self.fade, 0.0)
        self.scores = self.score_gram * self.fade

    def taps(self, start, width):
        source = self.raw_ref
        if start >= 2 * self.heads * KEY:
            source = self.value_ref
            start = start - 2 * self.heads * KEY
        current = source[pl.ds(self.base, GROUP), start : start + width].astype(f32)
        earlier = pl.multiple_of(jnp.maximum(self.base - HALO, 0), HALO)
        halo = source[pl.ds(earlier, HALO), start : start + width].astype(f32)
        extended = jnp.concatenate([halo, current], axis=0)
        return [current] + [
            pltpu.roll(extended, o, 0)[HALO:] * self.masks[o - 1] for o in range(1, CONV)
        ]

    def convolve(self, start, width):
        taps = self.taps(start, width)
        filters = self.filters_ref[:, start : start + width]
        total = taps[0] * filters[CONV - 1 : CONV]
        for o in range(1, CONV):
            total = total + taps[o] * filters[CONV - 1 - o : CONV - o]
        return total


def inverse(system, heads, row, place):
    eye = (row == place).astype(f32)

    def part(size):
        apart = jnp.bitwise_xor(row, place)
        return jnp.where((apart >= size) & (apart < 2 * size), system, 0.0)

    result = eye - part(1)
    size = 2
    while size < GROUP:
        low = result.astype(bf16)
        inner = dot(part(size).astype(bf16), block_diagonal(low, heads))
        result = result - dot(low, block_diagonal(inner.astype(bf16), heads))
        size *= 2
    return result


def forward_kernel(
    heads, starts_ref, raw_ref, value_ref, filters_ref, decay_ref, gate_ref, gain_ref,
    gated_ref, mixed_ref, inverse_ref, delta_ref, rest_ref, memory_ref, state,
):
    step = pl.program_id(0)

    @pl.when(step == 0)
    def _():
        state[...] = jnp.zeros_like(state)

    blocks = []
    for s in range(SUB):
        base = pl.multiple_of((step * SUB + s) * GROUP, GROUP)
        block = Block(heads, base, raw_ref, value_ref, filters_ref, decay_ref, starts_ref)
        block.values = []
        for h in range(heads):
            pre = block.convolve(2 * heads * KEY + h * VALUE, VALUE)
            block.values.append(pre * sigmoid(pre))
        block.solve = inverse(block.system, heads, block.row, block.place)
        inverse_ref[s * GROUP : (s + 1) * GROUP] = block.solve.astype(bf16)
        blocks.append(block)
    for s, block in enumerate(blocks):
        from_state, rest, right = [], [], []
        for h in range(heads):
            entering = block.entering[:, h : h + 1]
            memory = state[h * KEY : (h + 1) * KEY].astype(bf16)
            memory_ref[(s * heads + h) * KEY : (s * heads + h + 1) * KEY] = memory
            both = jnp.concatenate([block.low_keys[h], block.low_query[h]], axis=0)
            read = dot(both, memory)
            from_state.append(entering * read[GROUP:])
            missing = block.values[h] - entering * read[:GROUP]
            rest.append(missing.astype(bf16))
            right.append(block.strength[:, h : h + 1] * missing)
        rest_ref[s * heads * GROUP : (s + 1) * heads * GROUP] = jnp.concatenate(rest, axis=0)
        solve = tuple(block_diagonal(p, heads) for p in halves(block.solve))
        delta = fine_dot(solve, halves(jnp.concatenate(right, axis=0)))
        delta_ref[s * heads * GROUP : (s + 1) * heads * GROUP] = delta
        scores = tuple(block_diagonal(p, heads) for p in halves(block.scores))
        outputs = fine_dot(scores, halves(delta))
        for h in range(heads):
            rows = slice(h * GROUP, (h + 1) * GROUP)
            out = from_state[h] + outputs[rows]
            here = slice(s * GROUP, (s + 1) * GROUP)
            lanes = slice(h * VALUE, (h + 1) * VALUE)
            low = out.astype(bf16)
            mixed_ref[here, lanes] = low
            low = low.astype(f32)
            gate = gate_ref[here, lanes]
            scale = lax.rsqrt(jnp.mean(low * low, axis=1, keepdims=True) + epsilon)
            gated = low * scale * gain_ref[0:1] * (gate * sigmoid(gate))
            gated_ref[here, lanes] = gated.astype(bf16)
            leaving = halves(block.leaving[:, h : h + 1] * delta[rows])
            keep = block.retain[:, h : h + 1]
            own = slice(h * KEY, (h + 1) * KEY)
            state[own] = keep * state[own] + fine_dot(block.low_keys[h], leaving, 0, 0)


def silu_slope(pre):
    gate = sigmoid(pre)
    return gate * (1.0 + pre * (1.0 - gate))


def backward_kernel(
    heads, starts_ref, raw_ref, value_ref, filters_ref, decay_ref, gate_ref, gain_ref,
    gated_grad_ref, mixed_ref, inverse_ref, delta_ref, rest_ref, memory_ref,
    raw_grad_ref, filters_grad_ref, decay_grad_ref, gain_grad_ref,
    state, halo,
):
    step = pl.program_id(0)
    steps = pl.num_programs(0)
    width = 2 * heads * KEY

    @pl.when(step == 0)
    def _():
        state[...] = jnp.zeros_like(state)
        gain_grad_ref[...] = jnp.zeros_like(gain_grad_ref)
        halo[...] = jnp.zeros_like(halo)
        filters_grad_ref[...] = jnp.zeros_like(filters_grad_ref)
        decay_grad_ref[...] = jnp.zeros_like(decay_grad_ref)

    for s in range(SUB - 1, -1, -1):
        base = pl.multiple_of(((steps - 1 - step) * SUB + s) * GROUP, GROUP)
        block = Block(heads, base, raw_ref, value_ref, filters_ref, decay_ref, starts_ref)
        here = slice(s * GROUP, (s + 1) * GROUP)
        stacked = slice(s * heads * GROUP, (s + 1) * heads * GROUP)
        solve = inverse_ref[here]
        delta = delta_ref[stacked]
        rest = rest_ref[stacked]
        mixed_grads = []
        for h in range(heads):
            lanes = slice(h * VALUE, (h + 1) * VALUE)
            grad = gated_grad_ref[here, lanes].astype(f32)
            mixed = mixed_ref[here, lanes].astype(f32)
            gate = gate_ref[here, lanes]
            scale = lax.rsqrt(jnp.mean(mixed * mixed, axis=1, keepdims=True) + epsilon)
            unit = mixed * scale
            open_gate = sigmoid(gate)
            swish = gate * open_gate
            along = grad * unit
            product = (along * swish).reshape(GROUP // 8, 8, VALUE)
            gain_grad_ref[...] = gain_grad_ref[...] + jnp.sum(product, axis=0)
            gate_grad = along * gain_ref[0:1] * (open_gate * (1.0 + gate * (1.0 - open_gate)))
            behind = width + KEY + (heads + h) * VALUE
            raw_grad_ref[here, behind : behind + VALUE] = gate_grad.astype(bf16)
            unit_grad = grad * swish * gain_ref[0:1]
            inner = jnp.mean(unit_grad * unit, axis=1, keepdims=True)
            mixed_grads.append((scale * (unit_grad - unit * inner)).astype(bf16))
        out_grad = jnp.concatenate(mixed_grads, axis=0)
        later = [state[h * KEY : (h + 1) * KEY] for h in range(heads)]
        later_low = [m.astype(bf16) for m in later]
        pulled = jnp.concatenate(
            [
                block.leaving[:, h : h + 1] * dot(block.low_keys[h], later_low[h])
                for h in range(heads)
            ],
            axis=0,
        )
        scores = tuple(block_diagonal(p, heads) for p in halves(block.scores))
        delta_grad = pulled + fine_dot(scores, out_grad, 0, 0)
        right_grad = dot(block_diagonal(solve, heads), delta_grad.astype(bf16), 0, 0)
        delta = halves(delta)
        rest_grad, strength_grad = [], []
        for h in range(heads):
            rows = slice(h * GROUP, (h + 1) * GROUP)
            rest_grad.append(block.strength[:, h : h + 1] * right_grad[rows])
            strength_grad.append(
                jnp.sum(right_grad[rows] * rest[rows].astype(f32), axis=1, keepdims=True)
            )
        rest_low = [r.astype(bf16) for r in rest_grad]
        entering_query_grad, entering_key_grad, leaving_key_grad, retain_grad = [], [], [], []
        for h in range(heads):
            rows = slice(h * GROUP, (h + 1) * GROUP)
            entering = block.entering[:, h : h + 1]
            memory = memory_ref[(s * heads + h) * KEY : (s * heads + h + 1) * KEY]
            pair = jnp.concatenate([out_grad[rows], rest_low[h]], axis=0)
            back = dot(pair, memory, 1, 1)
            entering_query_grad.append(back[:GROUP])
            entering_key_grad.append(-back[GROUP:])
            leaving_key_grad.append(sum(dot(d[rows], later_low[h], 1, 1) for d in delta))
            product = later[h] * memory.astype(f32)
            retain_grad.append(
                jnp.sum(jnp.sum(product, axis=0, keepdims=True), axis=1, keepdims=True)
            )
            left = jnp.concatenate(
                [entering * block.query[h], -entering * block.keys[h]], axis=0
            ).astype(bf16)
            state[h * KEY : (h + 1) * KEY] = (
                block.retain[:, h : h + 1] * later[h] + dot(left, pair, 0, 0)
            )
        right_low = right_grad.astype(bf16)
        score_part = diagonal_panel(sum(dot(out_grad, d, 1, 1) for d in delta), heads)
        system_part = diagonal_panel(sum(dot(right_low, d, 1, 1) for d in delta), heads)
        scores_grad = jnp.where(block.inclusive, score_part, 0.0)
        system_grad = jnp.where(block.strict, -system_part, 0.0)
        score_gram_grad = scores_grad * block.fade
        faded = system_grad * block.fade
        key_gram_grad = block.strength_down * faded
        gap_grad = score_gram_grad * block.score_gram + key_gram_grad * block.key_gram
        strength_panel = head_sums(faded * block.key_gram, heads, GROUP)
        down = jnp.sum(gap_grad, axis=0, keepdims=True)
        gap_rows = head_sums(
            gap_grad - jnp.where(block.row == block.place, down, 0.0), heads, GROUP
        )
        both_low = jnp.concatenate([key_gram_grad, score_gram_grad], axis=0).astype(bf16)
        straight = dot(both_low, block.key_diag)
        turned = dot(both_low, block.query_key_rows, 0, 0)
        entering_grad, leaving_grad = [], []
        for h in range(heads):
            lanes = slice(h * KEY, (h + 1) * KEY)
            entering = block.entering[:, h : h + 1]
            fading = block.leaving[:, h : h + 1]
            query_grad = entering * entering_query_grad[h] + straight[GROUP:, lanes]
            key_grad = (
                turned[h * GROUP : (h + 1) * GROUP, lanes]
                + straight[:GROUP, lanes]
                + fading * leaving_key_grad[h]
                + entering * entering_key_grad[h]
            )
            entering_grad.append(
                jnp.sum(
                    entering_query_grad[h] * block.query[h] + entering_key_grad[h] * block.keys[h],
                    axis=1,
                    keepdims=True,
                )
            )
            leaving_grad.append(
                jnp.sum(leaving_key_grad[h] * block.keys[h], axis=1, keepdims=True)
            )
            for start, grad, conv, scale, pre, factor in (
                (h * KEY, query_grad, block.query_conv[h], block.query_scale[h],
                 block.query_pre[h], KEY ** (-0.5)),
                ((heads + h) * KEY, key_grad, block.key_conv[h], block.key_scale[h],
                 block.key_pre[h], 1.0),
            ):
                along = jnp.sum(grad * conv, axis=1, keepdims=True)
                conv_grad = (factor * scale) * (grad - conv * (scale * scale * along))
                convolve_back(
                    block, s, start, start, KEY, conv_grad * silu_slope(pre), starts_ref,
                    raw_grad_ref, filters_grad_ref, halo,
                )
            start = 2 * heads * KEY + h * VALUE
            pre = block.convolve(start, VALUE)
            convolve_back(
                block, s, start, start + KEY, VALUE, rest_grad[h] * silu_slope(pre), starts_ref,
                raw_grad_ref, filters_grad_ref, halo,
            )
        entering_grad = columns(entering_grad) * block.entering
        leaving_grad = columns(leaving_grad) * block.leaving
        strength_grad = columns(strength_grad) + strength_panel
        retain_grad = columns(retain_grad) * block.retain
        at_last = jnp.sum(leaving_grad, axis=0, keepdims=True) + retain_grad
        index = iota((GROUP, heads), 0)
        sums_grad = (
            entering_grad - leaving_grad + gap_rows + jnp.where(index == GROUP - 1, at_last, 0.0)
        )
        log_decay_grad = scan_rows(sums_grad, reverse=True)
        logit_grad = log_decay_grad * block.decay_rate * sigmoid(block.decay_logit)
        beta_grad = strength_grad * block.strength * (1.0 - block.strength)
        lane = iota((GROUP, KEY), 1)
        packed = jnp.zeros((GROUP, KEY), f32)
        for h in range(heads):
            packed = jnp.where(lane == h, beta_grad[:, h : h + 1], packed)
            packed = jnp.where(lane == heads + h, logit_grad[:, h : h + 1], packed)
        raw_grad_ref[here, width : width + KEY] = packed.astype(bf16)
        scale_sum = jnp.sum(log_decay_grad * block.log_decay, axis=0, keepdims=True)
        bias_sum = jnp.sum(logit_grad, axis=0, keepdims=True)
        decay_grad_ref[0:1] = decay_grad_ref[0:1] + scale_sum
        decay_grad_ref[1:2] = decay_grad_ref[1:2] + bias_sum


def convolve_back(
    block, s, start, place, width, pre_grad, starts_ref, grad_ref, filters_grad_ref, halo
):
    lanes = slice(start, start + width)
    taps = block.taps(start, width)
    for o in range(CONV):
        j = CONV - 1 - o
        product = (pre_grad * taps[o]).reshape(GROUP // 8, 8, width)
        filters_grad_ref[j * 8 : (j + 1) * 8, lanes] = filters_grad_ref[
            j * 8 : (j + 1) * 8, lanes
        ] + jnp.sum(product, axis=0)
    filters = block.filters_ref[:, lanes]
    extended = jnp.concatenate([pre_grad, halo[:, lanes]], axis=0)
    rows = GROUP + 8
    times = block.base + iota((rows, 1), 0)
    docs = doc_count(starts_ref, times)
    total = pre_grad * filters[CONV - 1 : CONV]
    for o in range(1, CONV):
        mask = (docs == doc_count(starts_ref, times - o)).astype(f32)
        moved = pltpu.roll(extended * mask, rows - o, 0)[:GROUP]
        total = total + moved * filters[CONV - 1 - o : CONV - o]
    grad_ref[s * GROUP : (s + 1) * GROUP, place : place + width] = total.astype(bf16)
    halo[:, lanes] = pre_grad[:8]


SPACE = 56 * 2**20


def mixer_forward(raw, values, filters, decays, starts, gates, gain, heads):
    length, wide = raw.shape
    steps = length // (SUB * GROUP)
    rows = SUB * GROUP
    blocks = length // GROUP
    whole = lambda a: pl.BlockSpec(a.shape, lambda i: (0, 0))
    part = lambda r, c: pl.BlockSpec((r, c), lambda i: (i, 0))
    return pl.pallas_call(
        functools.partial(forward_kernel, heads),
        grid=(steps,),
        in_specs=[
            pl.BlockSpec(memory_space=pltpu.SMEM),
            whole(raw),
            whole(values),
            whole(filters),
            whole(decays),
            part(rows, heads * VALUE),
            whole(gain),
        ],
        out_specs=[
            part(rows, heads * VALUE),
            part(rows, heads * VALUE),
            part(rows, heads * GROUP),
            part(rows * heads, VALUE),
            part(rows * heads, VALUE),
            part(SUB * heads * KEY, VALUE),
        ],
        out_shape=[
            jax.ShapeDtypeStruct((length, heads * VALUE), bf16),
            jax.ShapeDtypeStruct((length, heads * VALUE), bf16),
            jax.ShapeDtypeStruct((length, heads * GROUP), bf16),
            jax.ShapeDtypeStruct((length * heads, VALUE), f32),
            jax.ShapeDtypeStruct((length * heads, VALUE), bf16),
            jax.ShapeDtypeStruct((blocks * heads * KEY, VALUE), bf16),
        ],
        scratch_shapes=[pltpu.VMEM((heads * KEY, VALUE), f32)],
        compiler_params=pltpu.CompilerParams(vmem_limit_bytes=SPACE),
        cost_estimate=pl.CostEstimate(
            flops=length * heads * 11_000_000, bytes_accessed=2**24, transcendentals=0
        ),
        name="mixer_forward",
    )(starts, raw, values, filters, decays, gates, gain)


def mixer_backward(raw, values, filters, decays, starts, gates, gain, gated_grad, kept, heads):
    length, wide = raw.shape
    steps = length // (SUB * GROUP)
    rows = SUB * GROUP
    whole = lambda a: pl.BlockSpec(a.shape, lambda i: (0, 0))
    same = lambda r, c: pl.BlockSpec((r, c), lambda i: (0, 0))
    part = lambda r, c: pl.BlockSpec((r, c), lambda i: (steps - 1 - i, 0))
    return pl.pallas_call(
        functools.partial(backward_kernel, heads),
        grid=(steps,),
        in_specs=[
            pl.BlockSpec(memory_space=pltpu.SMEM),
            whole(raw),
            whole(values),
            whole(filters),
            whole(decays),
            part(rows, heads * VALUE),
            whole(gain),
            part(rows, heads * VALUE),
            part(rows, heads * VALUE),
            part(rows, heads * GROUP),
            part(rows * heads, VALUE),
            part(rows * heads, VALUE),
            part(SUB * heads * KEY, VALUE),
        ],
        out_specs=[
            part(rows, wide + 2 * heads * VALUE),
            same(8 * CONV, filters.shape[1]),
            same(2, heads),
            same(8, VALUE),
        ],
        out_shape=[
            jax.ShapeDtypeStruct((length, wide + 2 * heads * VALUE), bf16),
            jax.ShapeDtypeStruct((8 * CONV, filters.shape[1]), f32),
            jax.ShapeDtypeStruct((2, heads), f32),
            jax.ShapeDtypeStruct((8, VALUE), f32),
        ],
        scratch_shapes=[
            pltpu.VMEM((heads * KEY, VALUE), f32),
            pltpu.VMEM((8, filters.shape[1]), f32),
        ],
        compiler_params=pltpu.CompilerParams(vmem_limit_bytes=SPACE),
        cost_estimate=pl.CostEstimate(
            flops=length * heads * 14_000_000, bytes_accessed=2**24, transcendentals=0
        ),
        name="mixer_backward",
    )(starts, raw, values, filters, decays, gates, gain, gated_grad, *kept)


def forward_dot(left_side, right_side):
    return jnp.dot(left_side, right_side, preferred_element_type=f32)


def times_transposed(left_side, right_side):
    return dot(left_side, right_side, 1, 1)


def transposed_times(left_side, right_side):
    return dot(left_side, right_side, 0, 0)


def rms_norm(values, gain):
    return values * lax.rsqrt(jnp.mean(values * values, axis=-1, keepdims=True) + epsilon) * gain


def swiglu(gate_rows, up_rows):
    return jax.nn.silu(gate_rows) * up_rows


def swap_seq(values):
    return lax.ppermute(values, "seq", [(0, 1), (1, 0)])


def in_order(own, other, axis):
    first = lax.axis_index("seq") == 0
    return jnp.where(
        first,
        jnp.concatenate([own, other], axis=axis),
        jnp.concatenate([other, own], axis=axis),
    )


def gather_seq(values, axis):
    if lax.axis_size("seq") == 2:
        return in_order(values, swap_seq(values), axis)
    return lax.all_gather(values, "seq", axis=axis, tiled=True)


def own_part(values, axis, index=None):
    size = values.shape[axis] // lax.axis_size("seq")
    index = lax.axis_index("seq") if index is None else index
    return lax.dynamic_slice_in_dim(values, index * size, size, axis=axis)


def sum_scatter_seq(values, axis):
    if lax.axis_size("seq") == 2:
        other = own_part(values, axis, 1 - lax.axis_index("seq")).astype(bf16)
        return own_part(values, axis) + swap_seq(other).astype(f32)
    return lax.psum_scatter(
        values.astype(bf16), "seq", scatter_dimension=axis, tiled=True
    ).astype(f32)


def own_first(values):
    if lax.axis_size("seq") == 2:
        return jnp.concatenate([values, swap_seq(values)], axis=0)
    return lax.all_gather(values, "seq", axis=0, tiled=True)


def sum_own_first(values):
    if lax.axis_size("seq") == 2:
        half = values.shape[0] // 2
        return values[:half] + swap_seq(values[half:].astype(bf16)).astype(f32)
    return sum_scatter_seq(values, 0)


def exchange_seq(values, split, join):
    if lax.axis_size("seq") == 2:
        other = own_part(values, split, 1 - lax.axis_index("seq"))
        return in_order(own_part(values, split), swap_seq(other), join)
    return lax.all_to_all(values, "seq", split_axis=split, concat_axis=join, tiled=True)


PLACES = 4


def in_grid():
    return lax.axis_size("shard") == 4 * PLACES and lax.axis_size("seq") == 2


def position():
    place = lax.axis_index("shard")
    return place // 4, (place // 2) % 2, place % 2


def flip(values, mask):
    size = lax.axis_size("shard")
    return lax.ppermute(values, "shard", [(i, i ^ mask) for i in range(size)])


def from_place(values, step):
    size = lax.axis_size("shard")
    return lax.ppermute(values, "shard", [(i, (i - 4 * step) % size) for i in range(size)])


def gather_shard(values):
    return lax.all_gather(values, "shard", axis=0, tiled=True)


def scatter_shard(values):
    return lax.psum_scatter(values, "shard", scatter_dimension=0, tiled=True)


def core_major(values):
    if not in_grid():
        return values
    rows, columns = values.shape
    places = values.reshape(rows, PLACES, 2, 2, columns // (4 * PLACES))
    return jnp.transpose(places, (0, 3, 2, 1, 4)).reshape(rows, columns)


def portion(values, index, count):
    size = values.shape[0] // count
    return lax.dynamic_slice_in_dim(values, index * size, size, axis=0)


def sum_pair(values, index, mask):
    sent = flip(portion(values, 1 - index, 2), mask)
    return (portion(values, index, 2).astype(f32) + sent.astype(f32)).astype(bf16)


def sum_along(values):
    z = position()[0]
    total = portion(values, z, PLACES).astype(f32)
    for r in range(1, PLACES):
        sent = from_place(portion(values, (z - r) % PLACES, PLACES), r)
        total = total + sent.astype(f32)
    return total.astype(bf16)


def first_sum(values):
    return sum_pair(values, position()[2], 1) if in_grid() else values


def second_sum(values):
    return sum_pair(values, position()[1], 2) if in_grid() else values


def third_sum(values):
    return sum_along(values) if in_grid() else scatter_shard(values)


def after(values, *earlier):
    return lax.optimization_barrier((values, earlier))[0]


def sum_small(values, axes):
    if not in_grid():
        return lax.psum(values, axes)
    for mask in (1, 2, 4, 8):
        values = values + flip(values, mask)
    return values


def on_device(
    tokens,
    doc_starts,
    norm_gain,
    query_weight,
    key_weight,
    value_weight,
    gate_weight,
    beta_decay_weight,
    conv_filters,
    decay_params,
    out_norm_gain,
    out_weight,
    ffn_norm_gain,
    ffn_gate_weight,
    ffn_up_weight,
    down_weight,
    out_cotangent,
):
    heads = HEADS // lax.axis_size("seq")
    shards = lax.axis_size("shard")
    rows = query_weight.shape[0]
    width = 2 * heads * KEY
    ff = ffn_gate_weight.shape[1]

    logit_weight = own_part(beta_decay_weight.reshape(rows, HEADS, 2), 1)
    gain_rows = out_norm_gain.shape[0]
    raw_piece = jnp.concatenate(
        [
            own_part(query_weight, 1),
            own_part(key_weight, 1),
            logit_weight[:, :, 0],
            logit_weight[:, :, 1],
            norm_gain[:, None],
            ffn_norm_gain[:, None],
            jnp.pad(out_norm_gain, (0, rows - gain_rows))[:, None],
            jnp.zeros((rows, KEY - 2 * heads - 3), bf16),
        ],
        axis=1,
    )
    units = ff // shards // lax.axis_size("seq")

    def own_units(weight):
        return own_part(weight.reshape(rows, shards, ff // shards), 2).reshape(rows, shards * units)

    raw_wide = raw_piece.shape[1]
    value_end = raw_wide + heads * VALUE
    mixer_full = gather_shard(
        jnp.concatenate([raw_piece, own_part(value_weight, 1), own_part(gate_weight, 1)], axis=1)
    )
    raw_full = mixer_full[:, :raw_wide]
    value_full = mixer_full[:, raw_wide:value_end]
    gate_full = mixer_full[:, value_end:]
    half = shards * units
    model = out_weight.shape[1]
    out_rows = out_weight.shape[0]
    tall_full = gather_shard(jnp.concatenate([out_weight, own_part(down_weight, 0)], axis=0))
    tall_full = tall_full.reshape(shards, out_rows + units, model)
    out_full = tall_full[:, :out_rows].reshape(shards * out_rows, model)
    down_full = tall_full[:, out_rows:].reshape(half, model)
    ffn_full = gather_shard(
        jnp.concatenate([own_units(ffn_gate_weight), own_units(ffn_up_weight)], axis=1)
    )
    first_gain = raw_full[:, width + 2 * heads].astype(f32)
    second_gain = raw_full[:, width + 2 * heads + 1].astype(f32)
    third_gain = (
        raw_full[:, width + 2 * heads + 2]
        .reshape(shards, rows)[:, :gain_rows]
        .reshape(1, shards * gain_rows)
        .astype(f32)
    )

    own_tokens = tokens[0]
    token_count = own_tokens.shape[0]
    inputs = own_tokens.astype(f32)
    cotangent = out_cotangent[0]
    if lax.axis_size("seq") == 2:
        other = swap_seq(jnp.concatenate([own_tokens, cotangent], axis=0))
        all_inputs = in_order(own_tokens, other[:token_count], 0).astype(f32)
        all_cotangent = jnp.concatenate([cotangent, other[token_count:]], axis=0)
    else:
        all_inputs = gather_seq(own_tokens, 0).astype(f32)
        all_cotangent = own_first(cotangent)
    length = all_inputs.shape[0]
    all_scaled = all_inputs * lax.rsqrt(
        jnp.mean(all_inputs * all_inputs, axis=-1, keepdims=True) + epsilon
    )
    normed = (all_scaled * first_gain).astype(bf16)
    raw = forward_dot(normed, raw_full).astype(bf16)
    values = forward_dot(normed, value_full).astype(bf16)
    gate_rows = forward_dot(normed, gate_full)
    filters = jnp.concatenate(
        [
            conv_filters[:, :, :KEY].reshape(CONV, heads * KEY),
            conv_filters[:, :, KEY : 2 * KEY].reshape(CONV, heads * KEY),
            conv_filters[:, :, 2 * KEY :].reshape(CONV, heads * VALUE),
        ],
        axis=1,
    )
    decays = decay_params.T
    gated, *kept = mixer_forward(
        raw, values, filters, decays, doc_starts, gate_rows, third_gain, heads
    )
    gated_low = exchange_seq(gated, 0, 1)
    gated_low, down_full = lax.optimization_barrier((gated_low, down_full))
    middle = inputs + forward_dot(gated_low, out_full)
    second_norm, second_pull = jax.vjp(rms_norm, middle, second_gain)
    hidden = own_first(second_norm.astype(bf16))
    both_ffn = forward_dot(hidden, ffn_full)
    activated, swiglu_pull = jax.vjp(swiglu, both_ffn[:, :half], both_ffn[:, half:])
    activated_low = activated.astype(bf16)
    act_grad = times_transposed(all_cotangent, down_full)
    both_grad = jnp.concatenate([g.astype(bf16) for g in swiglu_pull(act_grad)], axis=1)
    hidden_grad = sum_own_first(times_transposed(both_grad, ffn_full))
    out_parts = forward_dot(activated_low, down_full)
    down_grad = transposed_times(activated_low, all_cotangent).astype(bf16)
    ffn_grad = transposed_times(core_major(hidden), both_grad).astype(bf16)
    hidden_grad, ffn_grad = lax.optimization_barrier((hidden_grad, ffn_grad))
    ffn_grad = first_sum(ffn_grad)
    middle_part, ffn_gain_grad = second_pull(hidden_grad)
    middle_grad = cotangent.astype(f32) + middle_part
    branch_low = middle_grad.astype(bf16)
    out_grad = transposed_times(gated_low, branch_low).astype(bf16)
    gated_grad = exchange_seq(times_transposed(branch_low, out_full).astype(bf16), 1, 0)
    ffn_grad = second_sum(ffn_grad)
    tall_grad = jnp.concatenate(
        [out_grad.reshape(shards, out_rows, model), down_grad.reshape(shards, units, model)], axis=1
    ).reshape(shards * (out_rows + units), model)
    gated_grad, ffn_grad, tall_grad = lax.optimization_barrier((gated_grad, ffn_grad, tall_grad))
    ffn_share = third_sum(ffn_grad)
    tall_share = scatter_shard(tall_grad)
    block_out = (middle + sum_own_first(after(out_parts, gated_grad))).astype(bf16)
    mixer_grad, filters_grad, decays_grad, out_gain_grad = mixer_backward(
        raw,
        values,
        filters,
        decays,
        doc_starts,
        gate_rows,
        third_gain,
        gated_grad,
        kept,
        heads,
    )
    mixer_grad, ffn_share, block_out = lax.optimization_barrier((mixer_grad, ffn_share, block_out))
    mixer_weight_grad = transposed_times(normed, mixer_grad).astype(bf16)
    mixer_grad, mixer_weight_grad = lax.optimization_barrier((mixer_grad, mixer_weight_grad))
    mixer_share = scatter_shard(mixer_weight_grad)
    normed_grad = times_transposed(mixer_grad, mixer_full)
    norm_gain_grad = jnp.sum(normed_grad * all_scaled, axis=0)
    own_normed_grad = sum_scatter_seq(normed_grad, 0)
    _, first_pull = jax.vjp(lambda v: rms_norm(v, first_gain), inputs)
    tokens_grad = middle_grad + first_pull(own_normed_grad)[0]

    def all_units(share):
        share = gather_seq(share.reshape(rows, shards, units), 2)
        return share.reshape(rows, ff).astype(f32)

    ffn_gate_share = all_units(ffn_share[:, :half])
    ffn_up_share = all_units(ffn_share[:, half:])
    tall_share = gather_seq(after(tall_share, mixer_grad)[None], 0).astype(f32)
    out_share = jnp.sum(tall_share[:, :out_rows], axis=0)
    down_share = tall_share[:, out_rows:].reshape(-1, model)
    every = gather_seq(mixer_share[None], 0)
    pieces = every.shape[0]

    def side_by_side(start, stop):
        part = jnp.swapaxes(every[:, :, start:stop], 0, 1)
        return part.reshape(rows, pieces * (stop - start)).astype(f32)

    query_share = side_by_side(0, heads * KEY)
    key_share = side_by_side(heads * KEY, width)
    value_share = side_by_side(raw_wide, value_end)
    gate_share = side_by_side(value_end, mixer_share.shape[1])
    logit_share = every[:, :, width : width + 2 * heads].reshape(pieces, rows, 2, heads)
    logit_share = jnp.transpose(logit_share, (1, 0, 3, 2)).reshape(rows, 2 * HEADS).astype(f32)

    all_width = filters.shape[1]
    filters_grad = jnp.sum(filters_grad.reshape(CONV, 8, all_width), axis=1)
    lengths = [shards * n for n in (norm_gain.shape[0], gain_rows, ffn_norm_gain.shape[0])]
    small = jnp.concatenate(
        [
            filters_grad.reshape(CONV * all_width),
            decays_grad.reshape(2 * heads),
            norm_gain_grad,
            jnp.sum(out_gain_grad, axis=0),
            ffn_gain_grad,
        ]
    )
    small = sum_small(small, ("shard",))
    head_end = CONV * all_width + 2 * heads
    filters_grad = small[: CONV * all_width].reshape(CONV, all_width)
    decays_grad = small[CONV * all_width : head_end].reshape(2, heads)
    gains = small[head_end:]
    gains = gains + swap_seq(gains) if in_grid() else lax.psum(gains, "seq")
    split = (heads * KEY, 2 * heads * KEY)
    filters_out = jnp.concatenate(
        [
            filters_grad[:, : split[0]].reshape(CONV, heads, KEY),
            filters_grad[:, split[0] : split[1]].reshape(CONV, heads, KEY),
            filters_grad[:, split[1] :].reshape(CONV, heads, VALUE),
        ],
        axis=2,
    )
    gains = [
        gains[: lengths[0]],
        gains[lengths[0] : lengths[0] + lengths[1]],
        gains[lengths[0] + lengths[1] :],
    ]
    place = lax.axis_index("shard")
    gains = [
        lax.dynamic_slice_in_dim(g, place * (g.shape[0] // shards), g.shape[0] // shards)
        for g in gains
    ]
    return (
        block_out[None],
        tokens_grad[None],
        gains[0],
        query_share,
        key_share,
        value_share,
        gate_share,
        logit_share,
        filters_out,
        decays_grad.T,
        gains[1],
        out_share,
        gains[2],
        ffn_gate_share,
        ffn_up_share,
        down_share,
    )


def solution(mesh):
    in_specs = (
        P("shard", "seq", None),
        P("shard", None),
        P("shard"),
        P("shard", None),
        P("shard", None),
        P("shard", None),
        P("shard", None),
        P("shard", None),
        P(None, "seq", None),
        P("seq", None),
        P("shard"),
        P("shard", None),
        P("shard"),
        P("shard", None),
        P("shard", None),
        P("shard", None),
        P("shard", "seq", None),
    )
    out_specs = (
        P("shard", "seq", None),
        P("shard", "seq", None),
        P("shard"),
        P("shard", None),
        P("shard", None),
        P("shard", None),
        P("shard", None),
        P("shard", None),
        P(None, "seq", None),
        P("seq", None),
        P("shard"),
        P("shard", None),
        P("shard"),
        P("shard", None),
        P("shard", None),
        P("shard", None),
    )
    return jax.shard_map(
        on_device, mesh=mesh, in_specs=in_specs, out_specs=out_specs, check_vma=False
    )
```

```python
import functools

import jax
import jax.numpy as jnp
from jax import lax
from jax.experimental import pallas as pl
from jax.experimental.pallas import tpu as pltpu
from jax.sharding import PartitionSpec as P

HEADS = 8
KEY = 128
VALUE = 256
CONV = 4
GROUP = 64
HALO = 16
SUB = 4
epsilon = 1e-06
f32 = jnp.float32
bf16 = jnp.bfloat16


def dot(a, b, ca=1, cb=0):
    return lax.dot_general(a, b, (((ca,), (cb,)), ((), ())), preferred_element_type=f32)


def halves(values):
    high = values.astype(bf16)
    return high, (values - high.astype(f32)).astype(bf16)


def fine_dot(a, b, ca=1, cb=0):
    if not isinstance(a, tuple):
        return dot(a, b[0], ca, cb) + dot(a, b[1], ca, cb)
    if not isinstance(b, tuple):
        return dot(a[0], b, ca, cb) + dot(a[1], b, ca, cb)
    return dot(a[0], b[0], ca, cb) + (dot(a[0], b[1], ca, cb) + dot(a[1], b[0], ca, cb))


def iota(shape, dim):
    return lax.broadcasted_iota(jnp.int32, shape, dim)


def doc_count(starts_ref, times):
    count = jnp.zeros(times.shape, jnp.int32)
    for s in range(starts_ref.shape[1]):
        count = count + jnp.where(times >= starts_ref[0, s], 1, 0)
    return count


def scalar_doc(starts_ref, time):
    count = 0
    for s in range(starts_ref.shape[1]):
        count = count + (time >= starts_ref[0, s]).astype(jnp.int32)
    return count


def per_head(cols, heads, width):
    rows = cols.shape[0]
    lane = iota((rows, heads * width), 1)
    out = jnp.broadcast_to(cols[:, heads - 1 : heads], (rows, heads * width))
    for h in range(heads - 2, -1, -1):
        out = jnp.where(lane < (h + 1) * width, cols[:, h : h + 1], out)
    return out


def head_sums(panel, heads, width):
    lane = iota(panel.shape, 1)
    sums = []
    for h in range(heads):
        inside = (lane >= h * width) & (lane < (h + 1) * width)
        sums.append(jnp.sum(jnp.where(inside, panel, 0.0), axis=1, keepdims=True))
    return columns(sums)


def across(mask, width):
    return jnp.concatenate([mask] * (width // KEY), axis=1)


def columns(parts):
    rows = parts[0].shape[0]
    lane = iota((rows, len(parts)), 1)
    out = jnp.broadcast_to(parts[-1], (rows, len(parts)))
    for h in range(len(parts) - 2, -1, -1):
        out = jnp.where(lane == h, parts[h], out)
    return out


def block_diagonal(panel, heads):
    if heads == 1:
        return panel
    lane = iota(panel.shape, 1)
    zero = jnp.zeros_like(panel)
    parts = []
    for h in range(heads):
        inside = (lane >= h * GROUP) & (lane < (h + 1) * GROUP)
        parts.append(jnp.where(inside, panel, zero))
    return jnp.concatenate(parts, axis=0)


def diagonal_panel(full, heads):
    if heads == 1:
        return full
    lane = iota((GROUP, heads * GROUP), 1)
    out = full[(heads - 1) * GROUP :]
    for h in range(heads - 2, -1, -1):
        out = jnp.where(lane < (h + 1) * GROUP, full[h * GROUP : (h + 1) * GROUP], out)
    return out


def key_diagonal(keys):
    heads = len(keys)
    if heads == 1:
        return keys[0]
    zero = jnp.zeros_like(keys[0])
    rows = []
    for h in range(heads):
        rows.append(jnp.concatenate([keys[h] if o == h else zero for o in range(heads)], axis=1))
    return jnp.concatenate(rows, axis=0)


def scan_rows(values, reverse=False):
    rows = values.shape[0]
    index = iota(values.shape, 0)
    step = 1
    while step < rows:
        if reverse:
            moved = pltpu.roll(values, rows - step, 0)
            values = values + jnp.where(index < rows - step, moved, 0.0)
        else:
            moved = pltpu.roll(values, step, 0)
            values = values + jnp.where(index >= step, moved, 0.0)
        step *= 2
    return values


def sigmoid(v):
    return 1.0 / (1.0 + jnp.exp(-v))


def softplus(v):
    return jnp.maximum(v, 0.0) + jnp.log(1.0 + jnp.exp(-jnp.abs(v)))


def in_turn(generators):
    generators = list(generators)
    while generators:
        still = []
        for generator in generators:
            if next(generator, True) is None:
                still.append(generator)
        generators = still


class Block:
    def __init__(self, heads, base, raw_ref, value_ref, filters_ref, decay_ref, starts_ref):
        self.heads = heads
        self.base = base
        self.raw_ref = raw_ref
        self.value_ref = value_ref
        self.filters_ref = filters_ref
        self.decay_ref = decay_ref
        self.starts_ref = starts_ref

    def build(self):
        heads, base, starts_ref = self.heads, self.base, self.starts_ref
        raw_ref, decay_ref = self.raw_ref, self.decay_ref
        width = 2 * heads * KEY
        times = base + iota((GROUP, 1), 0)
        docs = doc_count(starts_ref, times)
        wide = (GROUP, KEY)
        self.masks, self.next_masks = [], []
        for o in range(1, CONV):
            same = (docs == doc_count(starts_ref, times - o)).astype(f32)
            self.masks.append(jnp.broadcast_to(same, wide))
            same = (docs == doc_count(starts_ref, times + o)).astype(f32)
            self.next_masks.append(jnp.broadcast_to(same, wide))
        self.query, self.keys, self.query_pre, self.key_pre = [], [], [], []
        self.query_conv, self.key_conv, self.query_scale, self.key_scale = [], [], [], []
        for h in range(heads):
            pre = self.convolve(h * KEY, KEY)
            conv = pre * sigmoid(pre)
            scale = lax.rsqrt(jnp.sum(conv * conv, axis=1, keepdims=True) + epsilon)
            self.query_pre.append(pre)
            self.query_conv.append(conv)
            self.query_scale.append(scale)
            self.query.append(conv * scale * KEY ** (-0.5))
        for h in range(heads):
            pre = self.convolve((heads + h) * KEY, KEY)
            conv = pre * sigmoid(pre)
            scale = lax.rsqrt(jnp.sum(conv * conv, axis=1, keepdims=True) + epsilon)
            self.key_pre.append(pre)
            self.key_conv.append(conv)
            self.key_scale.append(scale)
            self.keys.append(conv * scale)
        yield
        logits = raw_ref[pl.ds(base, GROUP), width : width + KEY].astype(f32)
        self.strength = sigmoid(logits[:, :heads])
        self.decay_logit = logits[:, heads : 2 * heads] + decay_ref[1:2, :heads]
        self.decay_rate = -jnp.exp(decay_ref[0:1, :heads])
        self.log_decay = self.decay_rate * softplus(self.decay_logit)
        yield
        sums = scan_rows(self.log_decay)
        yield
        self.sums = sums
        last = sums[GROUP - 1 : GROUP]
        before = scalar_doc(starts_ref, base - 1)
        final = scalar_doc(starts_ref, base + GROUP - 1)
        self.entering = jnp.where(docs == before, jnp.exp(sums), 0.0)
        same_last = docs == final
        self.leaving = jnp.where(same_last, jnp.exp(jnp.where(same_last, last - sums, 0.0)), 0.0)
        self.retain = self.entering[GROUP - 1 : GROUP]
        yield
        shape = (GROUP, heads * GROUP)
        row = iota(shape, 0)
        place = jnp.bitwise_and(iota(shape, 1), GROUP - 1)
        self.row, self.place = row, place
        across = jnp.bitwise_and(iota((1, heads * GROUP), 1), GROUP - 1)
        docs_across = doc_count(starts_ref, base + across)
        same = docs == docs_across
        self.inclusive = same & (row >= place)
        self.strict = same & (row > place)
        sums_down = per_head(sums, heads, GROUP)
        sums_across = jnp.sum(jnp.where(row == place, sums_down, 0.0), axis=0, keepdims=True)
        gap = jnp.where(self.inclusive, sums_down - sums_across, 0.0)
        self.fade = jnp.where(self.inclusive, jnp.exp(gap), 0.0)
        yield
        self.strength_down = per_head(self.strength, heads, GROUP)
        low_keys = [k.astype(bf16) for k in self.keys]
        low_query = [q.astype(bf16) for q in self.query]
        self.keys = [k.astype(f32) for k in low_keys]
        self.query = [q.astype(f32) for q in low_query]
        self.low_keys, self.low_query = low_keys, low_query
        self.key_diag = key_diagonal(low_keys)
        left = jnp.concatenate(
            [jnp.concatenate(low_keys, axis=1), jnp.concatenate(low_query, axis=1)], axis=0
        )
        self.query_key_rows = left
        grams = dot(left, self.key_diag, 1, 1)
        yield
        self.key_gram = grams[:GROUP]
        self.score_gram = grams[GROUP:]
        self.system = jnp.where(self.strict, self.strength_down * self.key_gram * self.fade, 0.0)
        self.scores = self.score_gram * self.fade

    def taps(self, start, width):
        source = self.raw_ref
        if start >= 2 * self.heads * KEY:
            source = self.value_ref
            start = start - 2 * self.heads * KEY
        current = source[pl.ds(self.base, GROUP), start : start + width].astype(f32)
        earlier = pl.multiple_of(jnp.maximum(self.base - HALO, 0), HALO)
        halo = source[pl.ds(earlier, HALO), start : start + width].astype(f32)
        extended = jnp.concatenate([halo, current], axis=0)
        return [current] + [
            pltpu.roll(extended, o, 0)[HALO:] * across(self.masks[o - 1], width)
            for o in range(1, CONV)
        ]

    def convolve(self, start, width):
        taps = self.taps(start, width)
        filters = self.filters_ref[:, start : start + width]
        total = taps[0] * filters[CONV - 1 : CONV]
        for o in range(1, CONV):
            total = total + taps[o] * filters[CONV - 1 - o : CONV - o]
        return total


def inverse(systems, heads, row, place):
    eye = (row == place).astype(f32)
    apart = jnp.bitwise_xor(row, place)

    def part(system, size):
        return jnp.where((apart >= size) & (apart < 2 * size), system, 0.0)

    results = [eye - part(system, 1) for system in systems]
    size = 2
    while size < GROUP:
        low = [result.astype(bf16) for result in results]
        inner = [
            dot(part(system, size).astype(bf16), block_diagonal(one, heads))
            for system, one in zip(systems, low)
        ]
        inner = [block_diagonal(one.astype(bf16), heads) for one in inner]
        results = [
            result - dot(one, right) for result, one, right in zip(results, low, inner)
        ]
        size *= 2
    return results


def forward_kernel(
    heads, starts_ref, raw_ref, value_ref, filters_ref, decay_ref, gate_ref, gain_ref,
    gated_ref, mixed_ref, inverse_ref, delta_ref, rest_ref, memory_ref, state,
):
    step = pl.program_id(0)

    @pl.when(step == 0)
    def _():
        state[...] = jnp.zeros_like(state)

    blocks = []
    for s in range(SUB):
        base = pl.multiple_of((step * SUB + s) * GROUP, GROUP)
        blocks.append(Block(heads, base, raw_ref, value_ref, filters_ref, decay_ref, starts_ref))
    in_turn(block.build() for block in blocks)
    solves = inverse([block.system for block in blocks], heads, blocks[0].row, blocks[0].place)
    for s, block in enumerate(blocks):
        block.values = []
        for h in range(heads):
            pre = block.convolve(2 * heads * KEY + h * VALUE, VALUE)
            block.values.append(pre * sigmoid(pre))
        block.solve = solves[s]
        inverse_ref[s * GROUP : (s + 1) * GROUP] = block.solve.astype(bf16)
    for s, block in enumerate(blocks):
        from_state, rest, right = [], [], []
        for h in range(heads):
            entering = block.entering[:, h : h + 1]
            memory = state[h * KEY : (h + 1) * KEY].astype(bf16)
            memory_ref[(s * heads + h) * KEY : (s * heads + h + 1) * KEY] = memory
            both = jnp.concatenate([block.low_keys[h], block.low_query[h]], axis=0)
            read = dot(both, memory)
            from_state.append(entering * read[GROUP:])
            missing = block.values[h] - entering * read[:GROUP]
            rest.append(missing.astype(bf16))
            right.append(block.strength[:, h : h + 1] * missing)
        rest_ref[s * heads * GROUP : (s + 1) * heads * GROUP] = jnp.concatenate(rest, axis=0)
        solve = tuple(block_diagonal(p, heads) for p in halves(block.solve))
        delta = fine_dot(solve, halves(jnp.concatenate(right, axis=0)))
        delta_ref[s * heads * GROUP : (s + 1) * heads * GROUP] = delta
        scores = tuple(block_diagonal(p, heads) for p in halves(block.scores))
        outputs = fine_dot(scores, halves(delta))
        for h in range(heads):
            rows = slice(h * GROUP, (h + 1) * GROUP)
            out = from_state[h] + outputs[rows]
            here = slice(s * GROUP, (s + 1) * GROUP)
            lanes = slice(h * VALUE, (h + 1) * VALUE)
            low = out.astype(bf16)
            mixed_ref[here, lanes] = low
            low = low.astype(f32)
            gate = gate_ref[here, lanes]
            scale = lax.rsqrt(jnp.mean(low * low, axis=1, keepdims=True) + epsilon)
            gated = low * scale * gain_ref[0:1] * (gate * sigmoid(gate))
            gated_ref[here, lanes] = gated.astype(bf16)
            leaving = halves(block.leaving[:, h : h + 1] * delta[rows])
            keep = block.retain[:, h : h + 1]
            own = slice(h * KEY, (h + 1) * KEY)
            state[own] = keep * state[own] + fine_dot(block.low_keys[h], leaving, 0, 0)


def silu_slope(pre):
    gate = sigmoid(pre)
    return gate * (1.0 + pre * (1.0 - gate))


def backward_kernel(
    heads, starts_ref, raw_ref, value_ref, filters_ref, decay_ref, gate_ref, gain_ref,
    gated_grad_ref, mixed_ref, inverse_ref, delta_ref, rest_ref, memory_ref,
    raw_grad_ref, filters_grad_ref, decay_grad_ref, gain_grad_ref,
    state, halo,
):
    step = pl.program_id(0)
    steps = pl.num_programs(0)
    width = 2 * heads * KEY

    @pl.when(step == 0)
    def _():
        state[...] = jnp.zeros_like(state)
        gain_grad_ref[...] = jnp.zeros_like(gain_grad_ref)
        halo[...] = jnp.zeros_like(halo)
        filters_grad_ref[...] = jnp.zeros_like(filters_grad_ref)
        decay_grad_ref[...] = jnp.zeros_like(decay_grad_ref)

    def pull(s):
        base = pl.multiple_of(((steps - 1 - step) * SUB + s) * GROUP, GROUP)
        block = Block(heads, base, raw_ref, value_ref, filters_ref, decay_ref, starts_ref)
        yield from block.build()
        yield
        here = slice(s * GROUP, (s + 1) * GROUP)
        stacked = slice(s * heads * GROUP, (s + 1) * heads * GROUP)
        solve = inverse_ref[here]
        delta = delta_ref[stacked]
        rest = rest_ref[stacked]
        mixed_grads = []
        for h in range(heads):
            lanes = slice(h * VALUE, (h + 1) * VALUE)
            grad = gated_grad_ref[here, lanes].astype(f32)
            mixed = mixed_ref[here, lanes].astype(f32)
            gate = gate_ref[here, lanes]
            scale = lax.rsqrt(jnp.mean(mixed * mixed, axis=1, keepdims=True) + epsilon)
            unit = mixed * scale
            open_gate = sigmoid(gate)
            swish = gate * open_gate
            along = grad * unit
            product = (along * swish).reshape(GROUP // 8, 8, VALUE)
            gain_grad_ref[...] = gain_grad_ref[...] + jnp.sum(product, axis=0)
            gate_grad = along * gain_ref[0:1] * (open_gate * (1.0 + gate * (1.0 - open_gate)))
            behind = width + KEY + (heads + h) * VALUE
            raw_grad_ref[here, behind : behind + VALUE] = gate_grad.astype(bf16)
            unit_grad = grad * swish * gain_ref[0:1]
            inner = jnp.mean(unit_grad * unit, axis=1, keepdims=True)
            mixed_grads.append((scale * (unit_grad - unit * inner)).astype(bf16))
        out_grad = jnp.concatenate(mixed_grads, axis=0)
        yield
        scores = tuple(block_diagonal(p, heads) for p in halves(block.scores))
        from_scores = fine_dot(scores, out_grad, 0, 0)
        delta = halves(delta)
        score_part = diagonal_panel(sum(dot(out_grad, d, 1, 1) for d in delta), heads)
        scores_grad = jnp.where(block.inclusive, score_part, 0.0)
        score_gram_grad = scores_grad * block.fade
        solve = block_diagonal(solve, heads)
        yield "chain"
        later = [state[h * KEY : (h + 1) * KEY] for h in range(heads)]
        later_low = [m.astype(bf16) for m in later]
        pulled = jnp.concatenate(
            [
                block.leaving[:, h : h + 1] * dot(block.low_keys[h], later_low[h])
                for h in range(heads)
            ],
            axis=0,
        )
        delta_grad = pulled + from_scores
        right_grad = dot(solve, delta_grad.astype(bf16), 0, 0)
        rest_grad, pairs = [], []
        for h in range(heads):
            rows = slice(h * GROUP, (h + 1) * GROUP)
            rest_grad.append(block.strength[:, h : h + 1] * right_grad[rows])
            pairs.append(jnp.concatenate([out_grad[rows], rest_grad[h].astype(bf16)], axis=0))
            entering = block.entering[:, h : h + 1]
            left = jnp.concatenate(
                [entering * block.query[h], -entering * block.keys[h]], axis=0
            ).astype(bf16)
            state[h * KEY : (h + 1) * KEY] = (
                block.retain[:, h : h + 1] * later[h] + dot(left, pairs[h], 0, 0)
            )
        yield "chain"
        entering_query_grad, entering_key_grad, leaving_key_grad, retain_grad = [], [], [], []
        strength_grad = []
        for h in range(heads):
            rows = slice(h * GROUP, (h + 1) * GROUP)
            strength_grad.append(
                jnp.sum(right_grad[rows] * rest[rows].astype(f32), axis=1, keepdims=True)
            )
            memory = memory_ref[(s * heads + h) * KEY : (s * heads + h + 1) * KEY]
            back = dot(pairs[h], memory, 1, 1)
            entering_query_grad.append(back[:GROUP])
            entering_key_grad.append(-back[GROUP:])
            leaving_key_grad.append(sum(dot(d[rows], later_low[h], 1, 1) for d in delta))
            product = later[h] * memory.astype(f32)
            retain_grad.append(
                jnp.sum(jnp.sum(product, axis=0, keepdims=True), axis=1, keepdims=True)
            )
        yield
        right_low = right_grad.astype(bf16)
        system_part = diagonal_panel(sum(dot(right_low, d, 1, 1) for d in delta), heads)
        system_grad = jnp.where(block.strict, -system_part, 0.0)
        faded = system_grad * block.fade
        key_gram_grad = block.strength_down * faded
        gap_grad = score_gram_grad * block.score_gram + key_gram_grad * block.key_gram
        yield
        strength_panel = head_sums(faded * block.key_gram, heads, GROUP)
        down = jnp.sum(gap_grad, axis=0, keepdims=True)
        gap_rows = head_sums(
            gap_grad - jnp.where(block.row == block.place, down, 0.0), heads, GROUP
        )
        yield
        both_low = jnp.concatenate([key_gram_grad, score_gram_grad], axis=0).astype(bf16)
        straight = dot(both_low, block.key_diag)
        turned = dot(both_low, block.query_key_rows, 0, 0)
        yield
        entering_grad, leaving_grad = [], []
        for h in range(heads):
            lanes = slice(h * KEY, (h + 1) * KEY)
            entering = block.entering[:, h : h + 1]
            fading = block.leaving[:, h : h + 1]
            query_grad = entering * entering_query_grad[h] + straight[GROUP:, lanes]
            key_grad = (
                turned[h * GROUP : (h + 1) * GROUP, lanes]
                + straight[:GROUP, lanes]
                + fading * leaving_key_grad[h]
                + entering * entering_key_grad[h]
            )
            entering_grad.append(
                jnp.sum(
                    entering_query_grad[h] * block.query[h] + entering_key_grad[h] * block.keys[h],
                    axis=1,
                    keepdims=True,
                )
            )
            leaving_grad.append(
                jnp.sum(leaving_key_grad[h] * block.keys[h], axis=1, keepdims=True)
            )
            for start, grad, conv, scale, pre, factor in (
                (h * KEY, query_grad, block.query_conv[h], block.query_scale[h],
                 block.query_pre[h], KEY ** (-0.5)),
                ((heads + h) * KEY, key_grad, block.key_conv[h], block.key_scale[h],
                 block.key_pre[h], 1.0),
            ):
                along = jnp.sum(grad * conv, axis=1, keepdims=True)
                conv_grad = (factor * scale) * (grad - conv * (scale * scale * along))
                convolve_back(
                    block, s, start, start, KEY, conv_grad * silu_slope(pre), starts_ref,
                    raw_grad_ref, filters_grad_ref, halo,
                )
            yield
            start = 2 * heads * KEY + h * VALUE
            pre = block.convolve(start, VALUE)
            convolve_back(
                block, s, start, start + KEY, VALUE, rest_grad[h] * silu_slope(pre), starts_ref,
                raw_grad_ref, filters_grad_ref, halo,
            )
        yield
        entering_grad = columns(entering_grad) * block.entering
        leaving_grad = columns(leaving_grad) * block.leaving
        strength_grad = columns(strength_grad) + strength_panel
        retain_grad = columns(retain_grad) * block.retain
        at_last = jnp.sum(leaving_grad, axis=0, keepdims=True) + retain_grad
        index = iota((GROUP, heads), 0)
        sums_grad = (
            entering_grad - leaving_grad + gap_rows + jnp.where(index == GROUP - 1, at_last, 0.0)
        )
        log_decay_grad = scan_rows(sums_grad, reverse=True)
        yield
        logit_grad = log_decay_grad * block.decay_rate * sigmoid(block.decay_logit)
        beta_grad = strength_grad * block.strength * (1.0 - block.strength)
        lane = iota((GROUP, KEY), 1)
        packed = jnp.zeros((GROUP, KEY), f32)
        for h in range(heads):
            packed = jnp.where(lane == h, beta_grad[:, h : h + 1], packed)
            packed = jnp.where(lane == heads + h, logit_grad[:, h : h + 1], packed)
        raw_grad_ref[here, width : width + KEY] = packed.astype(bf16)
        scale_sum = jnp.sum(log_decay_grad * block.log_decay, axis=0, keepdims=True)
        bias_sum = jnp.sum(logit_grad, axis=0, keepdims=True)
        decay_grad_ref[0:1] = decay_grad_ref[0:1] + scale_sum
        decay_grad_ref[1:2] = decay_grad_ref[1:2] + bias_sum

    pulls = [pull(s) for s in range(SUB - 1, -1, -1)]
    waiting = list(pulls)
    while waiting:
        waiting = [p for p in waiting if next(p) is None]
    for p in pulls:
        next(p)
    in_turn(pulls)


def convolve_back(
    block, s, start, place, width, pre_grad, starts_ref, grad_ref, filters_grad_ref, halo
):
    lanes = slice(start, start + width)
    taps = block.taps(start, width)
    for o in range(CONV):
        j = CONV - 1 - o
        product = (pre_grad * taps[o]).reshape(GROUP // 8, 8, width)
        filters_grad_ref[j * 8 : (j + 1) * 8, lanes] = filters_grad_ref[
            j * 8 : (j + 1) * 8, lanes
        ] + jnp.sum(product, axis=0)
    filters = block.filters_ref[:, lanes]
    extended = jnp.concatenate([pre_grad, halo[:, lanes]], axis=0)
    rows = GROUP + 8
    total = pre_grad * filters[CONV - 1 : CONV]
    for o in range(1, CONV):
        moved = pltpu.roll(extended, rows - o, 0)[:GROUP] * across(block.next_masks[o - 1], width)
        total = total + moved * filters[CONV - 1 - o : CONV - o]
    grad_ref[s * GROUP : (s + 1) * GROUP, place : place + width] = total.astype(bf16)
    halo[:, lanes] = pre_grad[:8]


SPACE = 56 * 2**20


def mixer_forward(raw, values, filters, decays, starts, gates, gain, heads):
    length, wide = raw.shape
    steps = length // (SUB * GROUP)
    rows = SUB * GROUP
    blocks = length // GROUP
    whole = lambda a: pl.BlockSpec(a.shape, lambda i: (0, 0))
    part = lambda r, c: pl.BlockSpec((r, c), lambda i: (i, 0))
    return pl.pallas_call(
        functools.partial(forward_kernel, heads),
        grid=(steps,),
        in_specs=[
            pl.BlockSpec(memory_space=pltpu.SMEM),
            whole(raw),
            whole(values),
            whole(filters),
            whole(decays),
            part(rows, heads * VALUE),
            whole(gain),
        ],
        out_specs=[
            part(rows, heads * VALUE),
            part(rows, heads * VALUE),
            part(rows, heads * GROUP),
            part(rows * heads, VALUE),
            part(rows * heads, VALUE),
            part(SUB * heads * KEY, VALUE),
        ],
        out_shape=[
            jax.ShapeDtypeStruct((length, heads * VALUE), bf16),
            jax.ShapeDtypeStruct((length, heads * VALUE), bf16),
            jax.ShapeDtypeStruct((length, heads * GROUP), bf16),
            jax.ShapeDtypeStruct((length * heads, VALUE), f32),
            jax.ShapeDtypeStruct((length * heads, VALUE), bf16),
            jax.ShapeDtypeStruct((blocks * heads * KEY, VALUE), bf16),
        ],
        scratch_shapes=[pltpu.VMEM((heads * KEY, VALUE), f32)],
        compiler_params=pltpu.CompilerParams(vmem_limit_bytes=SPACE),
        cost_estimate=pl.CostEstimate(
            flops=length * heads * 11_000_000, bytes_accessed=2**24, transcendentals=0
        ),
        name="mixer_forward",
    )(starts, raw, values, filters, decays, gates, gain)


def mixer_backward(raw, values, filters, decays, starts, gates, gain, gated_grad, kept, heads):
    length, wide = raw.shape
    steps = length // (SUB * GROUP)
    rows = SUB * GROUP
    whole = lambda a: pl.BlockSpec(a.shape, lambda i: (0, 0))
    same = lambda r, c: pl.BlockSpec((r, c), lambda i: (0, 0))
    part = lambda r, c: pl.BlockSpec((r, c), lambda i: (steps - 1 - i, 0))
    return pl.pallas_call(
        functools.partial(backward_kernel, heads),
        grid=(steps,),
        in_specs=[
            pl.BlockSpec(memory_space=pltpu.SMEM),
            whole(raw),
            whole(values),
            whole(filters),
            whole(decays),
            part(rows, heads * VALUE),
            whole(gain),
            part(rows, heads * VALUE),
            part(rows, heads * VALUE),
            part(rows, heads * GROUP),
            part(rows * heads, VALUE),
            part(rows * heads, VALUE),
            part(SUB * heads * KEY, VALUE),
        ],
        out_specs=[
            part(rows, wide + 2 * heads * VALUE),
            same(8 * CONV, filters.shape[1]),
            same(2, heads),
            same(8, VALUE),
        ],
        out_shape=[
            jax.ShapeDtypeStruct((length, wide + 2 * heads * VALUE), bf16),
            jax.ShapeDtypeStruct((8 * CONV, filters.shape[1]), f32),
            jax.ShapeDtypeStruct((2, heads), f32),
            jax.ShapeDtypeStruct((8, VALUE), f32),
        ],
        scratch_shapes=[
            pltpu.VMEM((heads * KEY, VALUE), f32),
            pltpu.VMEM((8, filters.shape[1]), f32),
        ],
        compiler_params=pltpu.CompilerParams(vmem_limit_bytes=SPACE),
        cost_estimate=pl.CostEstimate(
            flops=length * heads * 14_000_000, bytes_accessed=2**24, transcendentals=0
        ),
        name="mixer_backward",
    )(starts, raw, values, filters, decays, gates, gain, gated_grad, *kept)


def forward_dot(left_side, right_side):
    return jnp.dot(left_side, right_side, preferred_element_type=f32)


def times_transposed(left_side, right_side):
    return dot(left_side, right_side, 1, 1)


def transposed_times(left_side, right_side):
    return dot(left_side, right_side, 0, 0)


def rms_norm(values, gain):
    return values * lax.rsqrt(jnp.mean(values * values, axis=-1, keepdims=True) + epsilon) * gain


def swiglu(gate_rows, up_rows):
    return jax.nn.silu(gate_rows) * up_rows


def swap_seq(values):
    return lax.ppermute(values, "seq", [(0, 1), (1, 0)])


def in_order(own, other, axis):
    first = lax.axis_index("seq") == 0
    return jnp.where(
        first,
        jnp.concatenate([own, other], axis=axis),
        jnp.concatenate([other, own], axis=axis),
    )


def gather_seq(values, axis):
    if lax.axis_size("seq") == 2:
        return in_order(values, swap_seq(values), axis)
    return lax.all_gather(values, "seq", axis=axis, tiled=True)


def own_part(values, axis, index=None):
    size = values.shape[axis] // lax.axis_size("seq")
    index = lax.axis_index("seq") if index is None else index
    return lax.dynamic_slice_in_dim(values, index * size, size, axis=axis)


def sum_scatter_seq(values, axis):
    if lax.axis_size("seq") == 2:
        other = own_part(values, axis, 1 - lax.axis_index("seq")).astype(bf16)
        return own_part(values, axis) + swap_seq(other).astype(f32)
    return lax.psum_scatter(
        values.astype(bf16), "seq", scatter_dimension=axis, tiled=True
    ).astype(f32)


def own_first(values):
    if lax.axis_size("seq") == 2:
        return jnp.concatenate([values, swap_seq(values)], axis=0)
    return lax.all_gather(values, "seq", axis=0, tiled=True)


def sum_own_first(values):
    if lax.axis_size("seq") == 2:
        half = values.shape[0] // 2
        return values[:half] + swap_seq(values[half:].astype(bf16)).astype(f32)
    return sum_scatter_seq(values, 0)


def exchange_seq(values, split, join):
    if lax.axis_size("seq") == 2:
        other = own_part(values, split, 1 - lax.axis_index("seq"))
        return in_order(own_part(values, split), swap_seq(other), join)
    return lax.all_to_all(values, "seq", split_axis=split, concat_axis=join, tiled=True)


PLACES = 4


def in_grid():
    return lax.axis_size("shard") == 4 * PLACES and lax.axis_size("seq") == 2


def position():
    place = lax.axis_index("shard")
    return place // 4, (place // 2) % 2, place % 2


def flip(values, mask):
    size = lax.axis_size("shard")
    return lax.ppermute(values, "shard", [(i, i ^ mask) for i in range(size)])


def from_place(values, step):
    size = lax.axis_size("shard")
    return lax.ppermute(values, "shard", [(i, (i - 4 * step) % size) for i in range(size)])


def gather_shard(values):
    return lax.all_gather(values, "shard", axis=0, tiled=True)


def scatter_shard(values):
    return lax.psum_scatter(values, "shard", scatter_dimension=0, tiled=True)


def core_major(values):
    if not in_grid():
        return values
    rows, columns = values.shape
    places = values.reshape(rows, PLACES, 2, 2, columns // (4 * PLACES))
    return jnp.transpose(places, (0, 3, 2, 1, 4)).reshape(rows, columns)


def portion(values, index, count):
    size = values.shape[0] // count
    return lax.dynamic_slice_in_dim(values, index * size, size, axis=0)


def sum_pair(values, index, mask):
    sent = flip(portion(values, 1 - index, 2), mask)
    return (portion(values, index, 2).astype(f32) + sent.astype(f32)).astype(bf16)


def sum_along(values):
    z = position()[0]
    total = portion(values, z, PLACES).astype(f32)
    for r in range(1, PLACES):
        sent = from_place(portion(values, (z - r) % PLACES, PLACES), r)
        total = total + sent.astype(f32)
    return total.astype(bf16)


def first_sum(values):
    return sum_pair(values, position()[2], 1) if in_grid() else values


def second_sum(values):
    return sum_pair(values, position()[1], 2) if in_grid() else values


def third_sum(values):
    return sum_along(values) if in_grid() else scatter_shard(values)


def after(values, *earlier):
    return lax.optimization_barrier((values, earlier))[0]


def sum_small(values, axes):
    if not in_grid():
        return lax.psum(values, axes)
    for mask in (1, 2, 4, 8):
        values = values + flip(values, mask)
    return values


def on_device(
    tokens,
    doc_starts,
    norm_gain,
    query_weight,
    key_weight,
    value_weight,
    gate_weight,
    beta_decay_weight,
    conv_filters,
    decay_params,
    out_norm_gain,
    out_weight,
    ffn_norm_gain,
    ffn_gate_weight,
    ffn_up_weight,
    down_weight,
    out_cotangent,
):
    heads = HEADS // lax.axis_size("seq")
    shards = lax.axis_size("shard")
    rows = query_weight.shape[0]
    width = 2 * heads * KEY
    ff = ffn_gate_weight.shape[1]

    logit_weight = own_part(beta_decay_weight.reshape(rows, HEADS, 2), 1)
    gain_rows = out_norm_gain.shape[0]
    raw_piece = jnp.concatenate(
        [
            own_part(query_weight, 1),
            own_part(key_weight, 1),
            logit_weight[:, :, 0],
            logit_weight[:, :, 1],
            norm_gain[:, None],
            ffn_norm_gain[:, None],
            jnp.pad(out_norm_gain, (0, rows - gain_rows))[:, None],
            jnp.zeros((rows, KEY - 2 * heads - 3), bf16),
        ],
        axis=1,
    )
    units = ff // shards // lax.axis_size("seq")

    def own_units(weight):
        return own_part(weight.reshape(rows, shards, ff // shards), 2).reshape(rows, shards * units)

    raw_wide = raw_piece.shape[1]
    value_end = raw_wide + heads * VALUE
    mixer_full = gather_shard(
        jnp.concatenate([raw_piece, own_part(value_weight, 1), own_part(gate_weight, 1)], axis=1)
    )
    raw_full = mixer_full[:, :raw_wide]
    value_full = mixer_full[:, raw_wide:value_end]
    gate_full = mixer_full[:, value_end:]
    half = shards * units
    model = out_weight.shape[1]
    out_rows = out_weight.shape[0]
    tall_full = gather_shard(jnp.concatenate([out_weight, own_part(down_weight, 0)], axis=0))
    tall_full = tall_full.reshape(shards, out_rows + units, model)
    out_full = tall_full[:, :out_rows].reshape(shards * out_rows, model)
    down_full = tall_full[:, out_rows:].reshape(half, model)
    ffn_full = gather_shard(
        jnp.concatenate([own_units(ffn_gate_weight), own_units(ffn_up_weight)], axis=1)
    )
    first_gain = raw_full[:, width + 2 * heads].astype(f32)
    second_gain = raw_full[:, width + 2 * heads + 1].astype(f32)
    third_gain = (
        raw_full[:, width + 2 * heads + 2]
        .reshape(shards, rows)[:, :gain_rows]
        .reshape(1, shards * gain_rows)
        .astype(f32)
    )

    own_tokens = tokens[0]
    token_count = own_tokens.shape[0]
    inputs = own_tokens.astype(f32)
    cotangent = out_cotangent[0]
    if lax.axis_size("seq") == 2:
        other = swap_seq(jnp.concatenate([own_tokens, cotangent], axis=0))
        all_inputs = in_order(own_tokens, other[:token_count], 0).astype(f32)
        all_cotangent = jnp.concatenate([cotangent, other[token_count:]], axis=0)
    else:
        all_inputs = gather_seq(own_tokens, 0).astype(f32)
        all_cotangent = own_first(cotangent)
    length = all_inputs.shape[0]
    all_scaled = all_inputs * lax.rsqrt(
        jnp.mean(all_inputs * all_inputs, axis=-1, keepdims=True) + epsilon
    )
    normed = (all_scaled * first_gain).astype(bf16)
    raw = forward_dot(normed, raw_full).astype(bf16)
    values = forward_dot(normed, value_full).astype(bf16)
    gate_rows = forward_dot(normed, gate_full)
    filters = jnp.concatenate(
        [
            conv_filters[:, :, :KEY].reshape(CONV, heads * KEY),
            conv_filters[:, :, KEY : 2 * KEY].reshape(CONV, heads * KEY),
            conv_filters[:, :, 2 * KEY :].reshape(CONV, heads * VALUE),
        ],
        axis=1,
    )
    decays = decay_params.T
    gated, *kept = mixer_forward(
        raw, values, filters, decays, doc_starts, gate_rows, third_gain, heads
    )
    gated_low = exchange_seq(gated, 0, 1)
    gated_low, down_full = lax.optimization_barrier((gated_low, down_full))
    middle = inputs + forward_dot(gated_low, out_full)
    second_norm, second_pull = jax.vjp(rms_norm, middle, second_gain)
    hidden = own_first(second_norm.astype(bf16))
    both_ffn = forward_dot(hidden, ffn_full)
    activated, swiglu_pull = jax.vjp(swiglu, both_ffn[:, :half], both_ffn[:, half:])
    activated_low = activated.astype(bf16)
    act_grad = times_transposed(all_cotangent, down_full)
    both_grad = jnp.concatenate([g.astype(bf16) for g in swiglu_pull(act_grad)], axis=1)
    hidden_grad = sum_own_first(times_transposed(both_grad, ffn_full))
    out_parts = forward_dot(activated_low, down_full)
    down_grad = transposed_times(activated_low, all_cotangent).astype(bf16)
    ffn_grad = transposed_times(core_major(after(hidden, both_ffn)), both_grad).astype(bf16)
    ffn_grad = first_sum(ffn_grad)
    out_sent = out_parts[token_count:].astype(bf16)
    hidden_grad, ffn_grad, down_grad, out_parts, out_sent = lax.optimization_barrier(
        (hidden_grad, ffn_grad, down_grad, out_parts, out_sent)
    )
    middle_part, ffn_gain_grad = second_pull(hidden_grad)
    middle_grad = cotangent.astype(f32) + middle_part
    branch_low = middle_grad.astype(bf16)
    out_grad = transposed_times(gated_low, branch_low).astype(bf16)
    gated_grad = exchange_seq(times_transposed(branch_low, out_full).astype(bf16), 1, 0)
    ffn_grad = second_sum(ffn_grad)
    tall_grad = jnp.concatenate(
        [out_grad.reshape(shards, out_rows, model), down_grad.reshape(shards, units, model)], axis=1
    ).reshape(shards * (out_rows + units), model)
    gated_grad, ffn_grad, tall_grad = lax.optimization_barrier((gated_grad, ffn_grad, tall_grad))
    ffn_share = third_sum(ffn_grad)
    tall_share = scatter_shard(tall_grad)
    if lax.axis_size("seq") == 2:
        out_parts = out_parts[:token_count] + swap_seq(after(out_sent, gated_grad)).astype(f32)
    else:
        out_parts = sum_own_first(out_parts)
    block_out = (middle + out_parts).astype(bf16)
    mixer_grad, filters_grad, decays_grad, out_gain_grad = mixer_backward(
        raw,
        values,
        filters,
        decays,
        doc_starts,
        gate_rows,
        third_gain,
        gated_grad,
        kept,
        heads,
    )
    mixer_grad, ffn_share, block_out = lax.optimization_barrier((mixer_grad, ffn_share, block_out))
    mixer_weight_grad = transposed_times(normed, mixer_grad).astype(bf16)
    mixer_grad, mixer_weight_grad = lax.optimization_barrier((mixer_grad, mixer_weight_grad))
    mixer_share = scatter_shard(mixer_weight_grad)
    normed_grad = times_transposed(mixer_grad, mixer_full)
    norm_gain_grad = jnp.sum(normed_grad * all_scaled, axis=0)
    if lax.axis_size("seq") == 2:
        sent = own_part(normed_grad, 0, 1 - lax.axis_index("seq")).astype(bf16)
        own_normed_grad = own_part(normed_grad, 0) + swap_seq(sent).astype(f32)
    else:
        sent = normed_grad
        own_normed_grad = sum_scatter_seq(normed_grad, 0)
    _, first_pull = jax.vjp(lambda v: rms_norm(v, first_gain), inputs)
    tokens_grad = middle_grad + first_pull(own_normed_grad)[0]

    def all_units(share):
        share = gather_seq(share.reshape(rows, shards, units), 2)
        return share.reshape(rows, ff).astype(f32)

    ffn_gate_share = all_units(ffn_share[:, :half])
    ffn_up_share = all_units(ffn_share[:, half:])
    tall_share = gather_seq(after(tall_share, mixer_grad)[None], 0).astype(f32)
    out_share = jnp.sum(tall_share[:, :out_rows], axis=0)
    down_share = tall_share[:, out_rows:].reshape(-1, model)
    if lax.axis_size("seq") == 2:
        other_share = swap_seq(mixer_share)

        def side_by_side(start, stop):
            own, other = mixer_share[:, start:stop], other_share[:, start:stop]
            return in_order(own.astype(f32), other.astype(f32), 1)
    else:
        every = gather_seq(mixer_share[None], 0)

        def side_by_side(start, stop):
            part = jnp.swapaxes(every[:, :, start:stop], 0, 1)
            return part.reshape(rows, -1).astype(f32)

    query_share = side_by_side(0, heads * KEY)
    key_share = side_by_side(heads * KEY, width)
    value_share = side_by_side(raw_wide, value_end)
    gate_share = side_by_side(value_end, mixer_share.shape[1])
    logit_share = side_by_side(width, width + 2 * heads).reshape(rows, -1, 2, heads)
    logit_share = jnp.swapaxes(logit_share, 2, 3).reshape(rows, 2 * HEADS)

    all_width = filters.shape[1]
    filters_grad = jnp.sum(filters_grad.reshape(CONV, 8, all_width), axis=1)
    lengths = [shards * n for n in (norm_gain.shape[0], gain_rows, ffn_norm_gain.shape[0])]
    small = jnp.concatenate(
        [
            filters_grad.reshape(CONV * all_width),
            decays_grad.reshape(2 * heads),
            norm_gain_grad,
            jnp.sum(out_gain_grad, axis=0),
            ffn_gain_grad,
        ]
    )
    small = sum_small(after(small, sent), ("shard",))
    head_end = CONV * all_width + 2 * heads
    filters_grad = small[: CONV * all_width].reshape(CONV, all_width)
    decays_grad = small[CONV * all_width : head_end].reshape(2, heads)
    gains = small[head_end:]
    gains = gains + swap_seq(gains) if in_grid() else lax.psum(gains, "seq")
    split = (heads * KEY, 2 * heads * KEY)
    filters_out = jnp.concatenate(
        [
            filters_grad[:, : split[0]].reshape(CONV, heads, KEY),
            filters_grad[:, split[0] : split[1]].reshape(CONV, heads, KEY),
            filters_grad[:, split[1] :].reshape(CONV, heads, VALUE),
        ],
        axis=2,
    )
    gains = [
        gains[: lengths[0]],
        gains[lengths[0] : lengths[0] + lengths[1]],
        gains[lengths[0] + lengths[1] :],
    ]
    place = lax.axis_index("shard")
    gains = [
        lax.dynamic_slice_in_dim(g, place * (g.shape[0] // shards), g.shape[0] // shards)
        for g in gains
    ]
    return (
        block_out[None],
        tokens_grad[None],
        gains[0],
        query_share,
        key_share,
        value_share,
        gate_share,
        logit_share,
        filters_out,
        decays_grad.T,
        gains[1],
        out_share,
        gains[2],
        ffn_gate_share,
        ffn_up_share,
        down_share,
    )


def solution(mesh):
    in_specs = (
        P("shard", "seq", None),
        P("shard", None),
        P("shard"),
        P("shard", None),
        P("shard", None),
        P("shard", None),
        P("shard", None),
        P("shard", None),
        P(None, "seq", None),
        P("seq", None),
        P("shard"),
        P("shard", None),
        P("shard"),
        P("shard", None),
        P("shard", None),
        P("shard", None),
        P("shard", "seq", None),
    )
    out_specs = (
        P("shard", "seq", None),
        P("shard", "seq", None),
        P("shard"),
        P("shard", None),
        P("shard", None),
        P("shard", None),
        P("shard", None),
        P("shard", None),
        P(None, "seq", None),
        P("seq", None),
        P("shard"),
        P("shard", None),
        P("shard"),
        P("shard", None),
        P("shard", None),
        P("shard", None),
    )
    return jax.shard_map(
        on_device, mesh=mesh, in_specs=in_specs, out_specs=out_specs, check_vma=False
    )
```

```python
import functools

import jax
import jax.numpy as jnp
from jax import lax
from jax.experimental import pallas as pl
from jax.experimental.pallas import tpu as pltpu
from jax.sharding import PartitionSpec as P

HEADS = 8
KEY = 128
VALUE = 256
CONV = 4
GROUP = 64
HALO = 16
SUB = 4
epsilon = 1e-06
f32 = jnp.float32
bf16 = jnp.bfloat16


def dot(a, b, ca=1, cb=0):
    return lax.dot_general(a, b, (((ca,), (cb,)), ((), ())), preferred_element_type=f32)


def halves(values):
    high = values.astype(bf16)
    return high, (values - high.astype(f32)).astype(bf16)


def fine_dot(a, b, ca=1, cb=0):
    if not isinstance(a, tuple):
        return dot(a, b[0], ca, cb) + dot(a, b[1], ca, cb)
    if not isinstance(b, tuple):
        return dot(a[0], b, ca, cb) + dot(a[1], b, ca, cb)
    return dot(a[0], b[0], ca, cb) + (dot(a[0], b[1], ca, cb) + dot(a[1], b[0], ca, cb))


def iota(shape, dim):
    return lax.broadcasted_iota(jnp.int32, shape, dim)


def doc_count(starts_ref, times):
    count = jnp.zeros(times.shape, jnp.int32)
    for s in range(starts_ref.shape[1]):
        count = count + jnp.where(times >= starts_ref[0, s], 1, 0)
    return count


def scalar_doc(starts_ref, time):
    count = 0
    for s in range(starts_ref.shape[1]):
        count = count + (time >= starts_ref[0, s]).astype(jnp.int32)
    return count


def per_head(cols, heads, width):
    rows = cols.shape[0]
    lane = iota((rows, heads * width), 1)
    out = jnp.broadcast_to(cols[:, heads - 1 : heads], (rows, heads * width))
    for h in range(heads - 2, -1, -1):
        out = jnp.where(lane < (h + 1) * width, cols[:, h : h + 1], out)
    return out


def head_sums(panel, heads, width):
    lane = iota(panel.shape, 1)
    sums = []
    for h in range(heads):
        inside = (lane >= h * width) & (lane < (h + 1) * width)
        sums.append(jnp.sum(jnp.where(inside, panel, 0.0), axis=1, keepdims=True))
    return columns(sums)


def across(mask, width):
    return jnp.concatenate([mask] * (width // KEY), axis=1)


def columns(parts):
    rows = parts[0].shape[0]
    lane = iota((rows, len(parts)), 1)
    out = jnp.broadcast_to(parts[-1], (rows, len(parts)))
    for h in range(len(parts) - 2, -1, -1):
        out = jnp.where(lane == h, parts[h], out)
    return out


def block_diagonal(panel, heads):
    if heads == 1:
        return panel
    lane = iota(panel.shape, 1)
    zero = jnp.zeros_like(panel)
    parts = []
    for h in range(heads):
        inside = (lane >= h * GROUP) & (lane < (h + 1) * GROUP)
        parts.append(jnp.where(inside, panel, zero))
    return jnp.concatenate(parts, axis=0)


def diagonal_panel(full, heads):
    if heads == 1:
        return full
    lane = iota((GROUP, heads * GROUP), 1)
    out = full[(heads - 1) * GROUP :]
    for h in range(heads - 2, -1, -1):
        out = jnp.where(lane < (h + 1) * GROUP, full[h * GROUP : (h + 1) * GROUP], out)
    return out


def key_diagonal(keys):
    heads = len(keys)
    if heads == 1:
        return keys[0]
    zero = jnp.zeros_like(keys[0])
    rows = []
    for h in range(heads):
        rows.append(jnp.concatenate([keys[h] if o == h else zero for o in range(heads)], axis=1))
    return jnp.concatenate(rows, axis=0)


def scan_rows(values, reverse=False):
    rows = values.shape[0]
    index = iota(values.shape, 0)
    step = 1
    while step < rows:
        if reverse:
            moved = pltpu.roll(values, rows - step, 0)
            values = values + jnp.where(index < rows - step, moved, 0.0)
        else:
            moved = pltpu.roll(values, step, 0)
            values = values + jnp.where(index >= step, moved, 0.0)
        step *= 2
    return values


def sigmoid(v):
    return 1.0 / (1.0 + jnp.exp(-v))


def softplus(v):
    return jnp.maximum(v, 0.0) + jnp.log(1.0 + jnp.exp(-jnp.abs(v)))


def in_turn(generators):
    generators = list(generators)
    while generators:
        still = []
        for generator in generators:
            if next(generator, True) is None:
                still.append(generator)
        generators = still


class Block:
    def __init__(self, heads, base, raw_ref, value_ref, filters_ref, decay_ref, starts_ref):
        self.heads = heads
        self.base = base
        self.raw_ref = raw_ref
        self.value_ref = value_ref
        self.filters_ref = filters_ref
        self.decay_ref = decay_ref
        self.starts_ref = starts_ref

    def build(self):
        heads, base, starts_ref = self.heads, self.base, self.starts_ref
        raw_ref, decay_ref = self.raw_ref, self.decay_ref
        width = 2 * heads * KEY
        times = base + iota((GROUP, 1), 0)
        docs = doc_count(starts_ref, times)
        wide = (GROUP, KEY)
        self.masks, self.next_masks = [], []
        for o in range(1, CONV):
            same = (docs == doc_count(starts_ref, times - o)).astype(f32)
            self.masks.append(jnp.broadcast_to(same, wide))
            same = (docs == doc_count(starts_ref, times + o)).astype(f32)
            self.next_masks.append(jnp.broadcast_to(same, wide))
        self.query, self.keys, self.query_pre, self.key_pre = [], [], [], []
        self.query_conv, self.key_conv, self.query_scale, self.key_scale = [], [], [], []
        for h in range(heads):
            pre = self.convolve(h * KEY, KEY)
            conv = pre * sigmoid(pre)
            scale = lax.rsqrt(jnp.sum(conv * conv, axis=1, keepdims=True) + epsilon)
            self.query_pre.append(pre)
            self.query_conv.append(conv)
            self.query_scale.append(scale)
            self.query.append(conv * scale * KEY ** (-0.5))
        for h in range(heads):
            pre = self.convolve((heads + h) * KEY, KEY)
            conv = pre * sigmoid(pre)
            scale = lax.rsqrt(jnp.sum(conv * conv, axis=1, keepdims=True) + epsilon)
            self.key_pre.append(pre)
            self.key_conv.append(conv)
            self.key_scale.append(scale)
            self.keys.append(conv * scale)
        yield
        logits = raw_ref[pl.ds(base, GROUP), width : width + KEY].astype(f32)
        self.strength = sigmoid(logits[:, :heads])
        self.decay_logit = logits[:, heads : 2 * heads] + decay_ref[1:2, :heads]
        self.decay_rate = -jnp.exp(decay_ref[0:1, :heads])
        self.log_decay = self.decay_rate * softplus(self.decay_logit)
        yield
        sums = scan_rows(self.log_decay)
        yield
        self.sums = sums
        last = sums[GROUP - 1 : GROUP]
        before = scalar_doc(starts_ref, base - 1)
        final = scalar_doc(starts_ref, base + GROUP - 1)
        self.entering = jnp.where(docs == before, jnp.exp(sums), 0.0)
        same_last = docs == final
        self.leaving = jnp.where(same_last, jnp.exp(jnp.where(same_last, last - sums, 0.0)), 0.0)
        self.retain = self.entering[GROUP - 1 : GROUP]
        yield
        shape = (GROUP, heads * GROUP)
        row = iota(shape, 0)
        place = jnp.bitwise_and(iota(shape, 1), GROUP - 1)
        self.row, self.place = row, place
        across = jnp.bitwise_and(iota((1, heads * GROUP), 1), GROUP - 1)
        docs_across = doc_count(starts_ref, base + across)
        same = docs == docs_across
        self.inclusive = same & (row >= place)
        self.strict = same & (row > place)
        sums_down = per_head(sums, heads, GROUP)
        sums_across = jnp.sum(jnp.where(row == place, sums_down, 0.0), axis=0, keepdims=True)
        gap = jnp.where(self.inclusive, sums_down - sums_across, 0.0)
        self.fade = jnp.where(self.inclusive, jnp.exp(gap), 0.0)
        yield
        self.strength_down = per_head(self.strength, heads, GROUP)
        low_keys = [k.astype(bf16) for k in self.keys]
        low_query = [q.astype(bf16) for q in self.query]
        self.keys = [k.astype(f32) for k in low_keys]
        self.query = [q.astype(f32) for q in low_query]
        self.low_keys, self.low_query = low_keys, low_query
        self.key_diag = key_diagonal(low_keys)
        left = jnp.concatenate(
            [jnp.concatenate(low_keys, axis=1), jnp.concatenate(low_query, axis=1)], axis=0
        )
        self.query_key_rows = left
        grams = dot(left, self.key_diag, 1, 1)
        yield
        self.key_gram = grams[:GROUP]
        self.score_gram = grams[GROUP:]
        self.system = jnp.where(self.strict, self.strength_down * self.key_gram * self.fade, 0.0)
        self.scores = self.score_gram * self.fade

    def taps(self, start, width):
        source = self.raw_ref
        if start >= 2 * self.heads * KEY:
            source = self.value_ref
            start = start - 2 * self.heads * KEY
        current = source[pl.ds(self.base, GROUP), start : start + width].astype(f32)
        earlier = pl.multiple_of(jnp.maximum(self.base - HALO, 0), HALO)
        halo = source[pl.ds(earlier, HALO), start : start + width].astype(f32)
        extended = jnp.concatenate([halo, current], axis=0)
        return [current] + [
            pltpu.roll(extended, o, 0)[HALO:] * across(self.masks[o - 1], width)
            for o in range(1, CONV)
        ]

    def convolve(self, start, width):
        taps = self.taps(start, width)
        filters = self.filters_ref[:, start : start + width]
        total = taps[0] * filters[CONV - 1 : CONV]
        for o in range(1, CONV):
            total = total + taps[o] * filters[CONV - 1 - o : CONV - o]
        return total


def inverse(systems, heads, row, place):
    eye = (row == place).astype(f32)
    apart = jnp.bitwise_xor(row, place)

    def part(system, size):
        return jnp.where((apart >= size) & (apart < 2 * size), system, 0.0)

    results = [eye - part(system, 1) for system in systems]
    size = 2
    while size < GROUP:
        low = [result.astype(bf16) for result in results]
        inner = [
            dot(part(system, size).astype(bf16), block_diagonal(one, heads))
            for system, one in zip(systems, low)
        ]
        inner = [block_diagonal(one.astype(bf16), heads) for one in inner]
        results = [
            result - dot(one, right) for result, one, right in zip(results, low, inner)
        ]
        size *= 2
    return results


def forward_kernel(
    heads, starts_ref, raw_ref, value_ref, filters_ref, decay_ref, gate_ref, gain_ref,
    gated_ref, mixed_ref, inverse_ref, delta_ref, rest_ref, memory_ref, state,
):
    step = pl.program_id(0)

    @pl.when(step == 0)
    def _():
        state[...] = jnp.zeros_like(state)

    blocks = []
    for s in range(SUB):
        base = pl.multiple_of((step * SUB + s) * GROUP, GROUP)
        blocks.append(Block(heads, base, raw_ref, value_ref, filters_ref, decay_ref, starts_ref))
    in_turn(block.build() for block in blocks)
    solves = inverse([block.system for block in blocks], heads, blocks[0].row, blocks[0].place)
    for s, block in enumerate(blocks):
        block.values = []
        for h in range(heads):
            pre = block.convolve(2 * heads * KEY + h * VALUE, VALUE)
            block.values.append(pre * sigmoid(pre))
        block.solve = solves[s]
        inverse_ref[s * GROUP : (s + 1) * GROUP] = block.solve.astype(bf16)
    for s, block in enumerate(blocks):
        from_state, rest, right = [], [], []
        for h in range(heads):
            entering = block.entering[:, h : h + 1]
            memory = state[h * KEY : (h + 1) * KEY].astype(bf16)
            memory_ref[(s * heads + h) * KEY : (s * heads + h + 1) * KEY] = memory
            both = jnp.concatenate([block.low_keys[h], block.low_query[h]], axis=0)
            read = dot(both, memory)
            from_state.append(entering * read[GROUP:])
            missing = block.values[h] - entering * read[:GROUP]
            rest.append(missing.astype(bf16))
            right.append(block.strength[:, h : h + 1] * missing)
        rest_ref[s * heads * GROUP : (s + 1) * heads * GROUP] = jnp.concatenate(rest, axis=0)
        solve = tuple(block_diagonal(p, heads) for p in halves(block.solve))
        delta = fine_dot(solve, halves(jnp.concatenate(right, axis=0)))
        delta_ref[s * heads * GROUP : (s + 1) * heads * GROUP] = delta
        scores = tuple(block_diagonal(p, heads) for p in halves(block.scores))
        outputs = fine_dot(scores, halves(delta))
        for h in range(heads):
            rows = slice(h * GROUP, (h + 1) * GROUP)
            out = from_state[h] + outputs[rows]
            here = slice(s * GROUP, (s + 1) * GROUP)
            lanes = slice(h * VALUE, (h + 1) * VALUE)
            low = out.astype(bf16)
            mixed_ref[here, lanes] = low
            low = low.astype(f32)
            gate = gate_ref[here, lanes]
            scale = lax.rsqrt(jnp.mean(low * low, axis=1, keepdims=True) + epsilon)
            gated = low * scale * gain_ref[0:1] * (gate * sigmoid(gate))
            gated_ref[here, lanes] = gated.astype(bf16)
            leaving = halves(block.leaving[:, h : h + 1] * delta[rows])
            keep = block.retain[:, h : h + 1]
            own = slice(h * KEY, (h + 1) * KEY)
            state[own] = keep * state[own] + fine_dot(block.low_keys[h], leaving, 0, 0)


def silu_slope(pre):
    gate = sigmoid(pre)
    return gate * (1.0 + pre * (1.0 - gate))


def backward_kernel(
    heads, starts_ref, seq_ref, raw_ref, value_ref, filters_ref, decay_ref, gate_ref, gain_ref,
    own_grad_ref, other_grad_ref, mixed_ref, inverse_ref, delta_ref, rest_ref, memory_ref,
    raw_grad_ref, filters_grad_ref, decay_grad_ref, gain_grad_ref,
    state, halo,
):
    step = pl.program_id(0)
    steps = pl.num_programs(0)
    width = 2 * heads * KEY
    own_rows = (2 * (steps - 1 - step) >= steps) == (seq_ref[0] != 0)

    @pl.when(step == 0)
    def _():
        state[...] = jnp.zeros_like(state)
        gain_grad_ref[...] = jnp.zeros_like(gain_grad_ref)
        halo[...] = jnp.zeros_like(halo)
        filters_grad_ref[...] = jnp.zeros_like(filters_grad_ref)
        decay_grad_ref[...] = jnp.zeros_like(decay_grad_ref)

    def pull(s):
        base = pl.multiple_of(((steps - 1 - step) * SUB + s) * GROUP, GROUP)
        block = Block(heads, base, raw_ref, value_ref, filters_ref, decay_ref, starts_ref)
        yield from block.build()
        yield
        here = slice(s * GROUP, (s + 1) * GROUP)
        stacked = slice(s * heads * GROUP, (s + 1) * heads * GROUP)
        solve = inverse_ref[here]
        delta = delta_ref[stacked]
        rest = rest_ref[stacked]
        mixed_grads = []
        for h in range(heads):
            lanes = slice(h * VALUE, (h + 1) * VALUE)
            grad = jnp.where(
                own_rows,
                own_grad_ref[here, lanes].astype(f32),
                other_grad_ref[here, lanes].astype(f32),
            )
            mixed = mixed_ref[here, lanes].astype(f32)
            gate = gate_ref[here, lanes]
            scale = lax.rsqrt(jnp.mean(mixed * mixed, axis=1, keepdims=True) + epsilon)
            unit = mixed * scale
            open_gate = sigmoid(gate)
            swish = gate * open_gate
            along = grad * unit
            product = (along * swish).reshape(GROUP // 8, 8, VALUE)
            gain_grad_ref[...] = gain_grad_ref[...] + jnp.sum(product, axis=0)
            gate_grad = along * gain_ref[0:1] * (open_gate * (1.0 + gate * (1.0 - open_gate)))
            behind = width + KEY + (heads + h) * VALUE
            raw_grad_ref[here, behind : behind + VALUE] = gate_grad.astype(bf16)
            unit_grad = grad * swish * gain_ref[0:1]
            inner = jnp.mean(unit_grad * unit, axis=1, keepdims=True)
            mixed_grads.append((scale * (unit_grad - unit * inner)).astype(bf16))
        out_grad = jnp.concatenate(mixed_grads, axis=0)
        yield
        scores = tuple(block_diagonal(p, heads) for p in halves(block.scores))
        from_scores = fine_dot(scores, out_grad, 0, 0)
        delta = halves(delta)
        score_part = diagonal_panel(sum(dot(out_grad, d, 1, 1) for d in delta), heads)
        scores_grad = jnp.where(block.inclusive, score_part, 0.0)
        score_gram_grad = scores_grad * block.fade
        solve = block_diagonal(solve, heads)
        yield "chain"
        later = [state[h * KEY : (h + 1) * KEY] for h in range(heads)]
        later_low = [m.astype(bf16) for m in later]
        pulled = jnp.concatenate(
            [
                block.leaving[:, h : h + 1] * dot(block.low_keys[h], later_low[h])
                for h in range(heads)
            ],
            axis=0,
        )
        delta_grad = pulled + from_scores
        right_grad = dot(solve, delta_grad.astype(bf16), 0, 0)
        rest_grad, pairs = [], []
        for h in range(heads):
            rows = slice(h * GROUP, (h + 1) * GROUP)
            rest_grad.append(block.strength[:, h : h + 1] * right_grad[rows])
            pairs.append(jnp.concatenate([out_grad[rows], rest_grad[h].astype(bf16)], axis=0))
            entering = block.entering[:, h : h + 1]
            left = jnp.concatenate(
                [entering * block.query[h], -entering * block.keys[h]], axis=0
            ).astype(bf16)
            state[h * KEY : (h + 1) * KEY] = (
                block.retain[:, h : h + 1] * later[h] + dot(left, pairs[h], 0, 0)
            )
        yield "chain"
        entering_query_grad, entering_key_grad, leaving_key_grad, retain_grad = [], [], [], []
        strength_grad = []
        for h in range(heads):
            rows = slice(h * GROUP, (h + 1) * GROUP)
            strength_grad.append(
                jnp.sum(right_grad[rows] * rest[rows].astype(f32), axis=1, keepdims=True)
            )
            memory = memory_ref[(s * heads + h) * KEY : (s * heads + h + 1) * KEY]
            back = dot(pairs[h], memory, 1, 1)
            entering_query_grad.append(back[:GROUP])
            entering_key_grad.append(-back[GROUP:])
            leaving_key_grad.append(sum(dot(d[rows], later_low[h], 1, 1) for d in delta))
            product = later[h] * memory.astype(f32)
            retain_grad.append(
                jnp.sum(jnp.sum(product, axis=0, keepdims=True), axis=1, keepdims=True)
            )
        yield
        right_low = right_grad.astype(bf16)
        system_part = diagonal_panel(sum(dot(right_low, d, 1, 1) for d in delta), heads)
        system_grad = jnp.where(block.strict, -system_part, 0.0)
        faded = system_grad * block.fade
        key_gram_grad = block.strength_down * faded
        gap_grad = score_gram_grad * block.score_gram + key_gram_grad * block.key_gram
        yield
        strength_panel = head_sums(faded * block.key_gram, heads, GROUP)
        down = jnp.sum(gap_grad, axis=0, keepdims=True)
        gap_rows = head_sums(
            gap_grad - jnp.where(block.row == block.place, down, 0.0), heads, GROUP
        )
        yield
        both_low = jnp.concatenate([key_gram_grad, score_gram_grad], axis=0).astype(bf16)
        straight = dot(both_low, block.key_diag)
        turned = dot(both_low, block.query_key_rows, 0, 0)
        yield
        entering_grad, leaving_grad = [], []
        for h in range(heads):
            lanes = slice(h * KEY, (h + 1) * KEY)
            entering = block.entering[:, h : h + 1]
            fading = block.leaving[:, h : h + 1]
            query_grad = entering * entering_query_grad[h] + straight[GROUP:, lanes]
            key_grad = (
                turned[h * GROUP : (h + 1) * GROUP, lanes]
                + straight[:GROUP, lanes]
                + fading * leaving_key_grad[h]
                + entering * entering_key_grad[h]
            )
            entering_grad.append(
                jnp.sum(
                    entering_query_grad[h] * block.query[h] + entering_key_grad[h] * block.keys[h],
                    axis=1,
                    keepdims=True,
                )
            )
            leaving_grad.append(
                jnp.sum(leaving_key_grad[h] * block.keys[h], axis=1, keepdims=True)
            )
            for start, grad, conv, scale, pre, factor in (
                (h * KEY, query_grad, block.query_conv[h], block.query_scale[h],
                 block.query_pre[h], KEY ** (-0.5)),
                ((heads + h) * KEY, key_grad, block.key_conv[h], block.key_scale[h],
                 block.key_pre[h], 1.0),
            ):
                along = jnp.sum(grad * conv, axis=1, keepdims=True)
                conv_grad = (factor * scale) * (grad - conv * (scale * scale * along))
                convolve_back(
                    block, s, start, start, KEY, conv_grad * silu_slope(pre), starts_ref,
                    raw_grad_ref, filters_grad_ref, halo,
                )
            yield
            start = 2 * heads * KEY + h * VALUE
            pre = block.convolve(start, VALUE)
            convolve_back(
                block, s, start, start + KEY, VALUE, rest_grad[h] * silu_slope(pre), starts_ref,
                raw_grad_ref, filters_grad_ref, halo,
            )
        yield
        entering_grad = columns(entering_grad) * block.entering
        leaving_grad = columns(leaving_grad) * block.leaving
        strength_grad = columns(strength_grad) + strength_panel
        retain_grad = columns(retain_grad) * block.retain
        at_last = jnp.sum(leaving_grad, axis=0, keepdims=True) + retain_grad
        index = iota((GROUP, heads), 0)
        sums_grad = (
            entering_grad - leaving_grad + gap_rows + jnp.where(index == GROUP - 1, at_last, 0.0)
        )
        log_decay_grad = scan_rows(sums_grad, reverse=True)
        yield
        logit_grad = log_decay_grad * block.decay_rate * sigmoid(block.decay_logit)
        beta_grad = strength_grad * block.strength * (1.0 - block.strength)
        lane = iota((GROUP, KEY), 1)
        packed = jnp.zeros((GROUP, KEY), f32)
        for h in range(heads):
            packed = jnp.where(lane == h, beta_grad[:, h : h + 1], packed)
            packed = jnp.where(lane == heads + h, logit_grad[:, h : h + 1], packed)
        raw_grad_ref[here, width : width + KEY] = packed.astype(bf16)
        scale_sum = jnp.sum(log_decay_grad * block.log_decay, axis=0, keepdims=True)
        bias_sum = jnp.sum(logit_grad, axis=0, keepdims=True)
        decay_grad_ref[0:1] = decay_grad_ref[0:1] + scale_sum
        decay_grad_ref[1:2] = decay_grad_ref[1:2] + bias_sum

    pulls = [pull(s) for s in range(SUB - 1, -1, -1)]
    waiting = list(pulls)
    while waiting:
        waiting = [p for p in waiting if next(p) is None]
    for p in pulls:
        next(p)
    in_turn(pulls)


def convolve_back(
    block, s, start, place, width, pre_grad, starts_ref, grad_ref, filters_grad_ref, halo
):
    lanes = slice(start, start + width)
    taps = block.taps(start, width)
    for o in range(CONV):
        j = CONV - 1 - o
        product = (pre_grad * taps[o]).reshape(GROUP // 8, 8, width)
        filters_grad_ref[j * 8 : (j + 1) * 8, lanes] = filters_grad_ref[
            j * 8 : (j + 1) * 8, lanes
        ] + jnp.sum(product, axis=0)
    filters = block.filters_ref[:, lanes]
    extended = jnp.concatenate([pre_grad, halo[:, lanes]], axis=0)
    rows = GROUP + 8
    total = pre_grad * filters[CONV - 1 : CONV]
    for o in range(1, CONV):
        moved = pltpu.roll(extended, rows - o, 0)[:GROUP] * across(block.next_masks[o - 1], width)
        total = total + moved * filters[CONV - 1 - o : CONV - o]
    grad_ref[s * GROUP : (s + 1) * GROUP, place : place + width] = total.astype(bf16)
    halo[:, lanes] = pre_grad[:8]


SPACE = 56 * 2**20


def mixer_forward(raw, values, filters, decays, starts, gates, gain, heads):
    length, wide = raw.shape
    steps = length // (SUB * GROUP)
    rows = SUB * GROUP
    blocks = length // GROUP
    whole = lambda a: pl.BlockSpec(a.shape, lambda i: (0, 0))
    part = lambda r, c: pl.BlockSpec((r, c), lambda i: (i, 0))
    return pl.pallas_call(
        functools.partial(forward_kernel, heads),
        grid=(steps,),
        in_specs=[
            pl.BlockSpec(memory_space=pltpu.SMEM),
            whole(raw),
            whole(values),
            whole(filters),
            whole(decays),
            part(rows, heads * VALUE),
            whole(gain),
        ],
        out_specs=[
            part(rows, heads * VALUE),
            part(rows, heads * VALUE),
            part(rows, heads * GROUP),
            part(rows * heads, VALUE),
            part(rows * heads, VALUE),
            part(SUB * heads * KEY, VALUE),
        ],
        out_shape=[
            jax.ShapeDtypeStruct((length, heads * VALUE), bf16),
            jax.ShapeDtypeStruct((length, heads * VALUE), bf16),
            jax.ShapeDtypeStruct((length, heads * GROUP), bf16),
            jax.ShapeDtypeStruct((length * heads, VALUE), f32),
            jax.ShapeDtypeStruct((length * heads, VALUE), bf16),
            jax.ShapeDtypeStruct((blocks * heads * KEY, VALUE), bf16),
        ],
        scratch_shapes=[pltpu.VMEM((heads * KEY, VALUE), f32)],
        compiler_params=pltpu.CompilerParams(vmem_limit_bytes=SPACE),
        cost_estimate=pl.CostEstimate(
            flops=length * heads * 11_000_000, bytes_accessed=2**24, transcendentals=0
        ),
        name="mixer_forward",
    )(starts, raw, values, filters, decays, gates, gain)


def mixer_backward(raw, values, filters, decays, starts, gates, gain, gated_grads, kept, heads):
    length, wide = raw.shape
    steps = length // (SUB * GROUP)
    rows = SUB * GROUP
    whole = lambda a: pl.BlockSpec(a.shape, lambda i: (0, 0))
    same = lambda r, c: pl.BlockSpec((r, c), lambda i: (0, 0))
    part = lambda r, c: pl.BlockSpec((r, c), lambda i: (steps - 1 - i, 0))
    count = gated_grads[0].shape[0] // rows
    part_grad = pl.BlockSpec((rows, heads * VALUE), lambda i: (lax.rem(steps - 1 - i, count), 0))
    return pl.pallas_call(
        functools.partial(backward_kernel, heads),
        grid=(steps,),
        in_specs=[
            pl.BlockSpec(memory_space=pltpu.SMEM),
            pl.BlockSpec(memory_space=pltpu.SMEM),
            whole(raw),
            whole(values),
            whole(filters),
            whole(decays),
            part(rows, heads * VALUE),
            whole(gain),
            part_grad,
            part_grad,
            part(rows, heads * VALUE),
            part(rows, heads * GROUP),
            part(rows * heads, VALUE),
            part(rows * heads, VALUE),
            part(SUB * heads * KEY, VALUE),
        ],
        out_specs=[
            part(rows, wide + 2 * heads * VALUE),
            same(8 * CONV, filters.shape[1]),
            same(2, heads),
            same(8, VALUE),
        ],
        out_shape=[
            jax.ShapeDtypeStruct((length, wide + 2 * heads * VALUE), bf16),
            jax.ShapeDtypeStruct((8 * CONV, filters.shape[1]), f32),
            jax.ShapeDtypeStruct((2, heads), f32),
            jax.ShapeDtypeStruct((8, VALUE), f32),
        ],
        scratch_shapes=[
            pltpu.VMEM((heads * KEY, VALUE), f32),
            pltpu.VMEM((8, filters.shape[1]), f32),
        ],
        compiler_params=pltpu.CompilerParams(vmem_limit_bytes=SPACE),
        cost_estimate=pl.CostEstimate(
            flops=length * heads * 14_000_000, bytes_accessed=2**24, transcendentals=0
        ),
        name="mixer_backward",
    )(starts, seq_index(), raw, values, filters, decays, gates, gain, *gated_grads, *kept)


def forward_dot(left_side, right_side):
    return jnp.dot(left_side, right_side, preferred_element_type=f32)


def times_transposed(left_side, right_side):
    return dot(left_side, right_side, 1, 1)


def transposed_times(left_side, right_side):
    return dot(left_side, right_side, 0, 0)


def rms_norm(values, gain):
    return values * lax.rsqrt(jnp.mean(values * values, axis=-1, keepdims=True) + epsilon) * gain


def swiglu(gate_rows, up_rows):
    return jax.nn.silu(gate_rows) * up_rows


def swap_seq(values):
    return lax.ppermute(values, "seq", [(0, 1), (1, 0)])


def in_order(own, other, axis):
    first = lax.axis_index("seq") == 0
    return jnp.where(
        first,
        jnp.concatenate([own, other], axis=axis),
        jnp.concatenate([other, own], axis=axis),
    )


def gather_seq(values, axis):
    if lax.axis_size("seq") == 2:
        return in_order(values, swap_seq(values), axis)
    return lax.all_gather(values, "seq", axis=axis, tiled=True)


def own_part(values, axis, index=None):
    size = values.shape[axis] // lax.axis_size("seq")
    index = lax.axis_index("seq") if index is None else index
    return lax.dynamic_slice_in_dim(values, index * size, size, axis=axis)


def sum_scatter_seq(values, axis):
    if lax.axis_size("seq") == 2:
        other = own_part(values, axis, 1 - lax.axis_index("seq")).astype(bf16)
        return own_part(values, axis) + swap_seq(other).astype(f32)
    return lax.psum_scatter(
        values.astype(bf16), "seq", scatter_dimension=axis, tiled=True
    ).astype(f32)


def own_first(values):
    if lax.axis_size("seq") == 2:
        return jnp.concatenate([values, swap_seq(values)], axis=0)
    return lax.all_gather(values, "seq", axis=0, tiled=True)


def sum_own_first(values):
    if lax.axis_size("seq") == 2:
        half = values.shape[0] // 2
        return values[:half] + swap_seq(values[half:].astype(bf16)).astype(f32)
    return sum_scatter_seq(values, 0)


def exchange_seq(values, split, join):
    if lax.axis_size("seq") == 2:
        other = own_part(values, split, 1 - lax.axis_index("seq"))
        return in_order(own_part(values, split), swap_seq(other), join)
    return lax.all_to_all(values, "seq", split_axis=split, concat_axis=join, tiled=True)


PLACES = 4


def in_grid():
    return lax.axis_size("shard") == 4 * PLACES and lax.axis_size("seq") == 2


def position():
    place = lax.axis_index("shard")
    return place // 4, (place // 2) % 2, place % 2


def flip(values, mask):
    size = lax.axis_size("shard")
    return lax.ppermute(values, "shard", [(i, i ^ mask) for i in range(size)])


def from_place(values, step):
    size = lax.axis_size("shard")
    return lax.ppermute(values, "shard", [(i, (i - 4 * step) % size) for i in range(size)])


def gather_shard(values):
    return lax.all_gather(values, "shard", axis=0, tiled=True)


def scatter_shard(values):
    return lax.psum_scatter(values, "shard", scatter_dimension=0, tiled=True)


def core_major(values):
    if not in_grid():
        return values
    rows, columns = values.shape
    places = values.reshape(rows, PLACES, 2, 2, columns // (4 * PLACES))
    return jnp.transpose(places, (0, 3, 2, 1, 4)).reshape(rows, columns)


def portion(values, index, count):
    size = values.shape[0] // count
    return lax.dynamic_slice_in_dim(values, index * size, size, axis=0)


def sum_pair(values, index, mask):
    sent = flip(portion(values, 1 - index, 2), mask)
    return (portion(values, index, 2).astype(f32) + sent.astype(f32)).astype(bf16)


def sum_along(values):
    z = position()[0]
    total = portion(values, z, PLACES).astype(f32)
    for r in range(1, PLACES):
        sent = from_place(portion(values, (z - r) % PLACES, PLACES), r)
        total = total + sent.astype(f32)
    return total.astype(bf16)


def first_sum(values):
    return sum_pair(values, position()[2], 1) if in_grid() else values


def second_sum(values):
    return sum_pair(values, position()[1], 2) if in_grid() else values


def third_sum(values):
    return sum_along(values) if in_grid() else scatter_shard(values)


def spread_kernel(cuts, seq_ref, own_ref, other_ref, *out_refs):
    def write(first, second):
        for (start, stop), out_ref in zip(cuts, out_refs):
            out_ref[:, : stop - start] = first[:, start:stop].astype(f32)
            out_ref[:, stop - start :] = second[:, start:stop].astype(f32)

    @pl.when(seq_ref[0] == 0)
    def _():
        write(own_ref, other_ref)

    @pl.when(seq_ref[0] != 0)
    def _():
        write(other_ref, own_ref)


def spread(own, other, cuts):
    rows = own.shape[0]
    memory = pl.BlockSpec(memory_space=pltpu.VMEM)
    return pl.pallas_call(
        functools.partial(spread_kernel, cuts),
        in_specs=[pl.BlockSpec(memory_space=pltpu.SMEM), memory, memory],
        out_specs=[memory] * len(cuts),
        out_shape=[jax.ShapeDtypeStruct((rows, 2 * (b - a)), f32) for a, b in cuts],
        compiler_params=pltpu.CompilerParams(vmem_limit_bytes=SPACE // 4),
        cost_estimate=pl.CostEstimate(flops=2**20, bytes_accessed=2**22, transcendentals=0),
        name="spread",
    )(seq_index(), own, other)


def seq_index():
    return jnp.stack([lax.axis_index("seq")]).astype(jnp.int32)


def after(values, *earlier):
    return lax.optimization_barrier((values, earlier))[0]


def sum_small(values, axes):
    if not in_grid():
        return lax.psum(values, axes)
    for mask in (1, 2, 4, 8):
        values = values + flip(values, mask)
    return values


def on_device(
    tokens,
    doc_starts,
    norm_gain,
    query_weight,
    key_weight,
    value_weight,
    gate_weight,
    beta_decay_weight,
    conv_filters,
    decay_params,
    out_norm_gain,
    out_weight,
    ffn_norm_gain,
    ffn_gate_weight,
    ffn_up_weight,
    down_weight,
    out_cotangent,
):
    heads = HEADS // lax.axis_size("seq")
    shards = lax.axis_size("shard")
    rows = query_weight.shape[0]
    width = 2 * heads * KEY
    ff = ffn_gate_weight.shape[1]

    logit_weight = own_part(beta_decay_weight.reshape(rows, HEADS, 2), 1)
    gain_rows = out_norm_gain.shape[0]
    raw_piece = jnp.concatenate(
        [
            own_part(query_weight, 1),
            own_part(key_weight, 1),
            logit_weight[:, :, 0],
            logit_weight[:, :, 1],
            norm_gain[:, None],
            ffn_norm_gain[:, None],
            jnp.pad(out_norm_gain, (0, rows - gain_rows))[:, None],
            jnp.zeros((rows, KEY - 2 * heads - 3), bf16),
        ],
        axis=1,
    )
    units = ff // shards // lax.axis_size("seq")

    def own_units(weight):
        return own_part(weight.reshape(rows, shards, ff // shards), 2).reshape(rows, shards * units)

    raw_wide = raw_piece.shape[1]
    value_end = raw_wide + heads * VALUE
    mixer_full = gather_shard(
        jnp.concatenate([raw_piece, own_part(value_weight, 1), own_part(gate_weight, 1)], axis=1)
    )
    raw_full = mixer_full[:, :raw_wide]
    value_full = mixer_full[:, raw_wide:value_end]
    gate_full = mixer_full[:, value_end:]
    half = shards * units
    model = out_weight.shape[1]
    out_rows = out_weight.shape[0]
    tall_full = gather_shard(jnp.concatenate([out_weight, own_part(down_weight, 0)], axis=0))
    tall_full = tall_full.reshape(shards, out_rows + units, model)
    out_full = tall_full[:, :out_rows].reshape(shards * out_rows, model)
    down_full = tall_full[:, out_rows:].reshape(half, model)
    ffn_full = gather_shard(
        jnp.concatenate([own_units(ffn_gate_weight), own_units(ffn_up_weight)], axis=1)
    )
    first_gain = raw_full[:, width + 2 * heads].astype(f32)
    second_gain = raw_full[:, width + 2 * heads + 1].astype(f32)
    third_gain = (
        raw_full[:, width + 2 * heads + 2]
        .reshape(shards, rows)[:, :gain_rows]
        .reshape(1, shards * gain_rows)
        .astype(f32)
    )

    own_tokens = tokens[0]
    token_count = own_tokens.shape[0]
    inputs = own_tokens.astype(f32)
    cotangent = out_cotangent[0]
    if lax.axis_size("seq") == 2:
        other = swap_seq(jnp.concatenate([own_tokens, cotangent], axis=0))
        all_inputs = in_order(own_tokens, other[:token_count], 0).astype(f32)
        all_cotangent = jnp.concatenate([cotangent, other[token_count:]], axis=0)
    else:
        all_inputs = gather_seq(own_tokens, 0).astype(f32)
        all_cotangent = own_first(cotangent)
    length = all_inputs.shape[0]
    all_scaled = all_inputs * lax.rsqrt(
        jnp.mean(all_inputs * all_inputs, axis=-1, keepdims=True) + epsilon
    )
    normed = (all_scaled * first_gain).astype(bf16)
    raw = forward_dot(normed, raw_full).astype(bf16)
    values = forward_dot(normed, value_full).astype(bf16)
    gate_rows = forward_dot(normed, gate_full)
    filters = jnp.concatenate(
        [
            conv_filters[:, :, :KEY].reshape(CONV, heads * KEY),
            conv_filters[:, :, KEY : 2 * KEY].reshape(CONV, heads * KEY),
            conv_filters[:, :, 2 * KEY :].reshape(CONV, heads * VALUE),
        ],
        axis=1,
    )
    decays = decay_params.T
    gated, *kept = mixer_forward(
        raw, values, filters, decays, doc_starts, gate_rows, third_gain, heads
    )
    gated_low = exchange_seq(gated, 0, 1)
    gated_low, down_full = lax.optimization_barrier((gated_low, down_full))
    middle = inputs + forward_dot(gated_low, out_full)
    second_norm, second_pull = jax.vjp(rms_norm, middle, second_gain)
    hidden = own_first(second_norm.astype(bf16))
    both_ffn = forward_dot(hidden, ffn_full)
    activated, swiglu_pull = jax.vjp(swiglu, both_ffn[:, :half], both_ffn[:, half:])
    activated_low = activated.astype(bf16)
    act_grad = times_transposed(all_cotangent, down_full)
    both_grad = jnp.concatenate([g.astype(bf16) for g in swiglu_pull(act_grad)], axis=1)
    hidden_grad = sum_own_first(times_transposed(both_grad, ffn_full))
    out_parts = forward_dot(activated_low, down_full)
    down_grad = transposed_times(activated_low, all_cotangent).astype(bf16)
    ffn_grad = transposed_times(core_major(after(hidden, both_ffn)), both_grad).astype(bf16)
    ffn_grad = first_sum(ffn_grad)
    out_sent = out_parts[token_count:].astype(bf16)
    hidden_grad, ffn_grad, down_grad, out_parts, out_sent = lax.optimization_barrier(
        (hidden_grad, ffn_grad, down_grad, out_parts, out_sent)
    )
    middle_part, ffn_gain_grad = second_pull(hidden_grad)
    middle_grad = cotangent.astype(f32) + middle_part
    branch_low = middle_grad.astype(bf16)
    out_grad = transposed_times(gated_low, branch_low).astype(bf16)
    gated_grad = times_transposed(branch_low, out_full).astype(bf16)
    if lax.axis_size("seq") == 2:
        other_grad = swap_seq(own_part(gated_grad, 1, 1 - lax.axis_index("seq")))
        own_grad = own_part(gated_grad, 1)
    else:
        own_grad = other_grad = exchange_seq(gated_grad, 1, 0)
    ffn_grad = second_sum(ffn_grad)
    tall_grad = jnp.concatenate(
        [out_grad.reshape(shards, out_rows, model), down_grad.reshape(shards, units, model)], axis=1
    ).reshape(shards * (out_rows + units), model)
    own_grad, other_grad, ffn_grad, tall_grad = lax.optimization_barrier(
        (own_grad, other_grad, ffn_grad, tall_grad)
    )
    ffn_share = third_sum(ffn_grad)
    tall_share = scatter_shard(tall_grad)
    if lax.axis_size("seq") == 2:
        out_parts = out_parts[:token_count] + swap_seq(after(out_sent, other_grad)).astype(f32)
    else:
        out_parts = sum_own_first(out_parts)
    block_out = (middle + out_parts).astype(bf16)
    mixer_grad, filters_grad, decays_grad, out_gain_grad = mixer_backward(
        raw,
        values,
        filters,
        decays,
        doc_starts,
        gate_rows,
        third_gain,
        (own_grad, other_grad),
        kept,
        heads,
    )
    mixer_grad, ffn_share, block_out = lax.optimization_barrier((mixer_grad, ffn_share, block_out))
    mixer_weight_grad = transposed_times(normed, mixer_grad).astype(bf16)
    mixer_grad, mixer_weight_grad = lax.optimization_barrier((mixer_grad, mixer_weight_grad))
    mixer_share = scatter_shard(mixer_weight_grad)
    normed_grad = times_transposed(mixer_grad, mixer_full)
    norm_gain_grad = jnp.sum(normed_grad * all_scaled, axis=0)
    if lax.axis_size("seq") == 2:
        sent = own_part(normed_grad, 0, 1 - lax.axis_index("seq")).astype(bf16)
        own_normed_grad = own_part(normed_grad, 0) + swap_seq(sent).astype(f32)
    else:
        sent = normed_grad
        own_normed_grad = sum_scatter_seq(normed_grad, 0)
    _, first_pull = jax.vjp(lambda v: rms_norm(v, first_gain), inputs)
    tokens_grad = middle_grad + first_pull(own_normed_grad)[0]

    def all_units(share):
        share = gather_seq(share.reshape(rows, shards, units), 2)
        return share.reshape(rows, ff).astype(f32)

    ffn_gate_share = all_units(ffn_share[:, :half])
    ffn_up_share = all_units(ffn_share[:, half:])
    tall_share = gather_seq(after(tall_share, mixer_grad)[None], 0).astype(f32)
    out_share = jnp.sum(tall_share[:, :out_rows], axis=0)
    down_share = tall_share[:, out_rows:].reshape(-1, model)
    if lax.axis_size("seq") == 2:
        other_share = swap_seq(mixer_share)

        def side_by_side(start, stop):
            own, other = mixer_share[:, start:stop], other_share[:, start:stop]
            return in_order(own.astype(f32), other.astype(f32), 1)
    else:
        every = gather_seq(mixer_share[None], 0)

        def side_by_side(start, stop):
            part = jnp.swapaxes(every[:, :, start:stop], 0, 1)
            return part.reshape(rows, -1).astype(f32)

    cuts = (
        (0, heads * KEY),
        (heads * KEY, width),
        (raw_wide, value_end),
        (value_end, mixer_share.shape[1]),
    )
    if lax.axis_size("seq") == 2:
        shares = spread(mixer_share, other_share, cuts)
    else:
        shares = [side_by_side(start, stop) for start, stop in cuts]
    query_share, key_share, value_share, gate_share = shares
    logit_share = side_by_side(width, width + 2 * heads).reshape(rows, -1, 2, heads)
    logit_share = jnp.swapaxes(logit_share, 2, 3).reshape(rows, 2 * HEADS)

    all_width = filters.shape[1]
    filters_grad = jnp.sum(filters_grad.reshape(CONV, 8, all_width), axis=1)
    lengths = [shards * n for n in (norm_gain.shape[0], gain_rows, ffn_norm_gain.shape[0])]
    small = jnp.concatenate(
        [
            filters_grad.reshape(CONV * all_width),
            decays_grad.reshape(2 * heads),
            norm_gain_grad,
            jnp.sum(out_gain_grad, axis=0),
            ffn_gain_grad,
        ]
    )
    small = sum_small(after(small, sent), ("shard",))
    head_end = CONV * all_width + 2 * heads
    filters_grad = small[: CONV * all_width].reshape(CONV, all_width)
    decays_grad = small[CONV * all_width : head_end].reshape(2, heads)
    gains = small[head_end:]
    gains = gains + swap_seq(gains) if in_grid() else lax.psum(gains, "seq")
    split = (heads * KEY, 2 * heads * KEY)
    filters_out = jnp.concatenate(
        [
            filters_grad[:, : split[0]].reshape(CONV, heads, KEY),
            filters_grad[:, split[0] : split[1]].reshape(CONV, heads, KEY),
            filters_grad[:, split[1] :].reshape(CONV, heads, VALUE),
        ],
        axis=2,
    )
    gains = [
        gains[: lengths[0]],
        gains[lengths[0] : lengths[0] + lengths[1]],
        gains[lengths[0] + lengths[1] :],
    ]
    place = lax.axis_index("shard")
    gains = [
        lax.dynamic_slice_in_dim(g, place * (g.shape[0] // shards), g.shape[0] // shards)
        for g in gains
    ]
    return (
        block_out[None],
        tokens_grad[None],
        gains[0],
        query_share,
        key_share,
        value_share,
        gate_share,
        logit_share,
        filters_out,
        decays_grad.T,
        gains[1],
        out_share,
        gains[2],
        ffn_gate_share,
        ffn_up_share,
        down_share,
    )


def solution(mesh):
    in_specs = (
        P("shard", "seq", None),
        P("shard", None),
        P("shard"),
        P("shard", None),
        P("shard", None),
        P("shard", None),
        P("shard", None),
        P("shard", None),
        P(None, "seq", None),
        P("seq", None),
        P("shard"),
        P("shard", None),
        P("shard"),
        P("shard", None),
        P("shard", None),
        P("shard", None),
        P("shard", "seq", None),
    )
    out_specs = (
        P("shard", "seq", None),
        P("shard", "seq", None),
        P("shard"),
        P("shard", None),
        P("shard", None),
        P("shard", None),
        P("shard", None),
        P("shard", None),
        P(None, "seq", None),
        P("seq", None),
        P("shard"),
        P("shard", None),
        P("shard"),
        P("shard", None),
        P("shard", None),
        P("shard", None),
    )
    return jax.shard_map(
        on_device, mesh=mesh, in_specs=in_specs, out_specs=out_specs, check_vma=False
    )
```

```python
import functools

import jax
import jax.numpy as jnp
from jax import lax
from jax.experimental import pallas as pl
from jax.experimental.pallas import tpu as pltpu
from jax.sharding import PartitionSpec as P

HEADS = 8
KEY = 128
VALUE = 256
CONV = 4
GROUP = 64
HALO = 16
SUB = 4
epsilon = 1e-06
f32 = jnp.float32
bf16 = jnp.bfloat16


def dot(a, b, ca=1, cb=0):
    return lax.dot_general(a, b, (((ca,), (cb,)), ((), ())), preferred_element_type=f32)


def halves(values):
    high = values.astype(bf16)
    return high, (values - high.astype(f32)).astype(bf16)


def fine_dot(a, b, ca=1, cb=0):
    if not isinstance(a, tuple):
        return dot(a, b[0], ca, cb) + dot(a, b[1], ca, cb)
    if not isinstance(b, tuple):
        return dot(a[0], b, ca, cb) + dot(a[1], b, ca, cb)
    return dot(a[0], b[0], ca, cb) + (dot(a[0], b[1], ca, cb) + dot(a[1], b[0], ca, cb))


def iota(shape, dim):
    return lax.broadcasted_iota(jnp.int32, shape, dim)


def doc_count(starts_ref, times):
    count = jnp.zeros(times.shape, jnp.int32)
    for s in range(starts_ref.shape[1]):
        count = count + jnp.where(times >= starts_ref[0, s], 1, 0)
    return count


def scalar_doc(starts_ref, time):
    count = 0
    for s in range(starts_ref.shape[1]):
        count = count + (time >= starts_ref[0, s]).astype(jnp.int32)
    return count


def per_head(cols, heads, width):
    rows = cols.shape[0]
    lane = iota((rows, heads * width), 1)
    out = jnp.broadcast_to(cols[:, heads - 1 : heads], (rows, heads * width))
    for h in range(heads - 2, -1, -1):
        out = jnp.where(lane < (h + 1) * width, cols[:, h : h + 1], out)
    return out


def head_sums(panel, heads, width):
    lane = iota(panel.shape, 1)
    sums = []
    for h in range(heads):
        inside = (lane >= h * width) & (lane < (h + 1) * width)
        sums.append(jnp.sum(jnp.where(inside, panel, 0.0), axis=1, keepdims=True))
    return columns(sums)


def across(mask, width):
    return jnp.concatenate([mask] * (width // KEY), axis=1)


def columns(parts):
    rows = parts[0].shape[0]
    lane = iota((rows, len(parts)), 1)
    out = jnp.broadcast_to(parts[-1], (rows, len(parts)))
    for h in range(len(parts) - 2, -1, -1):
        out = jnp.where(lane == h, parts[h], out)
    return out


def block_diagonal(panel, heads):
    if heads == 1:
        return panel
    lane = iota(panel.shape, 1)
    zero = jnp.zeros_like(panel)
    parts = []
    for h in range(heads):
        inside = (lane >= h * GROUP) & (lane < (h + 1) * GROUP)
        parts.append(jnp.where(inside, panel, zero))
    return jnp.concatenate(parts, axis=0)


def diagonal_panel(full, heads):
    if heads == 1:
        return full
    lane = iota((GROUP, heads * GROUP), 1)
    out = full[(heads - 1) * GROUP :]
    for h in range(heads - 2, -1, -1):
        out = jnp.where(lane < (h + 1) * GROUP, full[h * GROUP : (h + 1) * GROUP], out)
    return out


def key_diagonal(keys):
    heads = len(keys)
    if heads == 1:
        return keys[0]
    zero = jnp.zeros_like(keys[0])
    rows = []
    for h in range(heads):
        rows.append(jnp.concatenate([keys[h] if o == h else zero for o in range(heads)], axis=1))
    return jnp.concatenate(rows, axis=0)


def scan_rows(values, reverse=False):
    rows = values.shape[0]
    index = iota(values.shape, 0)
    step = 1
    while step < rows:
        if reverse:
            moved = pltpu.roll(values, rows - step, 0)
            values = values + jnp.where(index < rows - step, moved, 0.0)
        else:
            moved = pltpu.roll(values, step, 0)
            values = values + jnp.where(index >= step, moved, 0.0)
        step *= 2
    return values


def sigmoid(v):
    return 1.0 / (1.0 + jnp.exp(-v))


def softplus(v):
    return jnp.maximum(v, 0.0) + jnp.log(1.0 + jnp.exp(-jnp.abs(v)))


def in_turn(generators):
    generators = list(generators)
    while generators:
        still = []
        for generator in generators:
            if next(generator, True) is None:
                still.append(generator)
        generators = still


class Block:
    def __init__(self, heads, base, raw_ref, value_ref, filters_ref, decay_ref, starts_ref):
        self.heads = heads
        self.base = base
        self.raw_ref = raw_ref
        self.value_ref = value_ref
        self.filters_ref = filters_ref
        self.decay_ref = decay_ref
        self.starts_ref = starts_ref

    def build(self):
        heads, base, starts_ref = self.heads, self.base, self.starts_ref
        raw_ref, decay_ref = self.raw_ref, self.decay_ref
        width = 2 * heads * KEY
        times = base + iota((GROUP, 1), 0)
        docs = doc_count(starts_ref, times)
        wide = (GROUP, KEY)
        self.masks, self.next_masks = [], []
        for o in range(1, CONV):
            same = (docs == doc_count(starts_ref, times - o)).astype(f32)
            self.masks.append(jnp.broadcast_to(same, wide))
            same = (docs == doc_count(starts_ref, times + o)).astype(f32)
            self.next_masks.append(jnp.broadcast_to(same, wide))
        self.query, self.keys, self.query_pre, self.key_pre = [], [], [], []
        self.query_conv, self.key_conv, self.query_scale, self.key_scale = [], [], [], []
        for h in range(heads):
            pre = self.convolve(h * KEY, KEY)
            conv = pre * sigmoid(pre)
            scale = lax.rsqrt(jnp.sum(conv * conv, axis=1, keepdims=True) + epsilon)
            self.query_pre.append(pre)
            self.query_conv.append(conv)
            self.query_scale.append(scale)
            self.query.append(conv * scale * KEY ** (-0.5))
        for h in range(heads):
            pre = self.convolve((heads + h) * KEY, KEY)
            conv = pre * sigmoid(pre)
            scale = lax.rsqrt(jnp.sum(conv * conv, axis=1, keepdims=True) + epsilon)
            self.key_pre.append(pre)
            self.key_conv.append(conv)
            self.key_scale.append(scale)
            self.keys.append(conv * scale)
        yield
        logits = raw_ref[pl.ds(base, GROUP), width : width + KEY].astype(f32)
        self.strength = sigmoid(logits[:, :heads])
        self.decay_logit = logits[:, heads : 2 * heads] + decay_ref[1:2, :heads]
        self.decay_rate = -jnp.exp(decay_ref[0:1, :heads])
        self.log_decay = self.decay_rate * softplus(self.decay_logit)
        yield
        sums = scan_rows(self.log_decay)
        yield
        self.sums = sums
        last = sums[GROUP - 1 : GROUP]
        before = scalar_doc(starts_ref, base - 1)
        final = scalar_doc(starts_ref, base + GROUP - 1)
        self.entering = jnp.where(docs == before, jnp.exp(sums), 0.0)
        same_last = docs == final
        self.leaving = jnp.where(same_last, jnp.exp(jnp.where(same_last, last - sums, 0.0)), 0.0)
        self.retain = self.entering[GROUP - 1 : GROUP]
        yield
        shape = (GROUP, heads * GROUP)
        row = iota(shape, 0)
        place = jnp.bitwise_and(iota(shape, 1), GROUP - 1)
        self.row, self.place = row, place
        across = jnp.bitwise_and(iota((1, heads * GROUP), 1), GROUP - 1)
        docs_across = doc_count(starts_ref, base + across)
        same = docs == docs_across
        self.inclusive = same & (row >= place)
        self.strict = same & (row > place)
        sums_down = per_head(sums, heads, GROUP)
        sums_across = jnp.sum(jnp.where(row == place, sums_down, 0.0), axis=0, keepdims=True)
        gap = jnp.where(self.inclusive, sums_down - sums_across, 0.0)
        self.fade = jnp.where(self.inclusive, jnp.exp(gap), 0.0)
        yield
        self.strength_down = per_head(self.strength, heads, GROUP)
        low_keys = [k.astype(bf16) for k in self.keys]
        low_query = [q.astype(bf16) for q in self.query]
        self.keys = [k.astype(f32) for k in low_keys]
        self.query = [q.astype(f32) for q in low_query]
        self.low_keys, self.low_query = low_keys, low_query
        self.key_diag = key_diagonal(low_keys)
        left = jnp.concatenate(
            [jnp.concatenate(low_keys, axis=1), jnp.concatenate(low_query, axis=1)], axis=0
        )
        self.query_key_rows = left
        grams = dot(left, self.key_diag, 1, 1)
        yield
        self.key_gram = grams[:GROUP]
        self.score_gram = grams[GROUP:]
        self.system = jnp.where(self.strict, self.strength_down * self.key_gram * self.fade, 0.0)
        self.scores = self.score_gram * self.fade

    def taps(self, start, width):
        source = self.raw_ref
        if start >= 2 * self.heads * KEY:
            source = self.value_ref
            start = start - 2 * self.heads * KEY
        current = source[pl.ds(self.base, GROUP), start : start + width].astype(f32)
        earlier = pl.multiple_of(jnp.maximum(self.base - HALO, 0), HALO)
        halo = source[pl.ds(earlier, HALO), start : start + width].astype(f32)
        extended = jnp.concatenate([halo, current], axis=0)
        return [current] + [
            pltpu.roll(extended, o, 0)[HALO:] * across(self.masks[o - 1], width)
            for o in range(1, CONV)
        ]

    def convolve(self, start, width):
        taps = self.taps(start, width)
        filters = self.filters_ref[:, start : start + width]
        total = taps[0] * filters[CONV - 1 : CONV]
        for o in range(1, CONV):
            total = total + taps[o] * filters[CONV - 1 - o : CONV - o]
        return total


def inverse(systems, heads, row, place):
    eye = (row == place).astype(f32)
    apart = jnp.bitwise_xor(row, place)

    def part(system, size):
        return jnp.where((apart >= size) & (apart < 2 * size), system, 0.0)

    results = [eye - part(system, 1) for system in systems]
    size = 2
    while size < GROUP:
        low = [result.astype(bf16) for result in results]
        inner = [
            dot(part(system, size).astype(bf16), block_diagonal(one, heads))
            for system, one in zip(systems, low)
        ]
        inner = [block_diagonal(one.astype(bf16), heads) for one in inner]
        results = [
            result - dot(one, right) for result, one, right in zip(results, low, inner)
        ]
        size *= 2
    return results


def forward_kernel(
    heads, starts_ref, raw_ref, value_ref, filters_ref, decay_ref, gate_ref, gain_ref,
    gated_ref, mixed_ref, inverse_ref, delta_ref, rest_ref, memory_ref, state,
):
    step = pl.program_id(0)

    @pl.when(step == 0)
    def _():
        state[...] = jnp.zeros_like(state)

    blocks = []
    for s in range(SUB):
        base = pl.multiple_of((step * SUB + s) * GROUP, GROUP)
        blocks.append(Block(heads, base, raw_ref, value_ref, filters_ref, decay_ref, starts_ref))
    in_turn(block.build() for block in blocks)
    solves = inverse([block.system for block in blocks], heads, blocks[0].row, blocks[0].place)
    for s, block in enumerate(blocks):
        block.values = []
        for h in range(heads):
            pre = block.convolve(2 * heads * KEY + h * VALUE, VALUE)
            block.values.append(pre * sigmoid(pre))
        block.solve = solves[s]
        inverse_ref[s * GROUP : (s + 1) * GROUP] = block.solve.astype(bf16)
    for s, block in enumerate(blocks):
        from_state, rest, right = [], [], []
        for h in range(heads):
            entering = block.entering[:, h : h + 1]
            memory = state[h * KEY : (h + 1) * KEY].astype(bf16)
            memory_ref[(s * heads + h) * KEY : (s * heads + h + 1) * KEY] = memory
            both = jnp.concatenate([block.low_keys[h], block.low_query[h]], axis=0)
            read = dot(both, memory)
            from_state.append(entering * read[GROUP:])
            missing = block.values[h] - entering * read[:GROUP]
            rest.append(missing.astype(bf16))
            right.append(block.strength[:, h : h + 1] * missing)
        rest_ref[s * heads * GROUP : (s + 1) * heads * GROUP] = jnp.concatenate(rest, axis=0)
        solve = tuple(block_diagonal(p, heads) for p in halves(block.solve))
        delta = fine_dot(solve, halves(jnp.concatenate(right, axis=0)))
        delta_ref[s * heads * GROUP : (s + 1) * heads * GROUP] = delta
        scores = tuple(block_diagonal(p, heads) for p in halves(block.scores))
        outputs = fine_dot(scores, halves(delta))
        for h in range(heads):
            rows = slice(h * GROUP, (h + 1) * GROUP)
            out = from_state[h] + outputs[rows]
            here = slice(s * GROUP, (s + 1) * GROUP)
            lanes = slice(h * VALUE, (h + 1) * VALUE)
            low = out.astype(bf16)
            mixed_ref[here, lanes] = low
            low = low.astype(f32)
            gate = gate_ref[here, lanes]
            scale = lax.rsqrt(jnp.mean(low * low, axis=1, keepdims=True) + epsilon)
            gated = low * scale * gain_ref[0:1] * (gate * sigmoid(gate))
            gated_ref[here, lanes] = gated.astype(bf16)
            leaving = halves(block.leaving[:, h : h + 1] * delta[rows])
            keep = block.retain[:, h : h + 1]
            own = slice(h * KEY, (h + 1) * KEY)
            state[own] = keep * state[own] + fine_dot(block.low_keys[h], leaving, 0, 0)


def silu_slope(pre):
    gate = sigmoid(pre)
    return gate * (1.0 + pre * (1.0 - gate))


def backward_kernel(
    heads, starts_ref, seq_ref, raw_ref, value_ref, filters_ref, decay_ref, gate_ref, gain_ref,
    own_grad_ref, other_grad_ref, mixed_ref, inverse_ref, delta_ref, rest_ref, memory_ref,
    raw_grad_ref, filters_grad_ref, decay_grad_ref, gain_grad_ref,
    state, halo,
):
    step = pl.program_id(0)
    steps = pl.num_programs(0)
    width = 2 * heads * KEY
    own_rows = (2 * (steps - 1 - step) >= steps) == (seq_ref[0] != 0)

    @pl.when(step == 0)
    def _():
        state[...] = jnp.zeros_like(state)
        gain_grad_ref[...] = jnp.zeros_like(gain_grad_ref)
        halo[...] = jnp.zeros_like(halo)
        filters_grad_ref[...] = jnp.zeros_like(filters_grad_ref)
        decay_grad_ref[...] = jnp.zeros_like(decay_grad_ref)

    def pull(s):
        base = pl.multiple_of(((steps - 1 - step) * SUB + s) * GROUP, GROUP)
        block = Block(heads, base, raw_ref, value_ref, filters_ref, decay_ref, starts_ref)
        yield from block.build()
        yield
        here = slice(s * GROUP, (s + 1) * GROUP)
        stacked = slice(s * heads * GROUP, (s + 1) * heads * GROUP)
        solve = inverse_ref[here]
        delta = delta_ref[stacked]
        rest = rest_ref[stacked]
        mixed_grads = []
        for h in range(heads):
            lanes = slice(h * VALUE, (h + 1) * VALUE)
            grad = jnp.where(
                own_rows,
                own_grad_ref[here, lanes].astype(f32),
                other_grad_ref[here, lanes].astype(f32),
            )
            mixed = mixed_ref[here, lanes].astype(f32)
            gate = gate_ref[here, lanes]
            scale = lax.rsqrt(jnp.mean(mixed * mixed, axis=1, keepdims=True) + epsilon)
            unit = mixed * scale
            open_gate = sigmoid(gate)
            swish = gate * open_gate
            along = grad * unit
            product = (along * swish).reshape(GROUP // 8, 8, VALUE)
            gain_grad_ref[...] = gain_grad_ref[...] + jnp.sum(product, axis=0)
            gate_grad = along * gain_ref[0:1] * (open_gate * (1.0 + gate * (1.0 - open_gate)))
            behind = width + KEY + (heads + h) * VALUE
            raw_grad_ref[here, behind : behind + VALUE] = gate_grad.astype(bf16)
            unit_grad = grad * swish * gain_ref[0:1]
            inner = jnp.mean(unit_grad * unit, axis=1, keepdims=True)
            mixed_grads.append((scale * (unit_grad - unit * inner)).astype(bf16))
        out_grad = jnp.concatenate(mixed_grads, axis=0)
        yield
        scores = tuple(block_diagonal(p, heads) for p in halves(block.scores))
        from_scores = fine_dot(scores, out_grad, 0, 0)
        delta = halves(delta)
        score_part = diagonal_panel(sum(dot(out_grad, d, 1, 1) for d in delta), heads)
        scores_grad = jnp.where(block.inclusive, score_part, 0.0)
        score_gram_grad = scores_grad * block.fade
        solve = block_diagonal(solve, heads)
        yield "chain"
        later = [state[h * KEY : (h + 1) * KEY] for h in range(heads)]
        later_low = [m.astype(bf16) for m in later]
        pulled = jnp.concatenate(
            [
                block.leaving[:, h : h + 1] * dot(block.low_keys[h], later_low[h])
                for h in range(heads)
            ],
            axis=0,
        )
        delta_grad = pulled + from_scores
        right_grad = dot(solve, delta_grad.astype(bf16), 0, 0)
        rest_grad, pairs = [], []
        for h in range(heads):
            rows = slice(h * GROUP, (h + 1) * GROUP)
            rest_grad.append(block.strength[:, h : h + 1] * right_grad[rows])
            pairs.append(jnp.concatenate([out_grad[rows], rest_grad[h].astype(bf16)], axis=0))
            entering = block.entering[:, h : h + 1]
            left = jnp.concatenate(
                [entering * block.query[h], -entering * block.keys[h]], axis=0
            ).astype(bf16)
            state[h * KEY : (h + 1) * KEY] = (
                block.retain[:, h : h + 1] * later[h] + dot(left, pairs[h], 0, 0)
            )
        yield "chain"
        entering_query_grad, entering_key_grad, leaving_key_grad, retain_grad = [], [], [], []
        strength_grad = []
        for h in range(heads):
            rows = slice(h * GROUP, (h + 1) * GROUP)
            strength_grad.append(
                jnp.sum(right_grad[rows] * rest[rows].astype(f32), axis=1, keepdims=True)
            )
            memory = memory_ref[(s * heads + h) * KEY : (s * heads + h + 1) * KEY]
            back = dot(pairs[h], memory, 1, 1)
            entering_query_grad.append(back[:GROUP])
            entering_key_grad.append(-back[GROUP:])
            leaving_key_grad.append(sum(dot(d[rows], later_low[h], 1, 1) for d in delta))
            product = later[h] * memory.astype(f32)
            retain_grad.append(
                jnp.sum(jnp.sum(product, axis=0, keepdims=True), axis=1, keepdims=True)
            )
        yield
        right_low = right_grad.astype(bf16)
        system_part = diagonal_panel(sum(dot(right_low, d, 1, 1) for d in delta), heads)
        system_grad = jnp.where(block.strict, -system_part, 0.0)
        faded = system_grad * block.fade
        key_gram_grad = block.strength_down * faded
        gap_grad = score_gram_grad * block.score_gram + key_gram_grad * block.key_gram
        yield
        strength_panel = head_sums(faded * block.key_gram, heads, GROUP)
        down = jnp.sum(gap_grad, axis=0, keepdims=True)
        gap_rows = head_sums(
            gap_grad - jnp.where(block.row == block.place, down, 0.0), heads, GROUP
        )
        yield
        both_low = jnp.concatenate([key_gram_grad, score_gram_grad], axis=0).astype(bf16)
        straight = dot(both_low, block.key_diag)
        turned = dot(both_low, block.query_key_rows, 0, 0)
        yield
        entering_grad, leaving_grad = [], []
        for h in range(heads):
            lanes = slice(h * KEY, (h + 1) * KEY)
            entering = block.entering[:, h : h + 1]
            fading = block.leaving[:, h : h + 1]
            query_grad = entering * entering_query_grad[h] + straight[GROUP:, lanes]
            key_grad = (
                turned[h * GROUP : (h + 1) * GROUP, lanes]
                + straight[:GROUP, lanes]
                + fading * leaving_key_grad[h]
                + entering * entering_key_grad[h]
            )
            entering_grad.append(
                jnp.sum(
                    entering_query_grad[h] * block.query[h] + entering_key_grad[h] * block.keys[h],
                    axis=1,
                    keepdims=True,
                )
            )
            leaving_grad.append(
                jnp.sum(leaving_key_grad[h] * block.keys[h], axis=1, keepdims=True)
            )
            for start, grad, conv, scale, pre, factor in (
                (h * KEY, query_grad, block.query_conv[h], block.query_scale[h],
                 block.query_pre[h], KEY ** (-0.5)),
                ((heads + h) * KEY, key_grad, block.key_conv[h], block.key_scale[h],
                 block.key_pre[h], 1.0),
            ):
                along = jnp.sum(grad * conv, axis=1, keepdims=True)
                conv_grad = (factor * scale) * (grad - conv * (scale * scale * along))
                convolve_back(
                    block, s, start, start, KEY, conv_grad * silu_slope(pre), starts_ref,
                    raw_grad_ref, filters_grad_ref, halo,
                )
            yield
            start = 2 * heads * KEY + h * VALUE
            pre = block.convolve(start, VALUE)
            convolve_back(
                block, s, start, start + KEY, VALUE, rest_grad[h] * silu_slope(pre), starts_ref,
                raw_grad_ref, filters_grad_ref, halo,
            )
        yield
        entering_grad = columns(entering_grad) * block.entering
        leaving_grad = columns(leaving_grad) * block.leaving
        strength_grad = columns(strength_grad) + strength_panel
        retain_grad = columns(retain_grad) * block.retain
        at_last = jnp.sum(leaving_grad, axis=0, keepdims=True) + retain_grad
        index = iota((GROUP, heads), 0)
        sums_grad = (
            entering_grad - leaving_grad + gap_rows + jnp.where(index == GROUP - 1, at_last, 0.0)
        )
        log_decay_grad = scan_rows(sums_grad, reverse=True)
        yield
        logit_grad = log_decay_grad * block.decay_rate * sigmoid(block.decay_logit)
        beta_grad = strength_grad * block.strength * (1.0 - block.strength)
        lane = iota((GROUP, KEY), 1)
        packed = jnp.zeros((GROUP, KEY), f32)
        for h in range(heads):
            packed = jnp.where(lane == h, beta_grad[:, h : h + 1], packed)
            packed = jnp.where(lane == heads + h, logit_grad[:, h : h + 1], packed)
        raw_grad_ref[here, width : width + KEY] = packed.astype(bf16)
        scale_sum = jnp.sum(log_decay_grad * block.log_decay, axis=0, keepdims=True)
        bias_sum = jnp.sum(logit_grad, axis=0, keepdims=True)
        decay_grad_ref[0:1] = decay_grad_ref[0:1] + scale_sum
        decay_grad_ref[1:2] = decay_grad_ref[1:2] + bias_sum

    pulls = [pull(s) for s in range(SUB - 1, -1, -1)]
    waiting = list(pulls)
    while waiting:
        waiting = [p for p in waiting if next(p) is None]
    for p in pulls:
        next(p)
    in_turn(pulls)


def convolve_back(
    block, s, start, place, width, pre_grad, starts_ref, grad_ref, filters_grad_ref, halo
):
    lanes = slice(start, start + width)
    taps = block.taps(start, width)
    for o in range(CONV):
        j = CONV - 1 - o
        product = (pre_grad * taps[o]).reshape(GROUP // 8, 8, width)
        filters_grad_ref[j * 8 : (j + 1) * 8, lanes] = filters_grad_ref[
            j * 8 : (j + 1) * 8, lanes
        ] + jnp.sum(product, axis=0)
    filters = block.filters_ref[:, lanes]
    extended = jnp.concatenate([pre_grad, halo[:, lanes]], axis=0)
    rows = GROUP + 8
    total = pre_grad * filters[CONV - 1 : CONV]
    for o in range(1, CONV):
        moved = pltpu.roll(extended, rows - o, 0)[:GROUP] * across(block.next_masks[o - 1], width)
        total = total + moved * filters[CONV - 1 - o : CONV - o]
    grad_ref[s * GROUP : (s + 1) * GROUP, place : place + width] = total.astype(bf16)
    halo[:, lanes] = pre_grad[:8]


SPACE = 56 * 2**20


def mixer_forward(raw, values, filters, decays, starts, gates, gain, heads):
    length, wide = raw.shape
    steps = length // (SUB * GROUP)
    rows = SUB * GROUP
    blocks = length // GROUP
    whole = lambda a: pl.BlockSpec(a.shape, lambda i: (0, 0))
    part = lambda r, c: pl.BlockSpec((r, c), lambda i: (i, 0))
    return pl.pallas_call(
        functools.partial(forward_kernel, heads),
        grid=(steps,),
        in_specs=[
            pl.BlockSpec(memory_space=pltpu.SMEM),
            whole(raw),
            whole(values),
            whole(filters),
            whole(decays),
            part(rows, heads * VALUE),
            whole(gain),
        ],
        out_specs=[
            part(rows, heads * VALUE),
            part(rows, heads * VALUE),
            part(rows, heads * GROUP),
            part(rows * heads, VALUE),
            part(rows * heads, VALUE),
            part(SUB * heads * KEY, VALUE),
        ],
        out_shape=[
            jax.ShapeDtypeStruct((length, heads * VALUE), bf16),
            jax.ShapeDtypeStruct((length, heads * VALUE), bf16),
            jax.ShapeDtypeStruct((length, heads * GROUP), bf16),
            jax.ShapeDtypeStruct((length * heads, VALUE), f32),
            jax.ShapeDtypeStruct((length * heads, VALUE), bf16),
            jax.ShapeDtypeStruct((blocks * heads * KEY, VALUE), bf16),
        ],
        scratch_shapes=[pltpu.VMEM((heads * KEY, VALUE), f32)],
        compiler_params=pltpu.CompilerParams(vmem_limit_bytes=SPACE),
        cost_estimate=pl.CostEstimate(
            flops=length * heads * 11_000_000, bytes_accessed=2**24, transcendentals=0
        ),
        name="mixer_forward",
    )(starts, raw, values, filters, decays, gates, gain)


def mixer_backward(raw, values, filters, decays, starts, gates, gain, gated_grads, kept, heads):
    length, wide = raw.shape
    steps = length // (SUB * GROUP)
    rows = SUB * GROUP
    whole = lambda a: pl.BlockSpec(a.shape, lambda i: (0, 0))
    same = lambda r, c: pl.BlockSpec((r, c), lambda i: (0, 0))
    part = lambda r, c: pl.BlockSpec((r, c), lambda i: (steps - 1 - i, 0))
    count = gated_grads[0].shape[0] // rows
    part_grad = pl.BlockSpec((rows, heads * VALUE), lambda i: (lax.rem(steps - 1 - i, count), 0))
    return pl.pallas_call(
        functools.partial(backward_kernel, heads),
        grid=(steps,),
        in_specs=[
            pl.BlockSpec(memory_space=pltpu.SMEM),
            pl.BlockSpec(memory_space=pltpu.SMEM),
            whole(raw),
            whole(values),
            whole(filters),
            whole(decays),
            part(rows, heads * VALUE),
            whole(gain),
            part_grad,
            part_grad,
            part(rows, heads * VALUE),
            part(rows, heads * GROUP),
            part(rows * heads, VALUE),
            part(rows * heads, VALUE),
            part(SUB * heads * KEY, VALUE),
        ],
        out_specs=[
            part(rows, wide + 2 * heads * VALUE),
            same(8 * CONV, filters.shape[1]),
            same(2, heads),
            same(8, VALUE),
        ],
        out_shape=[
            jax.ShapeDtypeStruct((length, wide + 2 * heads * VALUE), bf16),
            jax.ShapeDtypeStruct((8 * CONV, filters.shape[1]), f32),
            jax.ShapeDtypeStruct((2, heads), f32),
            jax.ShapeDtypeStruct((8, VALUE), f32),
        ],
        scratch_shapes=[
            pltpu.VMEM((heads * KEY, VALUE), f32),
            pltpu.VMEM((8, filters.shape[1]), f32),
        ],
        compiler_params=pltpu.CompilerParams(vmem_limit_bytes=SPACE),
        cost_estimate=pl.CostEstimate(
            flops=length * heads * 14_000_000, bytes_accessed=2**24, transcendentals=0
        ),
        name="mixer_backward",
    )(starts, seq_index(), raw, values, filters, decays, gates, gain, *gated_grads, *kept)


def forward_dot(left_side, right_side):
    return jnp.dot(left_side, right_side, preferred_element_type=f32)


def times_transposed(left_side, right_side):
    return dot(left_side, right_side, 1, 1)


def transposed_times(left_side, right_side):
    return dot(left_side, right_side, 0, 0)


def rms_norm(values, gain):
    return values * lax.rsqrt(jnp.mean(values * values, axis=-1, keepdims=True) + epsilon) * gain


def swiglu(gate_rows, up_rows):
    return jax.nn.silu(gate_rows) * up_rows


def swap_seq(values):
    return lax.ppermute(values, "seq", [(0, 1), (1, 0)])


def in_order(own, other, axis):
    first = lax.axis_index("seq") == 0
    return jnp.where(
        first,
        jnp.concatenate([own, other], axis=axis),
        jnp.concatenate([other, own], axis=axis),
    )


def gather_seq(values, axis):
    if lax.axis_size("seq") == 2:
        return in_order(values, swap_seq(values), axis)
    return lax.all_gather(values, "seq", axis=axis, tiled=True)


def own_part(values, axis, index=None):
    size = values.shape[axis] // lax.axis_size("seq")
    index = lax.axis_index("seq") if index is None else index
    return lax.dynamic_slice_in_dim(values, index * size, size, axis=axis)


def sum_scatter_seq(values, axis):
    if lax.axis_size("seq") == 2:
        other = own_part(values, axis, 1 - lax.axis_index("seq")).astype(bf16)
        return own_part(values, axis) + swap_seq(other).astype(f32)
    return lax.psum_scatter(
        values.astype(bf16), "seq", scatter_dimension=axis, tiled=True
    ).astype(f32)


def own_first(values):
    if lax.axis_size("seq") == 2:
        return jnp.concatenate([values, swap_seq(values)], axis=0)
    return lax.all_gather(values, "seq", axis=0, tiled=True)


def sum_own_first(values):
    if lax.axis_size("seq") == 2:
        half = values.shape[0] // 2
        return values[:half] + swap_seq(values[half:].astype(bf16)).astype(f32)
    return sum_scatter_seq(values, 0)


def exchange_seq(values, split, join):
    if lax.axis_size("seq") == 2:
        other = own_part(values, split, 1 - lax.axis_index("seq"))
        return in_order(own_part(values, split), swap_seq(other), join)
    return lax.all_to_all(values, "seq", split_axis=split, concat_axis=join, tiled=True)


PLACES = 4


def in_grid():
    return lax.axis_size("shard") == 4 * PLACES and lax.axis_size("seq") == 2


def position():
    place = lax.axis_index("shard")
    return place // 4, (place // 2) % 2, place % 2


def flip(values, mask):
    size = lax.axis_size("shard")
    return lax.ppermute(values, "shard", [(i, i ^ mask) for i in range(size)])


def from_place(values, step):
    size = lax.axis_size("shard")
    return lax.ppermute(values, "shard", [(i, (i - 4 * step) % size) for i in range(size)])


def gather_shard(values):
    return lax.all_gather(values, "shard", axis=0, tiled=True)


def scatter_shard(values):
    return lax.psum_scatter(values, "shard", scatter_dimension=0, tiled=True)


def core_major(values):
    if not in_grid():
        return values
    rows, columns = values.shape
    places = values.reshape(rows, PLACES, 2, 2, columns // (4 * PLACES))
    return jnp.transpose(places, (0, 3, 2, 1, 4)).reshape(rows, columns)


def portion(values, index, count):
    size = values.shape[0] // count
    return lax.dynamic_slice_in_dim(values, index * size, size, axis=0)


def sum_pair(values, index, mask):
    sent = flip(portion(values, 1 - index, 2), mask)
    return (portion(values, index, 2).astype(f32) + sent.astype(f32)).astype(bf16)


def sum_along(values):
    z = position()[0]
    total = portion(values, z, PLACES).astype(f32)
    for r in range(1, PLACES):
        sent = from_place(portion(values, (z - r) % PLACES, PLACES), r)
        total = total + sent.astype(f32)
    return total.astype(bf16)


def first_sum(values):
    return sum_pair(values, position()[2], 1) if in_grid() else values


def second_sum(values):
    return sum_pair(values, position()[1], 2) if in_grid() else values


def third_sum(values):
    return sum_along(values) if in_grid() else scatter_shard(values)


def spread_kernel(cuts, seq_ref, own_ref, other_ref, *out_refs):
    def write(first, second):
        for (start, stop), out_ref in zip(cuts, out_refs):
            out_ref[:, : stop - start] = first[:, start:stop].astype(f32)
            out_ref[:, stop - start :] = second[:, start:stop].astype(f32)

    @pl.when(seq_ref[0] == 0)
    def _():
        write(own_ref, other_ref)

    @pl.when(seq_ref[0] != 0)
    def _():
        write(other_ref, own_ref)


def spread(own, other, cuts):
    rows = own.shape[0]
    memory = pl.BlockSpec(memory_space=pltpu.VMEM)
    return pl.pallas_call(
        functools.partial(spread_kernel, cuts),
        in_specs=[pl.BlockSpec(memory_space=pltpu.SMEM), memory, memory],
        out_specs=[memory] * len(cuts),
        out_shape=[jax.ShapeDtypeStruct((rows, 2 * (b - a)), f32) for a, b in cuts],
        compiler_params=pltpu.CompilerParams(vmem_limit_bytes=SPACE // 4),
        cost_estimate=pl.CostEstimate(flops=2**20, bytes_accessed=2**22, transcendentals=0),
        name="spread",
    )(seq_index(), own, other)


def seq_index():
    return jnp.stack([lax.axis_index("seq")]).astype(jnp.int32)


def after(values, *earlier):
    return lax.optimization_barrier((values, earlier))[0]


def sum_small(values, axes):
    if not in_grid():
        return lax.psum(values, axes)
    for mask in (1, 2, 4, 8):
        values = values + flip(values, mask)
    return values


def on_device(
    tokens,
    doc_starts,
    norm_gain,
    query_weight,
    key_weight,
    value_weight,
    gate_weight,
    beta_decay_weight,
    conv_filters,
    decay_params,
    out_norm_gain,
    out_weight,
    ffn_norm_gain,
    ffn_gate_weight,
    ffn_up_weight,
    down_weight,
    out_cotangent,
):
    heads = HEADS // lax.axis_size("seq")
    shards = lax.axis_size("shard")
    rows = query_weight.shape[0]
    width = 2 * heads * KEY
    ff = ffn_gate_weight.shape[1]

    logit_weight = own_part(beta_decay_weight.reshape(rows, HEADS, 2), 1)
    gain_rows = out_norm_gain.shape[0]
    raw_piece = jnp.concatenate(
        [
            own_part(query_weight, 1),
            own_part(key_weight, 1),
            logit_weight[:, :, 0],
            logit_weight[:, :, 1],
            norm_gain[:, None],
            ffn_norm_gain[:, None],
            jnp.pad(out_norm_gain, (0, rows - gain_rows))[:, None],
            jnp.zeros((rows, KEY - 2 * heads - 3), bf16),
        ],
        axis=1,
    )
    units = ff // shards // lax.axis_size("seq")

    def own_units(weight):
        return own_part(weight.reshape(rows, shards, ff // shards), 2).reshape(rows, shards * units)

    raw_wide = raw_piece.shape[1]
    value_end = raw_wide + heads * VALUE
    mixer_full = gather_shard(
        jnp.concatenate([raw_piece, own_part(value_weight, 1), own_part(gate_weight, 1)], axis=1)
    )
    raw_full = mixer_full[:, :raw_wide]
    value_full = mixer_full[:, raw_wide:value_end]
    gate_full = mixer_full[:, value_end:]
    half = shards * units
    model = out_weight.shape[1]
    out_rows = out_weight.shape[0]
    tall_full = gather_shard(jnp.concatenate([out_weight, own_part(down_weight, 0)], axis=0))
    tall_full = tall_full.reshape(shards, out_rows + units, model)
    out_full = tall_full[:, :out_rows].reshape(shards * out_rows, model)
    down_full = tall_full[:, out_rows:].reshape(half, model)
    ffn_full = gather_shard(
        jnp.concatenate([own_units(ffn_gate_weight), own_units(ffn_up_weight)], axis=1)
    )
    first_gain = raw_full[:, width + 2 * heads].astype(f32)
    second_gain = raw_full[:, width + 2 * heads + 1].astype(f32)
    third_gain = (
        raw_full[:, width + 2 * heads + 2]
        .reshape(shards, rows)[:, :gain_rows]
        .reshape(1, shards * gain_rows)
        .astype(f32)
    )

    own_tokens = tokens[0]
    token_count = own_tokens.shape[0]
    inputs = own_tokens.astype(f32)
    cotangent = out_cotangent[0]
    if lax.axis_size("seq") == 2:
        other = swap_seq(jnp.concatenate([own_tokens, cotangent], axis=0))
        all_inputs = in_order(own_tokens, other[:token_count], 0).astype(f32)
        all_cotangent = jnp.concatenate([cotangent, other[token_count:]], axis=0)
    else:
        all_inputs = gather_seq(own_tokens, 0).astype(f32)
        all_cotangent = own_first(cotangent)
    length = all_inputs.shape[0]
    all_scaled = all_inputs * lax.rsqrt(
        jnp.mean(all_inputs * all_inputs, axis=-1, keepdims=True) + epsilon
    )
    normed = (all_scaled * first_gain).astype(bf16)
    raw = forward_dot(normed, raw_full).astype(bf16)
    values = forward_dot(normed, value_full).astype(bf16)
    gate_rows = forward_dot(normed, gate_full)
    filters = jnp.concatenate(
        [
            conv_filters[:, :, :KEY].reshape(CONV, heads * KEY),
            conv_filters[:, :, KEY : 2 * KEY].reshape(CONV, heads * KEY),
            conv_filters[:, :, 2 * KEY :].reshape(CONV, heads * VALUE),
        ],
        axis=1,
    )
    decays = decay_params.T
    gated, *kept = mixer_forward(
        raw, values, filters, decays, doc_starts, gate_rows, third_gain, heads
    )
    gated_low = exchange_seq(gated, 0, 1)
    gated_low, down_full = lax.optimization_barrier((gated_low, down_full))
    middle = inputs + forward_dot(gated_low, out_full)
    second_norm, second_pull = jax.vjp(rms_norm, middle, second_gain)
    hidden = own_first(second_norm.astype(bf16))
    turned, ffn_full = lax.optimization_barrier((core_major(hidden), ffn_full))
    both_ffn = forward_dot(hidden, ffn_full)
    activated, swiglu_pull = jax.vjp(swiglu, both_ffn[:, :half], both_ffn[:, half:])
    activated_low = activated.astype(bf16)
    act_grad = times_transposed(all_cotangent, down_full)
    both_grad = jnp.concatenate([g.astype(bf16) for g in swiglu_pull(act_grad)], axis=1)
    hidden_grad = sum_own_first(times_transposed(both_grad, ffn_full))
    out_parts = forward_dot(activated_low, down_full)
    down_grad = transposed_times(activated_low, all_cotangent).astype(bf16)
    ffn_grad = transposed_times(turned, both_grad).astype(bf16)
    ffn_grad = first_sum(ffn_grad)
    out_sent = out_parts[token_count:].astype(bf16)
    hidden_grad, ffn_grad, down_grad, out_parts, out_sent = lax.optimization_barrier(
        (hidden_grad, ffn_grad, down_grad, out_parts, out_sent)
    )
    middle_part, ffn_gain_grad = second_pull(hidden_grad)
    middle_grad = cotangent.astype(f32) + middle_part
    branch_low = middle_grad.astype(bf16)
    out_grad = transposed_times(gated_low, branch_low).astype(bf16)
    gated_grad = times_transposed(branch_low, out_full).astype(bf16)
    if lax.axis_size("seq") == 2:
        other_grad = swap_seq(own_part(gated_grad, 1, 1 - lax.axis_index("seq")))
        own_grad = own_part(gated_grad, 1)
    else:
        own_grad = other_grad = exchange_seq(gated_grad, 1, 0)
    ffn_grad = second_sum(ffn_grad)
    tall_grad = jnp.concatenate(
        [out_grad.reshape(shards, out_rows, model), down_grad.reshape(shards, units, model)], axis=1
    ).reshape(shards * (out_rows + units), model)
    own_grad, other_grad, ffn_grad, tall_grad = lax.optimization_barrier(
        (own_grad, other_grad, ffn_grad, tall_grad)
    )
    ffn_share = third_sum(ffn_grad)
    tall_share = scatter_shard(tall_grad)
    if lax.axis_size("seq") == 2:
        out_parts = out_parts[:token_count] + swap_seq(after(out_sent, other_grad)).astype(f32)
    else:
        out_parts = sum_own_first(out_parts)
    block_out = (middle + out_parts).astype(bf16)
    mixer_grad, filters_grad, decays_grad, out_gain_grad = mixer_backward(
        raw,
        values,
        filters,
        decays,
        doc_starts,
        gate_rows,
        third_gain,
        (own_grad, other_grad),
        kept,
        heads,
    )
    mixer_grad, ffn_share, block_out = lax.optimization_barrier((mixer_grad, ffn_share, block_out))
    mixer_weight_grad = transposed_times(normed, mixer_grad).astype(bf16)
    mixer_grad, mixer_weight_grad = lax.optimization_barrier((mixer_grad, mixer_weight_grad))
    mixer_share = scatter_shard(mixer_weight_grad)
    normed_grad = times_transposed(mixer_grad, mixer_full)
    norm_gain_grad = jnp.sum(normed_grad * all_scaled, axis=0)
    if lax.axis_size("seq") == 2:
        sent = own_part(normed_grad, 0, 1 - lax.axis_index("seq")).astype(bf16)
        own_normed_grad = own_part(normed_grad, 0) + swap_seq(sent).astype(f32)
    else:
        sent = normed_grad
        own_normed_grad = sum_scatter_seq(normed_grad, 0)
    _, first_pull = jax.vjp(lambda v: rms_norm(v, first_gain), inputs)
    tokens_grad = middle_grad + first_pull(own_normed_grad)[0]

    def all_units(share):
        share = gather_seq(share.reshape(rows, shards, units), 2)
        return share.reshape(rows, ff).astype(f32)

    ffn_gate_share = all_units(ffn_share[:, :half])
    ffn_up_share = all_units(ffn_share[:, half:])
    tall_share = gather_seq(after(tall_share, mixer_grad)[None], 0).astype(f32)
    out_share = jnp.sum(tall_share[:, :out_rows], axis=0)
    down_share = tall_share[:, out_rows:].reshape(-1, model)
    if lax.axis_size("seq") == 2:
        other_share = swap_seq(mixer_share)

        def side_by_side(start, stop):
            own, other = mixer_share[:, start:stop], other_share[:, start:stop]
            return in_order(own.astype(f32), other.astype(f32), 1)
    else:
        every = gather_seq(mixer_share[None], 0)

        def side_by_side(start, stop):
            part = jnp.swapaxes(every[:, :, start:stop], 0, 1)
            return part.reshape(rows, -1).astype(f32)

    cuts = (
        (0, heads * KEY),
        (heads * KEY, width),
        (raw_wide, value_end),
        (value_end, mixer_share.shape[1]),
    )
    if lax.axis_size("seq") == 2:
        shares = spread(mixer_share, other_share, cuts)
    else:
        shares = [side_by_side(start, stop) for start, stop in cuts]
    query_share, key_share, value_share, gate_share = shares
    logit_share = side_by_side(width, width + 2 * heads).reshape(rows, -1, 2, heads)
    logit_share = jnp.swapaxes(logit_share, 2, 3).reshape(rows, 2 * HEADS)

    all_width = filters.shape[1]
    filters_grad = jnp.sum(filters_grad.reshape(CONV, 8, all_width), axis=1)
    lengths = [shards * n for n in (norm_gain.shape[0], gain_rows, ffn_norm_gain.shape[0])]
    small = jnp.concatenate(
        [
            filters_grad.reshape(CONV * all_width),
            decays_grad.reshape(2 * heads),
            norm_gain_grad,
            jnp.sum(out_gain_grad, axis=0),
            ffn_gain_grad,
        ]
    )
    small = sum_small(after(small, sent), ("shard",))
    head_end = CONV * all_width + 2 * heads
    filters_grad = small[: CONV * all_width].reshape(CONV, all_width)
    decays_grad = small[CONV * all_width : head_end].reshape(2, heads)
    gains = small[head_end:]
    gains = gains + swap_seq(gains) if in_grid() else lax.psum(gains, "seq")
    split = (heads * KEY, 2 * heads * KEY)
    filters_out = jnp.concatenate(
        [
            filters_grad[:, : split[0]].reshape(CONV, heads, KEY),
            filters_grad[:, split[0] : split[1]].reshape(CONV, heads, KEY),
            filters_grad[:, split[1] :].reshape(CONV, heads, VALUE),
        ],
        axis=2,
    )
    gains = [
        gains[: lengths[0]],
        gains[lengths[0] : lengths[0] + lengths[1]],
        gains[lengths[0] + lengths[1] :],
    ]
    place = lax.axis_index("shard")
    gains = [
        lax.dynamic_slice_in_dim(g, place * (g.shape[0] // shards), g.shape[0] // shards)
        for g in gains
    ]
    return (
        block_out[None],
        tokens_grad[None],
        gains[0],
        query_share,
        key_share,
        value_share,
        gate_share,
        logit_share,
        filters_out,
        decays_grad.T,
        gains[1],
        out_share,
        gains[2],
        ffn_gate_share,
        ffn_up_share,
        down_share,
    )


def solution(mesh):
    in_specs = (
        P("shard", "seq", None),
        P("shard", None),
        P("shard"),
        P("shard", None),
        P("shard", None),
        P("shard", None),
        P("shard", None),
        P("shard", None),
        P(None, "seq", None),
        P("seq", None),
        P("shard"),
        P("shard", None),
        P("shard"),
        P("shard", None),
        P("shard", None),
        P("shard", None),
        P("shard", "seq", None),
    )
    out_specs = (
        P("shard", "seq", None),
        P("shard", "seq", None),
        P("shard"),
        P("shard", None),
        P("shard", None),
        P("shard", None),
        P("shard", None),
        P("shard", None),
        P(None, "seq", None),
        P("seq", None),
        P("shard"),
        P("shard", None),
        P("shard"),
        P("shard", None),
        P("shard", None),
        P("shard", None),
    )
    return jax.shard_map(
        on_device, mesh=mesh, in_specs=in_specs, out_specs=out_specs, check_vma=False
    )
```

```python
import functools

import jax
import jax.numpy as jnp
from jax import lax
from jax.experimental import pallas as pl
from jax.experimental.pallas import tpu as pltpu
from jax.sharding import PartitionSpec as P

HEADS = 8
KEY = 128
VALUE = 256
CONV = 4
GROUP = 64
HALO = 16
SUB = 4
epsilon = 1e-06
f32 = jnp.float32
bf16 = jnp.bfloat16


def dot(a, b, ca=1, cb=0):
    return lax.dot_general(a, b, (((ca,), (cb,)), ((), ())), preferred_element_type=f32)


def halves(values):
    high = values.astype(bf16)
    return high, (values - high.astype(f32)).astype(bf16)


def fine_dot(a, b, ca=1, cb=0):
    if not isinstance(a, tuple):
        return dot(a, b[0], ca, cb) + dot(a, b[1], ca, cb)
    if not isinstance(b, tuple):
        return dot(a[0], b, ca, cb) + dot(a[1], b, ca, cb)
    return dot(a[0], b[0], ca, cb) + (dot(a[0], b[1], ca, cb) + dot(a[1], b[0], ca, cb))


def iota(shape, dim):
    return lax.broadcasted_iota(jnp.int32, shape, dim)


def doc_count(starts_ref, times):
    count = jnp.zeros(times.shape, jnp.int32)
    for s in range(starts_ref.shape[1]):
        count = count + jnp.where(times >= starts_ref[0, s], 1, 0)
    return count


def scalar_doc(starts_ref, time):
    count = 0
    for s in range(starts_ref.shape[1]):
        count = count + (time >= starts_ref[0, s]).astype(jnp.int32)
    return count


def per_head(cols, heads, width):
    rows = cols.shape[0]
    lane = iota((rows, heads * width), 1)
    out = jnp.broadcast_to(cols[:, heads - 1 : heads], (rows, heads * width))
    for h in range(heads - 2, -1, -1):
        out = jnp.where(lane < (h + 1) * width, cols[:, h : h + 1], out)
    return out


def head_sums(panel, heads, width):
    lane = iota(panel.shape, 1)
    sums = []
    for h in range(heads):
        inside = (lane >= h * width) & (lane < (h + 1) * width)
        sums.append(jnp.sum(jnp.where(inside, panel, 0.0), axis=1, keepdims=True))
    return columns(sums)


def across(mask, width):
    return jnp.concatenate([mask] * (width // KEY), axis=1)


def columns(parts):
    rows = parts[0].shape[0]
    lane = iota((rows, len(parts)), 1)
    out = jnp.broadcast_to(parts[-1], (rows, len(parts)))
    for h in range(len(parts) - 2, -1, -1):
        out = jnp.where(lane == h, parts[h], out)
    return out


def block_diagonal(panel, heads):
    if heads == 1:
        return panel
    lane = iota(panel.shape, 1)
    zero = jnp.zeros_like(panel)
    parts = []
    for h in range(heads):
        inside = (lane >= h * GROUP) & (lane < (h + 1) * GROUP)
        parts.append(jnp.where(inside, panel, zero))
    return jnp.concatenate(parts, axis=0)


def diagonal_panel(full, heads):
    if heads == 1:
        return full
    lane = iota((GROUP, heads * GROUP), 1)
    out = full[(heads - 1) * GROUP :]
    for h in range(heads - 2, -1, -1):
        out = jnp.where(lane < (h + 1) * GROUP, full[h * GROUP : (h + 1) * GROUP], out)
    return out


def key_diagonal(keys):
    heads = len(keys)
    if heads == 1:
        return keys[0]
    zero = jnp.zeros_like(keys[0])
    rows = []
    for h in range(heads):
        rows.append(jnp.concatenate([keys[h] if o == h else zero for o in range(heads)], axis=1))
    return jnp.concatenate(rows, axis=0)


def scan_rows(values, reverse=False):
    rows = values.shape[0]
    index = iota(values.shape, 0)
    step = 1
    while step < rows:
        if reverse:
            moved = pltpu.roll(values, rows - step, 0)
            values = values + jnp.where(index < rows - step, moved, 0.0)
        else:
            moved = pltpu.roll(values, step, 0)
            values = values + jnp.where(index >= step, moved, 0.0)
        step *= 2
    return values


def sigmoid(v):
    return 1.0 / (1.0 + jnp.exp(-v))


def softplus(v):
    return jnp.maximum(v, 0.0) + jnp.log(1.0 + jnp.exp(-jnp.abs(v)))


def in_turn(generators):
    generators = list(generators)
    while generators:
        still = []
        for generator in generators:
            if next(generator, True) is None:
                still.append(generator)
        generators = still


class Block:
    def __init__(self, heads, base, raw_ref, value_ref, filters_ref, decay_ref, starts_ref):
        self.heads = heads
        self.base = base
        self.raw_ref = raw_ref
        self.value_ref = value_ref
        self.filters_ref = filters_ref
        self.decay_ref = decay_ref
        self.starts_ref = starts_ref

    def build(self):
        heads, base, starts_ref = self.heads, self.base, self.starts_ref
        raw_ref, decay_ref = self.raw_ref, self.decay_ref
        width = 2 * heads * KEY
        times = base + iota((GROUP, 1), 0)
        docs = doc_count(starts_ref, times)
        wide = (GROUP, KEY)
        self.masks, self.next_masks = [], []
        for o in range(1, CONV):
            same = (docs == doc_count(starts_ref, times - o)).astype(f32)
            self.masks.append(jnp.broadcast_to(same, wide))
            same = (docs == doc_count(starts_ref, times + o)).astype(f32)
            self.next_masks.append(jnp.broadcast_to(same, wide))
        self.query, self.keys, self.query_pre, self.key_pre = [], [], [], []
        self.query_conv, self.key_conv, self.query_scale, self.key_scale = [], [], [], []
        for h in range(heads):
            pre = self.convolve(h * KEY, KEY)
            conv = pre * sigmoid(pre)
            scale = lax.rsqrt(jnp.sum(conv * conv, axis=1, keepdims=True) + epsilon)
            self.query_pre.append(pre)
            self.query_conv.append(conv)
            self.query_scale.append(scale)
            self.query.append(conv * scale * KEY ** (-0.5))
        for h in range(heads):
            pre = self.convolve((heads + h) * KEY, KEY)
            conv = pre * sigmoid(pre)
            scale = lax.rsqrt(jnp.sum(conv * conv, axis=1, keepdims=True) + epsilon)
            self.key_pre.append(pre)
            self.key_conv.append(conv)
            self.key_scale.append(scale)
            self.keys.append(conv * scale)
        yield
        logits = raw_ref[pl.ds(base, GROUP), width : width + KEY].astype(f32)
        self.strength = sigmoid(logits[:, :heads])
        self.decay_logit = logits[:, heads : 2 * heads] + decay_ref[1:2, :heads]
        self.decay_rate = -jnp.exp(decay_ref[0:1, :heads])
        self.log_decay = self.decay_rate * softplus(self.decay_logit)
        yield
        sums = scan_rows(self.log_decay)
        yield
        self.sums = sums
        last = sums[GROUP - 1 : GROUP]
        before = scalar_doc(starts_ref, base - 1)
        final = scalar_doc(starts_ref, base + GROUP - 1)
        self.entering = jnp.where(docs == before, jnp.exp(sums), 0.0)
        same_last = docs == final
        self.leaving = jnp.where(same_last, jnp.exp(jnp.where(same_last, last - sums, 0.0)), 0.0)
        self.retain = self.entering[GROUP - 1 : GROUP]
        yield
        shape = (GROUP, heads * GROUP)
        row = iota(shape, 0)
        place = jnp.bitwise_and(iota(shape, 1), GROUP - 1)
        self.row, self.place = row, place
        across = jnp.bitwise_and(iota((1, heads * GROUP), 1), GROUP - 1)
        docs_across = doc_count(starts_ref, base + across)
        same = docs == docs_across
        self.inclusive = same & (row >= place)
        self.strict = same & (row > place)
        sums_down = per_head(sums, heads, GROUP)
        sums_across = jnp.sum(jnp.where(row == place, sums_down, 0.0), axis=0, keepdims=True)
        gap = jnp.where(self.inclusive, sums_down - sums_across, 0.0)
        self.fade = jnp.where(self.inclusive, jnp.exp(gap), 0.0)
        yield
        self.strength_down = per_head(self.strength, heads, GROUP)
        low_keys = [k.astype(bf16) for k in self.keys]
        low_query = [q.astype(bf16) for q in self.query]
        self.keys = [k.astype(f32) for k in low_keys]
        self.query = [q.astype(f32) for q in low_query]
        self.low_keys, self.low_query = low_keys, low_query
        self.key_diag = key_diagonal(low_keys)
        left = jnp.concatenate(
            [jnp.concatenate(low_keys, axis=1), jnp.concatenate(low_query, axis=1)], axis=0
        )
        self.query_key_rows = left
        grams = dot(left, self.key_diag, 1, 1)
        yield
        self.key_gram = grams[:GROUP]
        self.score_gram = grams[GROUP:]
        self.system = jnp.where(self.strict, self.strength_down * self.key_gram * self.fade, 0.0)
        self.scores = self.score_gram * self.fade

    def taps(self, start, width):
        source = self.raw_ref
        if start >= 2 * self.heads * KEY:
            source = self.value_ref
            start = start - 2 * self.heads * KEY
        current = source[pl.ds(self.base, GROUP), start : start + width].astype(f32)
        earlier = pl.multiple_of(jnp.maximum(self.base - HALO, 0), HALO)
        halo = source[pl.ds(earlier, HALO), start : start + width].astype(f32)
        extended = jnp.concatenate([halo, current], axis=0)
        return [current] + [
            pltpu.roll(extended, o, 0)[HALO:] * across(self.masks[o - 1], width)
            for o in range(1, CONV)
        ]

    def convolve(self, start, width):
        taps = self.taps(start, width)
        filters = self.filters_ref[:, start : start + width]
        total = taps[0] * filters[CONV - 1 : CONV]
        for o in range(1, CONV):
            total = total + taps[o] * filters[CONV - 1 - o : CONV - o]
        return total


def inverse(systems, heads, row, place):
    eye = (row == place).astype(f32)
    apart = jnp.bitwise_xor(row, place)

    def part(system, size):
        return jnp.where((apart >= size) & (apart < 2 * size), system, 0.0)

    results = [eye - part(system, 1) for system in systems]
    size = 2
    while size < GROUP:
        low = [result.astype(bf16) for result in results]
        inner = [
            dot(part(system, size).astype(bf16), block_diagonal(one, heads))
            for system, one in zip(systems, low)
        ]
        inner = [block_diagonal(one.astype(bf16), heads) for one in inner]
        results = [
            result - dot(one, right) for result, one, right in zip(results, low, inner)
        ]
        size *= 2
    return results


def forward_kernel(
    heads, starts_ref, raw_ref, value_ref, filters_ref, decay_ref, gate_ref, gain_ref,
    gated_ref, mixed_ref, inverse_ref, delta_ref, rest_ref, memory_ref, state,
):
    step = pl.program_id(0)

    @pl.when(step == 0)
    def _():
        state[...] = jnp.zeros_like(state)

    blocks = []
    for s in range(SUB):
        base = pl.multiple_of((step * SUB + s) * GROUP, GROUP)
        blocks.append(Block(heads, base, raw_ref, value_ref, filters_ref, decay_ref, starts_ref))
    in_turn(block.build() for block in blocks)
    solves = inverse([block.system for block in blocks], heads, blocks[0].row, blocks[0].place)
    for s, block in enumerate(blocks):
        block.values = []
        for h in range(heads):
            pre = block.convolve(2 * heads * KEY + h * VALUE, VALUE)
            block.values.append(pre * sigmoid(pre))
        block.solve = solves[s]
        inverse_ref[s * GROUP : (s + 1) * GROUP] = block.solve.astype(bf16)
    for s, block in enumerate(blocks):
        from_state, rest, right = [], [], []
        for h in range(heads):
            entering = block.entering[:, h : h + 1]
            memory = state[h * KEY : (h + 1) * KEY].astype(bf16)
            memory_ref[(s * heads + h) * KEY : (s * heads + h + 1) * KEY] = memory
            both = jnp.concatenate([block.low_keys[h], block.low_query[h]], axis=0)
            read = dot(both, memory)
            from_state.append(entering * read[GROUP:])
            missing = block.values[h] - entering * read[:GROUP]
            rest.append(missing.astype(bf16))
            right.append(block.strength[:, h : h + 1] * missing)
        rest_ref[s * heads * GROUP : (s + 1) * heads * GROUP] = jnp.concatenate(rest, axis=0)
        solve = tuple(block_diagonal(p, heads) for p in halves(block.solve))
        delta = fine_dot(solve, halves(jnp.concatenate(right, axis=0)))
        delta_ref[s * heads * GROUP : (s + 1) * heads * GROUP] = delta
        scores = tuple(block_diagonal(p, heads) for p in halves(block.scores))
        outputs = fine_dot(scores, halves(delta))
        for h in range(heads):
            rows = slice(h * GROUP, (h + 1) * GROUP)
            out = from_state[h] + outputs[rows]
            here = slice(s * GROUP, (s + 1) * GROUP)
            lanes = slice(h * VALUE, (h + 1) * VALUE)
            low = out.astype(bf16)
            mixed_ref[here, lanes] = low
            low = low.astype(f32)
            gate = gate_ref[here, lanes]
            scale = lax.rsqrt(jnp.mean(low * low, axis=1, keepdims=True) + epsilon)
            gated = low * scale * gain_ref[0:1] * (gate * sigmoid(gate))
            gated_ref[here, lanes] = gated.astype(bf16)
            leaving = halves(block.leaving[:, h : h + 1] * delta[rows])
            keep = block.retain[:, h : h + 1]
            own = slice(h * KEY, (h + 1) * KEY)
            state[own] = keep * state[own] + fine_dot(block.low_keys[h], leaving, 0, 0)


def silu_slope(pre):
    gate = sigmoid(pre)
    return gate * (1.0 + pre * (1.0 - gate))


def backward_kernel(
    heads, starts_ref, seq_ref, raw_ref, value_ref, filters_ref, decay_ref, gate_ref, gain_ref,
    own_grad_ref, other_grad_ref, mixed_ref, inverse_ref, delta_ref, rest_ref, memory_ref,
    raw_grad_ref, filters_grad_ref, decay_grad_ref, gain_grad_ref,
    state, halo,
):
    step = pl.program_id(0)
    steps = pl.num_programs(0)
    width = 2 * heads * KEY
    own_rows = (2 * (steps - 1 - step) >= steps) == (seq_ref[0] != 0)

    @pl.when(step == 0)
    def _():
        state[...] = jnp.zeros_like(state)
        gain_grad_ref[...] = jnp.zeros_like(gain_grad_ref)
        halo[...] = jnp.zeros_like(halo)
        filters_grad_ref[...] = jnp.zeros_like(filters_grad_ref)
        decay_grad_ref[...] = jnp.zeros_like(decay_grad_ref)

    def pull(s):
        base = pl.multiple_of(((steps - 1 - step) * SUB + s) * GROUP, GROUP)
        block = Block(heads, base, raw_ref, value_ref, filters_ref, decay_ref, starts_ref)
        yield from block.build()
        yield
        here = slice(s * GROUP, (s + 1) * GROUP)
        stacked = slice(s * heads * GROUP, (s + 1) * heads * GROUP)
        solve = inverse_ref[here]
        delta = delta_ref[stacked]
        rest = rest_ref[stacked]
        mixed_grads = []
        for h in range(heads):
            lanes = slice(h * VALUE, (h + 1) * VALUE)
            grad = jnp.where(
                own_rows,
                own_grad_ref[here, lanes].astype(f32),
                other_grad_ref[here, lanes].astype(f32),
            )
            mixed = mixed_ref[here, lanes].astype(f32)
            gate = gate_ref[here, lanes]
            scale = lax.rsqrt(jnp.mean(mixed * mixed, axis=1, keepdims=True) + epsilon)
            unit = mixed * scale
            open_gate = sigmoid(gate)
            swish = gate * open_gate
            along = grad * unit
            product = (along * swish).reshape(GROUP // 8, 8, VALUE)
            gain_grad_ref[...] = gain_grad_ref[...] + jnp.sum(product, axis=0)
            gate_grad = along * gain_ref[0:1] * (open_gate * (1.0 + gate * (1.0 - open_gate)))
            behind = width + KEY + (heads + h) * VALUE
            raw_grad_ref[here, behind : behind + VALUE] = gate_grad.astype(bf16)
            unit_grad = grad * swish * gain_ref[0:1]
            inner = jnp.mean(unit_grad * unit, axis=1, keepdims=True)
            mixed_grads.append((scale * (unit_grad - unit * inner)).astype(bf16))
        out_grad = jnp.concatenate(mixed_grads, axis=0)
        yield
        scores = tuple(block_diagonal(p, heads) for p in halves(block.scores))
        from_scores = fine_dot(scores, out_grad, 0, 0)
        delta = halves(delta)
        score_part = diagonal_panel(sum(dot(out_grad, d, 1, 1) for d in delta), heads)
        scores_grad = jnp.where(block.inclusive, score_part, 0.0)
        score_gram_grad = scores_grad * block.fade
        solve = block_diagonal(solve, heads)
        yield "chain"
        later = [state[h * KEY : (h + 1) * KEY] for h in range(heads)]
        later_low = [m.astype(bf16) for m in later]
        pulled = jnp.concatenate(
            [
                block.leaving[:, h : h + 1] * dot(block.low_keys[h], later_low[h])
                for h in range(heads)
            ],
            axis=0,
        )
        delta_grad = pulled + from_scores
        right_grad = dot(solve, delta_grad.astype(bf16), 0, 0)
        rest_grad, pairs = [], []
        for h in range(heads):
            rows = slice(h * GROUP, (h + 1) * GROUP)
            rest_grad.append(block.strength[:, h : h + 1] * right_grad[rows])
            pairs.append(jnp.concatenate([out_grad[rows], rest_grad[h].astype(bf16)], axis=0))
            entering = block.entering[:, h : h + 1]
            left = jnp.concatenate(
                [entering * block.query[h], -entering * block.keys[h]], axis=0
            ).astype(bf16)
            state[h * KEY : (h + 1) * KEY] = (
                block.retain[:, h : h + 1] * later[h] + dot(left, pairs[h], 0, 0)
            )
        yield "chain"
        entering_query_grad, entering_key_grad, leaving_key_grad, retain_grad = [], [], [], []
        strength_grad = []
        for h in range(heads):
            rows = slice(h * GROUP, (h + 1) * GROUP)
            strength_grad.append(
                jnp.sum(right_grad[rows] * rest[rows].astype(f32), axis=1, keepdims=True)
            )
            memory = memory_ref[(s * heads + h) * KEY : (s * heads + h + 1) * KEY]
            back = dot(pairs[h], memory, 1, 1)
            entering_query_grad.append(back[:GROUP])
            entering_key_grad.append(-back[GROUP:])
            leaving_key_grad.append(sum(dot(d[rows], later_low[h], 1, 1) for d in delta))
            product = later[h] * memory.astype(f32)
            retain_grad.append(
                jnp.sum(jnp.sum(product, axis=0, keepdims=True), axis=1, keepdims=True)
            )
        yield
        right_low = right_grad.astype(bf16)
        system_part = diagonal_panel(sum(dot(right_low, d, 1, 1) for d in delta), heads)
        system_grad = jnp.where(block.strict, -system_part, 0.0)
        faded = system_grad * block.fade
        key_gram_grad = block.strength_down * faded
        gap_grad = score_gram_grad * block.score_gram + key_gram_grad * block.key_gram
        yield
        strength_panel = head_sums(faded * block.key_gram, heads, GROUP)
        down = jnp.sum(gap_grad, axis=0, keepdims=True)
        gap_rows = head_sums(
            gap_grad - jnp.where(block.row == block.place, down, 0.0), heads, GROUP
        )
        yield
        both_low = jnp.concatenate([key_gram_grad, score_gram_grad], axis=0).astype(bf16)
        straight = dot(both_low, block.key_diag)
        turned = dot(both_low, block.query_key_rows, 0, 0)
        yield
        entering_grad, leaving_grad = [], []
        for h in range(heads):
            lanes = slice(h * KEY, (h + 1) * KEY)
            entering = block.entering[:, h : h + 1]
            fading = block.leaving[:, h : h + 1]
            query_grad = entering * entering_query_grad[h] + straight[GROUP:, lanes]
            key_grad = (
                turned[h * GROUP : (h + 1) * GROUP, lanes]
                + straight[:GROUP, lanes]
                + fading * leaving_key_grad[h]
                + entering * entering_key_grad[h]
            )
            entering_grad.append(
                jnp.sum(
                    entering_query_grad[h] * block.query[h] + entering_key_grad[h] * block.keys[h],
                    axis=1,
                    keepdims=True,
                )
            )
            leaving_grad.append(
                jnp.sum(leaving_key_grad[h] * block.keys[h], axis=1, keepdims=True)
            )
            for start, grad, conv, scale, pre, factor in (
                (h * KEY, query_grad, block.query_conv[h], block.query_scale[h],
                 block.query_pre[h], KEY ** (-0.5)),
                ((heads + h) * KEY, key_grad, block.key_conv[h], block.key_scale[h],
                 block.key_pre[h], 1.0),
            ):
                along = jnp.sum(grad * conv, axis=1, keepdims=True)
                conv_grad = (factor * scale) * (grad - conv * (scale * scale * along))
                convolve_back(
                    block, s, start, start, KEY, conv_grad * silu_slope(pre), starts_ref,
                    raw_grad_ref, filters_grad_ref, halo,
                )
            yield
            start = 2 * heads * KEY + h * VALUE
            pre = block.convolve(start, VALUE)
            convolve_back(
                block, s, start, start + KEY, VALUE, rest_grad[h] * silu_slope(pre), starts_ref,
                raw_grad_ref, filters_grad_ref, halo,
            )
        yield
        entering_grad = columns(entering_grad) * block.entering
        leaving_grad = columns(leaving_grad) * block.leaving
        strength_grad = columns(strength_grad) + strength_panel
        retain_grad = columns(retain_grad) * block.retain
        at_last = jnp.sum(leaving_grad, axis=0, keepdims=True) + retain_grad
        index = iota((GROUP, heads), 0)
        sums_grad = (
            entering_grad - leaving_grad + gap_rows + jnp.where(index == GROUP - 1, at_last, 0.0)
        )
        log_decay_grad = scan_rows(sums_grad, reverse=True)
        yield
        logit_grad = log_decay_grad * block.decay_rate * sigmoid(block.decay_logit)
        beta_grad = strength_grad * block.strength * (1.0 - block.strength)
        lane = iota((GROUP, KEY), 1)
        packed = jnp.zeros((GROUP, KEY), f32)
        for h in range(heads):
            packed = jnp.where(lane == h, beta_grad[:, h : h + 1], packed)
            packed = jnp.where(lane == heads + h, logit_grad[:, h : h + 1], packed)
        raw_grad_ref[here, width : width + KEY] = packed.astype(bf16)
        scale_sum = jnp.sum(log_decay_grad * block.log_decay, axis=0, keepdims=True)
        bias_sum = jnp.sum(logit_grad, axis=0, keepdims=True)
        decay_grad_ref[0:1] = decay_grad_ref[0:1] + scale_sum
        decay_grad_ref[1:2] = decay_grad_ref[1:2] + bias_sum

    pulls = [pull(s) for s in range(SUB - 1, -1, -1)]
    waiting = list(pulls)
    while waiting:
        waiting = [p for p in waiting if next(p) is None]
    for p in pulls:
        next(p)
    in_turn(pulls)


def convolve_back(
    block, s, start, place, width, pre_grad, starts_ref, grad_ref, filters_grad_ref, halo
):
    lanes = slice(start, start + width)
    taps = block.taps(start, width)
    for o in range(CONV):
        j = CONV - 1 - o
        product = (pre_grad * taps[o]).reshape(GROUP // 8, 8, width)
        filters_grad_ref[j * 8 : (j + 1) * 8, lanes] = filters_grad_ref[
            j * 8 : (j + 1) * 8, lanes
        ] + jnp.sum(product, axis=0)
    filters = block.filters_ref[:, lanes]
    extended = jnp.concatenate([pre_grad, halo[:, lanes]], axis=0)
    rows = GROUP + 8
    total = pre_grad * filters[CONV - 1 : CONV]
    for o in range(1, CONV):
        moved = pltpu.roll(extended, rows - o, 0)[:GROUP] * across(block.next_masks[o - 1], width)
        total = total + moved * filters[CONV - 1 - o : CONV - o]
    grad_ref[s * GROUP : (s + 1) * GROUP, place : place + width] = total.astype(bf16)
    halo[:, lanes] = pre_grad[:8]


SPACE = 56 * 2**20


def mixer_forward(raw, values, filters, decays, starts, gates, gain, heads):
    length, wide = raw.shape
    steps = length // (SUB * GROUP)
    rows = SUB * GROUP
    blocks = length // GROUP
    whole = lambda a: pl.BlockSpec(a.shape, lambda i: (0, 0))
    part = lambda r, c: pl.BlockSpec((r, c), lambda i: (i, 0))
    return pl.pallas_call(
        functools.partial(forward_kernel, heads),
        grid=(steps,),
        in_specs=[
            pl.BlockSpec(memory_space=pltpu.SMEM),
            whole(raw),
            whole(values),
            whole(filters),
            whole(decays),
            part(rows, heads * VALUE),
            whole(gain),
        ],
        out_specs=[
            part(rows, heads * VALUE),
            part(rows, heads * VALUE),
            part(rows, heads * GROUP),
            part(rows * heads, VALUE),
            part(rows * heads, VALUE),
            part(SUB * heads * KEY, VALUE),
        ],
        out_shape=[
            jax.ShapeDtypeStruct((length, heads * VALUE), bf16),
            jax.ShapeDtypeStruct((length, heads * VALUE), bf16),
            jax.ShapeDtypeStruct((length, heads * GROUP), bf16),
            jax.ShapeDtypeStruct((length * heads, VALUE), f32),
            jax.ShapeDtypeStruct((length * heads, VALUE), bf16),
            jax.ShapeDtypeStruct((blocks * heads * KEY, VALUE), bf16),
        ],
        scratch_shapes=[pltpu.VMEM((heads * KEY, VALUE), f32)],
        compiler_params=pltpu.CompilerParams(vmem_limit_bytes=SPACE),
        cost_estimate=pl.CostEstimate(
            flops=length * heads * 11_000_000, bytes_accessed=2**24, transcendentals=0
        ),
        name="mixer_forward",
    )(starts, raw, values, filters, decays, gates, gain)


def mixer_backward(raw, values, filters, decays, starts, gates, gain, gated_grads, kept, heads):
    length, wide = raw.shape
    steps = length // (SUB * GROUP)
    rows = SUB * GROUP
    whole = lambda a: pl.BlockSpec(a.shape, lambda i: (0, 0))
    same = lambda r, c: pl.BlockSpec((r, c), lambda i: (0, 0))
    part = lambda r, c: pl.BlockSpec((r, c), lambda i: (steps - 1 - i, 0))
    count = gated_grads[0].shape[0] // rows
    part_grad = pl.BlockSpec((rows, heads * VALUE), lambda i: (lax.rem(steps - 1 - i, count), 0))
    return pl.pallas_call(
        functools.partial(backward_kernel, heads),
        grid=(steps,),
        in_specs=[
            pl.BlockSpec(memory_space=pltpu.SMEM),
            pl.BlockSpec(memory_space=pltpu.SMEM),
            whole(raw),
            whole(values),
            whole(filters),
            whole(decays),
            part(rows, heads * VALUE),
            whole(gain),
            part_grad,
            part_grad,
            part(rows, heads * VALUE),
            part(rows, heads * GROUP),
            part(rows * heads, VALUE),
            part(rows * heads, VALUE),
            part(SUB * heads * KEY, VALUE),
        ],
        out_specs=[
            part(rows, wide + 2 * heads * VALUE),
            same(8 * CONV, filters.shape[1]),
            same(2, heads),
            same(8, VALUE),
        ],
        out_shape=[
            jax.ShapeDtypeStruct((length, wide + 2 * heads * VALUE), bf16),
            jax.ShapeDtypeStruct((8 * CONV, filters.shape[1]), f32),
            jax.ShapeDtypeStruct((2, heads), f32),
            jax.ShapeDtypeStruct((8, VALUE), f32),
        ],
        scratch_shapes=[
            pltpu.VMEM((heads * KEY, VALUE), f32),
            pltpu.VMEM((8, filters.shape[1]), f32),
        ],
        compiler_params=pltpu.CompilerParams(vmem_limit_bytes=SPACE),
        cost_estimate=pl.CostEstimate(
            flops=length * heads * 14_000_000, bytes_accessed=2**24, transcendentals=0
        ),
        name="mixer_backward",
    )(starts, seq_index(), raw, values, filters, decays, gates, gain, *gated_grads, *kept)


def forward_dot(left_side, right_side):
    return jnp.dot(left_side, right_side, preferred_element_type=f32)


def times_transposed(left_side, right_side):
    return dot(left_side, right_side, 1, 1)


def transposed_times(left_side, right_side):
    return dot(left_side, right_side, 0, 0)


def rms_norm(values, gain):
    return values * lax.rsqrt(jnp.mean(values * values, axis=-1, keepdims=True) + epsilon) * gain


def swiglu(gate_rows, up_rows):
    return jax.nn.silu(gate_rows) * up_rows


def swap_seq(values):
    return lax.ppermute(values, "seq", [(0, 1), (1, 0)])


def in_order(own, other, axis):
    first = lax.axis_index("seq") == 0
    return jnp.where(
        first,
        jnp.concatenate([own, other], axis=axis),
        jnp.concatenate([other, own], axis=axis),
    )


def gather_seq(values, axis):
    if lax.axis_size("seq") == 2:
        return in_order(values, swap_seq(values), axis)
    return lax.all_gather(values, "seq", axis=axis, tiled=True)


def own_part(values, axis, index=None):
    size = values.shape[axis] // lax.axis_size("seq")
    index = lax.axis_index("seq") if index is None else index
    return lax.dynamic_slice_in_dim(values, index * size, size, axis=axis)


def sum_scatter_seq(values, axis):
    if lax.axis_size("seq") == 2:
        other = own_part(values, axis, 1 - lax.axis_index("seq")).astype(bf16)
        return own_part(values, axis) + swap_seq(other).astype(f32)
    return lax.psum_scatter(
        values.astype(bf16), "seq", scatter_dimension=axis, tiled=True
    ).astype(f32)


def own_first(values):
    if lax.axis_size("seq") == 2:
        return jnp.concatenate([values, swap_seq(values)], axis=0)
    return lax.all_gather(values, "seq", axis=0, tiled=True)


def sum_own_first(values):
    if lax.axis_size("seq") == 2:
        half = values.shape[0] // 2
        return values[:half] + swap_seq(values[half:].astype(bf16)).astype(f32)
    return sum_scatter_seq(values, 0)


def exchange_seq(values, split, join):
    if lax.axis_size("seq") == 2:
        other = own_part(values, split, 1 - lax.axis_index("seq"))
        return in_order(own_part(values, split), swap_seq(other), join)
    return lax.all_to_all(values, "seq", split_axis=split, concat_axis=join, tiled=True)


PLACES = 4


def in_grid():
    return lax.axis_size("shard") == 4 * PLACES and lax.axis_size("seq") == 2


def position():
    place = lax.axis_index("shard")
    return place // 4, (place // 2) % 2, place % 2


def flip(values, mask):
    size = lax.axis_size("shard")
    return lax.ppermute(values, "shard", [(i, i ^ mask) for i in range(size)])


def from_place(values, step):
    size = lax.axis_size("shard")
    return lax.ppermute(values, "shard", [(i, (i - 4 * step) % size) for i in range(size)])


def gather_shard(values):
    return lax.all_gather(values, "shard", axis=0, tiled=True)


def scatter_shard(values):
    return lax.psum_scatter(values, "shard", scatter_dimension=0, tiled=True)


def core_major(values):
    if not in_grid():
        return values
    rows, columns = values.shape
    places = values.reshape(rows, PLACES, 2, 2, columns // (4 * PLACES))
    return jnp.transpose(places, (0, 3, 2, 1, 4)).reshape(rows, columns)


def portion(values, index, count):
    size = values.shape[0] // count
    return lax.dynamic_slice_in_dim(values, index * size, size, axis=0)


def sum_pair(values, index, mask):
    sent = flip(portion(values, 1 - index, 2), mask)
    return (portion(values, index, 2).astype(f32) + sent.astype(f32)).astype(bf16)


def sum_along(values):
    z = position()[0]
    total = portion(values, z, PLACES).astype(f32)
    for r in range(1, PLACES):
        sent = from_place(portion(values, (z - r) % PLACES, PLACES), r)
        total = total + sent.astype(f32)
    return total.astype(bf16)


def first_sum(values):
    return sum_pair(values, position()[2], 1) if in_grid() else values


def second_sum(values):
    return sum_pair(values, position()[1], 2) if in_grid() else values


def third_sum(values):
    return sum_along(values) if in_grid() else scatter_shard(values)


def spread_kernel(cuts, seq_ref, own_ref, other_ref, *out_refs):
    def write(first, second):
        for (start, stop), out_ref in zip(cuts, out_refs):
            out_ref[:, : stop - start] = first[:, start:stop].astype(f32)
            out_ref[:, stop - start :] = second[:, start:stop].astype(f32)

    @pl.when(seq_ref[0] == 0)
    def _():
        write(own_ref, other_ref)

    @pl.when(seq_ref[0] != 0)
    def _():
        write(other_ref, own_ref)


def spread(own, other, cuts):
    rows = own.shape[0]
    memory = pl.BlockSpec(memory_space=pltpu.VMEM)
    return pl.pallas_call(
        functools.partial(spread_kernel, cuts),
        in_specs=[pl.BlockSpec(memory_space=pltpu.SMEM), memory, memory],
        out_specs=[memory] * len(cuts),
        out_shape=[jax.ShapeDtypeStruct((rows, 2 * (b - a)), f32) for a, b in cuts],
        compiler_params=pltpu.CompilerParams(vmem_limit_bytes=SPACE // 4),
        cost_estimate=pl.CostEstimate(flops=2**20, bytes_accessed=2**22, transcendentals=0),
        name="spread",
    )(seq_index(), own, other)


def seq_index():
    return jnp.stack([lax.axis_index("seq")]).astype(jnp.int32)


def after(values, *earlier):
    return lax.optimization_barrier((values, earlier))[0]


def sum_small(values, axes):
    if not in_grid():
        return lax.psum(values, axes)
    for mask in (1, 2, 4, 8):
        values = values + flip(values, mask)
    return values


def on_device(
    tokens,
    doc_starts,
    norm_gain,
    query_weight,
    key_weight,
    value_weight,
    gate_weight,
    beta_decay_weight,
    conv_filters,
    decay_params,
    out_norm_gain,
    out_weight,
    ffn_norm_gain,
    ffn_gate_weight,
    ffn_up_weight,
    down_weight,
    out_cotangent,
):
    heads = HEADS // lax.axis_size("seq")
    shards = lax.axis_size("shard")
    rows = query_weight.shape[0]
    width = 2 * heads * KEY
    ff = ffn_gate_weight.shape[1]

    logit_weight = own_part(beta_decay_weight.reshape(rows, HEADS, 2), 1)
    gain_rows = out_norm_gain.shape[0]
    raw_piece = jnp.concatenate(
        [
            own_part(query_weight, 1),
            own_part(key_weight, 1),
            logit_weight[:, :, 0],
            logit_weight[:, :, 1],
            norm_gain[:, None],
            ffn_norm_gain[:, None],
            jnp.pad(out_norm_gain, (0, rows - gain_rows))[:, None],
            jnp.zeros((rows, KEY - 2 * heads - 3), bf16),
        ],
        axis=1,
    )
    units = ff // shards // lax.axis_size("seq")

    def own_units(weight):
        return own_part(weight.reshape(rows, shards, ff // shards), 2).reshape(rows, shards * units)

    raw_wide = raw_piece.shape[1]
    value_end = raw_wide + heads * VALUE
    mixer_full = gather_shard(
        jnp.concatenate([raw_piece, own_part(value_weight, 1), own_part(gate_weight, 1)], axis=1)
    )
    raw_full = mixer_full[:, :raw_wide]
    value_full = mixer_full[:, raw_wide:value_end]
    gate_full = mixer_full[:, value_end:]
    half = shards * units
    model = out_weight.shape[1]
    out_rows = out_weight.shape[0]
    tall_full = gather_shard(jnp.concatenate([out_weight, own_part(down_weight, 0)], axis=0))
    tall_full = tall_full.reshape(shards, out_rows + units, model)
    out_full = tall_full[:, :out_rows].reshape(shards * out_rows, model)
    down_full = tall_full[:, out_rows:].reshape(half, model)
    ffn_full = gather_shard(
        jnp.concatenate([own_units(ffn_gate_weight), own_units(ffn_up_weight)], axis=1)
    )
    first_gain = raw_full[:, width + 2 * heads].astype(f32)
    second_gain = raw_full[:, width + 2 * heads + 1].astype(f32)
    third_gain = (
        raw_full[:, width + 2 * heads + 2]
        .reshape(shards, rows)[:, :gain_rows]
        .reshape(1, shards * gain_rows)
        .astype(f32)
    )

    own_tokens = tokens[0]
    token_count = own_tokens.shape[0]
    inputs = own_tokens.astype(f32)
    cotangent = out_cotangent[0]
    if lax.axis_size("seq") == 2:
        other = swap_seq(jnp.concatenate([own_tokens, cotangent], axis=0))
        all_inputs = in_order(own_tokens, other[:token_count], 0).astype(f32)
        all_cotangent = jnp.concatenate([cotangent, other[token_count:]], axis=0)
    else:
        all_inputs = gather_seq(own_tokens, 0).astype(f32)
        all_cotangent = own_first(cotangent)
    length = all_inputs.shape[0]
    all_scaled = all_inputs * lax.rsqrt(
        jnp.mean(all_inputs * all_inputs, axis=-1, keepdims=True) + epsilon
    )
    normed = (all_scaled * first_gain).astype(bf16)
    raw = forward_dot(normed, raw_full).astype(bf16)
    values = forward_dot(normed, value_full).astype(bf16)
    gate_rows = forward_dot(normed, gate_full)
    filters = jnp.concatenate(
        [
            conv_filters[:, :, :KEY].reshape(CONV, heads * KEY),
            conv_filters[:, :, KEY : 2 * KEY].reshape(CONV, heads * KEY),
            conv_filters[:, :, 2 * KEY :].reshape(CONV, heads * VALUE),
        ],
        axis=1,
    )
    decays = decay_params.T
    gated, *kept = mixer_forward(
        raw, values, filters, decays, doc_starts, gate_rows, third_gain, heads
    )
    gated_low = exchange_seq(gated, 0, 1)
    gated_low, down_full = lax.optimization_barrier((gated_low, down_full))
    middle = inputs + forward_dot(gated_low, out_full)
    second_norm, second_pull = jax.vjp(rms_norm, middle, second_gain)
    hidden = own_first(second_norm.astype(bf16))
    turned, ffn_full = lax.optimization_barrier((core_major(hidden), ffn_full))
    both_ffn = forward_dot(hidden, ffn_full)
    activated, swiglu_pull = jax.vjp(swiglu, both_ffn[:, :half], both_ffn[:, half:])
    activated_low = activated.astype(bf16)
    act_grad = times_transposed(all_cotangent, down_full)
    both_grad = jnp.concatenate([g.astype(bf16) for g in swiglu_pull(act_grad)], axis=1)
    hidden_grad = sum_own_first(times_transposed(both_grad, ffn_full))
    out_parts = forward_dot(activated_low, down_full)
    down_grad = transposed_times(activated_low, all_cotangent).astype(bf16)
    ffn_grad = transposed_times(turned, both_grad).astype(bf16)
    ffn_grad = first_sum(ffn_grad)
    out_sent = out_parts[token_count:].astype(bf16)
    tall_grad = jnp.pad(down_grad.reshape(shards, units, model), ((0, 0), (out_rows, 0), (0, 0)))
    hidden_grad, ffn_grad, tall_grad, out_parts, out_sent = lax.optimization_barrier(
        (hidden_grad, ffn_grad, tall_grad, out_parts, out_sent)
    )
    middle_part, ffn_gain_grad = second_pull(hidden_grad)
    middle_grad = cotangent.astype(f32) + middle_part
    branch_low = middle_grad.astype(bf16)
    out_grad = transposed_times(gated_low, branch_low).astype(bf16)
    gated_grad = times_transposed(branch_low, out_full).astype(bf16)
    if lax.axis_size("seq") == 2:
        other_grad = swap_seq(own_part(gated_grad, 1, 1 - lax.axis_index("seq")))
        own_grad = own_part(gated_grad, 1)
    else:
        own_grad = other_grad = exchange_seq(gated_grad, 1, 0)
    ffn_grad = second_sum(ffn_grad)
    tall_grad = lax.dynamic_update_slice(
        tall_grad, out_grad.reshape(shards, out_rows, model), (0, 0, 0)
    ).reshape(shards * (out_rows + units), model)
    own_grad, other_grad, ffn_grad, tall_grad = lax.optimization_barrier(
        (own_grad, other_grad, ffn_grad, tall_grad)
    )
    ffn_share = third_sum(ffn_grad)
    tall_share = scatter_shard(tall_grad)
    if lax.axis_size("seq") == 2:
        out_parts = out_parts[:token_count] + swap_seq(after(out_sent, other_grad)).astype(f32)
    else:
        out_parts = sum_own_first(out_parts)
    block_out = (middle + out_parts).astype(bf16)
    mixer_grad, filters_grad, decays_grad, out_gain_grad = mixer_backward(
        raw,
        values,
        filters,
        decays,
        doc_starts,
        gate_rows,
        third_gain,
        (own_grad, other_grad),
        kept,
        heads,
    )
    mixer_grad, ffn_share, block_out = lax.optimization_barrier((mixer_grad, ffn_share, block_out))
    mixer_weight_grad = transposed_times(normed, mixer_grad).astype(bf16)
    mixer_grad, mixer_weight_grad = lax.optimization_barrier((mixer_grad, mixer_weight_grad))
    mixer_share = scatter_shard(mixer_weight_grad)
    normed_grad = times_transposed(mixer_grad, mixer_full)
    norm_gain_grad = jnp.sum(normed_grad * all_scaled, axis=0)
    if lax.axis_size("seq") == 2:
        sent = own_part(normed_grad, 0, 1 - lax.axis_index("seq")).astype(bf16)
        own_normed_grad = own_part(normed_grad, 0) + swap_seq(sent).astype(f32)
    else:
        sent = normed_grad
        own_normed_grad = sum_scatter_seq(normed_grad, 0)
    _, first_pull = jax.vjp(lambda v: rms_norm(v, first_gain), inputs)
    tokens_grad = middle_grad + first_pull(own_normed_grad)[0]

    def all_units(share):
        share = gather_seq(share.reshape(rows, shards, units), 2)
        return share.reshape(rows, ff).astype(f32)

    ffn_gate_share = all_units(ffn_share[:, :half])
    ffn_up_share = all_units(ffn_share[:, half:])
    tall_share = gather_seq(after(tall_share, mixer_grad)[None], 0).astype(f32)
    out_share = jnp.sum(tall_share[:, :out_rows], axis=0)
    down_share = tall_share[:, out_rows:].reshape(-1, model)
    if lax.axis_size("seq") == 2:
        other_share = swap_seq(mixer_share)

        def side_by_side(start, stop):
            own, other = mixer_share[:, start:stop], other_share[:, start:stop]
            return in_order(own.astype(f32), other.astype(f32), 1)
    else:
        every = gather_seq(mixer_share[None], 0)

        def side_by_side(start, stop):
            part = jnp.swapaxes(every[:, :, start:stop], 0, 1)
            return part.reshape(rows, -1).astype(f32)

    cuts = (
        (0, heads * KEY),
        (heads * KEY, width),
        (raw_wide, value_end),
        (value_end, mixer_share.shape[1]),
    )
    if lax.axis_size("seq") == 2:
        shares = spread(mixer_share, other_share, cuts)
    else:
        shares = [side_by_side(start, stop) for start, stop in cuts]
    query_share, key_share, value_share, gate_share = shares
    logit_share = side_by_side(width, width + 2 * heads).reshape(rows, -1, 2, heads)
    logit_share = jnp.swapaxes(logit_share, 2, 3).reshape(rows, 2 * HEADS)

    all_width = filters.shape[1]
    filters_grad = jnp.sum(filters_grad.reshape(CONV, 8, all_width), axis=1)
    lengths = [shards * n for n in (norm_gain.shape[0], gain_rows, ffn_norm_gain.shape[0])]
    small = jnp.concatenate(
        [
            filters_grad.reshape(CONV * all_width),
            decays_grad.reshape(2 * heads),
            norm_gain_grad,
            jnp.sum(out_gain_grad, axis=0),
            ffn_gain_grad,
        ]
    )
    small = sum_small(after(small, sent), ("shard",))
    head_end = CONV * all_width + 2 * heads
    filters_grad = small[: CONV * all_width].reshape(CONV, all_width)
    decays_grad = small[CONV * all_width : head_end].reshape(2, heads)
    gains = small[head_end:]
    gains = gains + swap_seq(gains) if in_grid() else lax.psum(gains, "seq")
    split = (heads * KEY, 2 * heads * KEY)
    filters_out = jnp.concatenate(
        [
            filters_grad[:, : split[0]].reshape(CONV, heads, KEY),
            filters_grad[:, split[0] : split[1]].reshape(CONV, heads, KEY),
            filters_grad[:, split[1] :].reshape(CONV, heads, VALUE),
        ],
        axis=2,
    )
    gains = [
        gains[: lengths[0]],
        gains[lengths[0] : lengths[0] + lengths[1]],
        gains[lengths[0] + lengths[1] :],
    ]
    place = lax.axis_index("shard")
    gains = [
        lax.dynamic_slice_in_dim(g, place * (g.shape[0] // shards), g.shape[0] // shards)
        for g in gains
    ]
    return (
        block_out[None],
        tokens_grad[None],
        gains[0],
        query_share,
        key_share,
        value_share,
        gate_share,
        logit_share,
        filters_out,
        decays_grad.T,
        gains[1],
        out_share,
        gains[2],
        ffn_gate_share,
        ffn_up_share,
        down_share,
    )


def solution(mesh):
    in_specs = (
        P("shard", "seq", None),
        P("shard", None),
        P("shard"),
        P("shard", None),
        P("shard", None),
        P("shard", None),
        P("shard", None),
        P("shard", None),
        P(None, "seq", None),
        P("seq", None),
        P("shard"),
        P("shard", None),
        P("shard"),
        P("shard", None),
        P("shard", None),
        P("shard", None),
        P("shard", "seq", None),
    )
    out_specs = (
        P("shard", "seq", None),
        P("shard", "seq", None),
        P("shard"),
        P("shard", None),
        P("shard", None),
        P("shard", None),
        P("shard", None),
        P("shard", None),
        P(None, "seq", None),
        P("seq", None),
        P("shard"),
        P("shard", None),
        P("shard"),
        P("shard", None),
        P("shard", None),
        P("shard", None),
    )
    return jax.shard_map(
        on_device, mesh=mesh, in_specs=in_specs, out_specs=out_specs, check_vma=False
    )
```
